32 devices in a mesh: region: 8 (over y, x, core), row: 4 (over z).
Axes of the slice: x: 2, y: 2, z: 4, core: 2. Of those that a mesh axis runs over, the one named last changes fastest.
Arguments:
- inputs: bfloat16 [12, 16384, 227], P('row', 'region'), may hold values from -6 to 6
- targets: bfloat16 [12, 16384, 227], P('row', 'region'), may hold values from -6 to 6
- valid_steps: int32 [12, 16384], P('row', 'region'), may hold values from 0 to 1, as said below
- var_weights: float32 [227], replicated, may hold values from 0.3 to 3
- grid_to_mesh: int32 [4096, 4], P('region'), may hold values from 0 to 2047
- mesh_edges: int32 [4096, 8], P('region'), may hold values from 0 to 639
- send_rows: int32 [1024], P('region'), may hold values from 0 to 511
- mesh_to_grid: int32 [16384, 3], P('region'), may hold values from 0 to 511
- date_index: int32 [12], P('row'), may hold values from 0 to 7
- matrices: float32 [7, 512, 512], P(None, 'row'), may hold values from -0.25 to 0.25
- matrices_momentum: float32 [7, 512, 512], P(None, 'row'), may hold values from -0.125 to 0.125
- in_proj: float32 [227, 512], P(None, 'row'), may hold values from -0.375 to 0.375
- in_first: float32 [227, 512], P(None, 'row'), may hold values from -0.015625 to 0.015625
- in_second: float32 [227, 512], P(None, 'row'), may hold values from 2.1362305e-06 to 3.4077962e-05
- out_proj: float32 [512, 227], P('row'), may hold values from -0.25 to 0.25
- out_first: float32 [512, 227], P('row'), may hold values from -0.015625 to 0.015625
- out_second: float32 [512, 227], P('row'), may hold values from 2.1362305e-06 to 3.4077962e-05
- norm_gains: float32 [3, 512], P(None, 'row'), may hold values from 0.5 to 1.5
- gains_first: float32 [3, 512], P(None, 'row'), may hold values from -0.046875 to 0.046875
- gains_second: float32 [3, 512], P(None, 'row'), may hold values from 1.93278e-05 to 0.00030517578
- date_table: float32 [8, 512], P(None, 'row'), may hold values from -3 to 3
- date_first: float32 [8, 512], P(None, 'row'), may hold values from -0.046875 to 0.046875
- date_second: float32 [8, 512], P(None, 'row'), may hold values from 1.93278e-05 to 0.00030517578
Outputs:
- new_matrices: float32 [7, 512, 512], P(None, 'row')
- new_momentum: float32 [7, 512, 512], P(None, 'row')
- new_in_proj: float32 [227, 512], P(None, 'row')
- new_in_first: float32 [227, 512], P(None, 'row')
- new_in_second: float32 [227, 512], P(None, 'row')
- new_out_proj: float32 [512, 227], P('row')
- new_out_first: float32 [512, 227], P('row')
- new_out_second: float32 [512, 227], P('row')
- new_gains: float32 [3, 512], P(None, 'row')
- new_gains_first: float32 [3, 512], P(None, 'row')
- new_gains_second: float32 [3, 512], P(None, 'row')
- new_dates: float32 [8, 512], P(None, 'row')
- new_date_first: float32 [8, 512], P(None, 'row')
- new_date_second: float32 [8, 512], P(None, 'row')
- loss_sum: float32 [], replicated
- valid_count: float32 [], replicated
The draws below stay inside these ranges and needn't reach their ends.
Inputs may be any that keep to these rules, and one draw needn't show every extreme that they name: `valid_steps`: each value is 0 or 1; the share of ones varies over members and grid points. `grid_to_mesh`: indices of grid points within the mesh node's own region. `mesh_edges`: rows below 512 are the region's own mesh nodes; the next 64 rows come from the previous region, the last 64 from the next one, cyclically. `send_rows`: within a region's 2 * 64 slots, the first 64 go to the previous region and the last 64 to the next one; a row may be sent several times. `mesh_to_grid`: indices of mesh nodes within the grid point's own region.
All inputs are finite; a program needn't handle non-finite values.
Results may differ from the reference program's by a relative error of at most 0.0011.
The reference program's roundings to bfloat16 on the way count: a program that leaves them out, or rounds other values in their place, can miss the bound.
Values may be sent and summed in bfloat16 or wider, within the bound.
A program may use at most 320 MiB of HBM per device.

```python
import math
import jax
import jax.numpy as jnp
from jax import lax

LATENT = 512
VARIABLES = 227
G_DEV = 2048
M_DEV = 512
HALO = 64
K_G = 4
K_M = 8
K_D = 3
DATES = 8
NS_ITERS = 2
STEP = 10
MEMBERS = 12
GRID = 16384
MESH = 4096
SENDS = 1024
N_REGION = 8


def draw_valid_steps(key, part):
    key = jax.random.fold_in(key, 11)
    member_rank = jnp.arange(MEMBERS, dtype=jnp.int32)[:, None]
    position = jnp.arange(GRID, dtype=jnp.int32)[None, :]
    threshold = (GRID + 2 * position) * (MEMBERS + 2 * member_rank)
    sample_value = jax.random.randint(key, (MEMBERS, GRID), 0, 9 * GRID * MEMBERS)
    return (sample_value < threshold).astype(jnp.int32)


def place_ends(array, rng, low, largest):
    shape = array.shape
    index_at = [jax.random.randint(jax.random.fold_in(rng, axis), (), 0, shape[axis]) for axis in range(len(shape))]
    array = array.at[tuple(index_at)].set(low)
    longest = shape.index(max(shape))
    index_at[longest] = (index_at[longest] + 1) % shape[longest]
    return array.at[tuple(index_at)].set(largest)


def steps_of(own_key, shape, shards, least, largest):
    loudness = 1.0
    for dim, parts in shards:
        draws = jax.random.uniform(jax.random.fold_in(jax.random.fold_in(own_key, 6), dim), (parts,), jnp.float32, least / len(shards), largest / len(shards))
        loudness = loudness * jnp.repeat(jnp.exp(draws), shape[dim] // parts).reshape((-1,) + (1,) * (len(shape) - 1 - dim))
    return loudness


def gaussian(own_key, shape, deviation, limit, shards=(), kind=jnp.bfloat16):
    values = jax.random.normal(own_key, shape, jnp.float32) * deviation
    if len(shards) > 0:
        values = steps_of(own_key, shape, shards, -0.22, 0.18) * values
    return jnp.clip(values, min=-limit, max=limit).astype(kind)


def setup_inputs(seed: int = 0) -> dict:
    seeds = jax.random.split(jax.random.key(seed), 24)
    inputs = gaussian(seeds[0], (MEMBERS, GRID, VARIABLES), 1.0, 6.0, ((0, 4), (1, 8)))
    targets = gaussian(seeds[1], (MEMBERS, GRID, VARIABLES), 1.0, 6.0, ((0, 4), (1, 8)))
    valid_steps = draw_valid_steps(jax.random.fold_in(seeds[23], 71), 0)
    var_weights = jnp.clip(jnp.exp(jax.random.uniform(seeds[3], (VARIABLES,), jnp.float32, math.log(0.3), math.log(3.0))), 0.3, 3.0)
    grid_to_mesh = place_ends(jax.random.randint(seeds[4], (MESH, K_G), 0, G_DEV), jax.random.fold_in(seeds[4], 1), 0, G_DEV - 1).astype(jnp.int32)
    mesh_edges = place_ends(jax.random.randint(seeds[5], (MESH, K_M), 0, M_DEV + 2 * HALO), jax.random.fold_in(seeds[5], 1), 0, (M_DEV + 2 * HALO) - 1).astype(jnp.int32)
    send_rows = place_ends(jax.random.randint(seeds[6], (SENDS,), 0, M_DEV), jax.random.fold_in(seeds[6], 1), 0, M_DEV - 1).astype(jnp.int32)
    mesh_to_grid = place_ends(jax.random.randint(seeds[7], (GRID, K_D), 0, M_DEV), jax.random.fold_in(seeds[7], 1), 0, M_DEV - 1).astype(jnp.int32)
    date_index = place_ends(jax.random.randint(seeds[8], (MEMBERS,), 0, DATES), jax.random.fold_in(seeds[8], 1), 0, DATES - 1).astype(jnp.int32)
    matrices = gaussian(seeds[9], (7, LATENT, LATENT), LATENT ** -0.5, 0.25, ((1, 4),), jnp.float32)
    matrices_momentum = gaussian(seeds[10], (7, LATENT, LATENT), (4.0 * (GRID * MEMBERS) ** -0.5), 0.125, ((1, 4),), jnp.float32)
    in_proj = gaussian(seeds[11], (VARIABLES, LATENT), VARIABLES ** -0.5, 0.375, ((1, 4),), jnp.float32)
    in_first = gaussian(seeds[12], (VARIABLES, LATENT), (0.44 * (GRID * MEMBERS) ** -0.5), 0.015625, ((1, 4),), jnp.float32)
    in_second = jnp.clip(jnp.exp(math.log(3.4077962482115254e-05) - 2.769608 * jax.random.uniform(seeds[13], (VARIABLES, LATENT), jnp.float32) ** steps_of(seeds[13], (VARIABLES, LATENT), ((1, 4),), -0.2, 0.2)), 2.136230477844947e-06, 3.4077962482115254e-05)
    out_proj = gaussian(seeds[14], (LATENT, VARIABLES), LATENT ** -0.5, 0.25, ((0, 4),), jnp.float32)
    out_first = gaussian(seeds[15], (LATENT, VARIABLES), (0.44 * (GRID * MEMBERS) ** -0.5), 0.015625, ((0, 4),), jnp.float32)
    out_second = jnp.clip(jnp.exp(math.log(3.4077962482115254e-05) - 2.769608 * jax.random.uniform(seeds[16], (LATENT, VARIABLES), jnp.float32) ** steps_of(seeds[16], (LATENT, VARIABLES), ((0, 4),), -0.2, 0.2)), 2.136230477844947e-06, 3.4077962482115254e-05)
    norm_gains = jnp.clip(1.0 + 0.1 * jax.random.normal(seeds[17], (3, LATENT), jnp.float32), 0.5, 1.5)
    gains_first = gaussian(seeds[18], (3, LATENT), (1.3 * (GRID * MEMBERS) ** -0.5), 0.046875, ((1, 4),), jnp.float32)
    gains_second = jnp.clip(jnp.exp(math.log(0.00030517578) - 2.75934351 * jax.random.uniform(seeds[19], (3, LATENT), jnp.float32) ** steps_of(seeds[19], (3, LATENT), ((1, 4),), -0.2, 0.2)), 1.9327799236634746e-05, 0.00030517578)
    date_table = gaussian(seeds[20], (DATES, LATENT), 0.5, 3.0, ((1, 4),), jnp.float32)
    date_first = gaussian(seeds[21], (DATES, LATENT), (1.3 * (GRID * MEMBERS) ** -0.5), 0.046875, ((1, 4),), jnp.float32)
    date_second = jnp.clip(jnp.exp(math.log(0.00030517578) - 2.75934351 * jax.random.uniform(seeds[22], (DATES, LATENT), jnp.float32) ** steps_of(seeds[22], (DATES, LATENT), ((1, 4),), -0.2, 0.2)), 1.9327799236634746e-05, 0.00030517578)
    return {"inputs": inputs, "targets": targets, "valid_steps": valid_steps, "var_weights": var_weights, "grid_to_mesh": grid_to_mesh, "mesh_edges": mesh_edges, "send_rows": send_rows, "mesh_to_grid": mesh_to_grid, "date_index": date_index, "matrices": matrices, "matrices_momentum": matrices_momentum, "in_proj": in_proj, "in_first": in_first, "in_second": in_second, "out_proj": out_proj, "out_first": out_first, "out_second": out_second, "norm_gains": norm_gains, "gains_first": gains_first, "gains_second": gains_second, "date_table": date_table, "date_first": date_first, "date_second": date_second}


@jax.custom_vjp
def low(v):
    return lax.optimization_barrier(v.astype(jnp.bfloat16)).astype(jnp.float32)

@jax.custom_vjp
def low_back(v):
    return v

def low_keep(v):
    return (low(v), None)

def low_pass(kept, grad):
    return (grad,)

def back_keep(v):
    return (v, None)

def back_low(kept, grad):
    return (low(grad),)
low.defvjp(low_keep, low_pass)
low_back.defvjp(back_keep, back_low)
HIGHEST = lax.Precision.HIGHEST
NS_COEFFS = (3.4445, -4.775, 2.0315)
MUON_RATE = 0.8
MUON_MOMENTUM = 0.95
MATRIX_RATE = 0.05
VECTOR_RATE = 0.2
BETA_ONE = 0.9
BETA_TWO = 0.95
WEIGHT_DECAY = 0.01

def product(left_side, right_side):
    return jnp.dot(left_side, right_side, precision=HIGHEST)

def norm_rows(values, gain_row):
    centred = values - lax.optimization_barrier(jnp.mean(values, axis=-1, keepdims=True))
    spread = lax.optimization_barrier(jnp.mean(centred * centred, axis=-1, keepdims=True))
    return centred * lax.rsqrt(spread + 1e-05) * gain_row

def branch_mlp(values, first_matrix, second_matrix, gain_row):
    hidden = low(jax.nn.silu(product(low(values), first_matrix)))
    return norm_rows(product(hidden, second_matrix), gain_row)

def pick_rows(source, indices):
    return source[indices]

def member_loss(params, inputs, targets, valid_row, date_row, var_weights, graph):
    matrices, in_proj, out_proj, norm_gains, date_table = params
    grid_to_mesh, mesh_edges, send_rows, mesh_to_grid = graph
    regions = N_REGION
    grid_start = product(inputs, in_proj) + date_table[date_row]
    grid_blocks = grid_start.reshape(regions, G_DEV, -1)
    gathered = jax.vmap(pick_rows)(grid_blocks, grid_to_mesh.reshape(regions, M_DEV, K_G))
    agg_start = lax.optimization_barrier(jnp.mean(gathered, axis=2))
    mesh_one = agg_start + branch_mlp(agg_start, matrices[0], matrices[1], norm_gains[0])
    sent = low(mesh_one)
    buffer = jax.vmap(pick_rows)(sent, send_rows.reshape(regions, 2 * HALO))
    left_rows = jnp.roll(buffer[:, HALO:], 1, axis=0)
    right_rows = jnp.roll(buffer[:, :HALO], -1, axis=0)
    extended = jnp.concatenate([sent, left_rows, right_rows], axis=1)
    senders = product(extended, matrices[2])
    receivers = product(sent, matrices[3])
    pre_act = jax.vmap(pick_rows)(senders, mesh_edges.reshape(regions, M_DEV, K_M)) + receivers[:, :, None, :]
    hidden = low(jax.nn.silu(pre_act))
    agg_mesh = product(lax.optimization_barrier(jnp.mean(hidden, axis=2)), matrices[4])
    mesh_two = mesh_one + norm_rows(agg_mesh, norm_gains[1])
    picked = jax.vmap(pick_rows)(mesh_two, mesh_to_grid.reshape(regions, G_DEV, K_D))
    decoded = lax.optimization_barrier(jnp.mean(picked, axis=2)).reshape(G_DEV * regions, -1)
    grid_one = grid_start + branch_mlp(decoded, matrices[5], matrices[6], norm_gains[2])
    predicted = inputs + product(low(grid_one), out_proj)
    misfit = predicted - targets
    return jnp.sum(valid_row[:, None] * var_weights[None, :] * misfit * misfit)

def orthogonal(momentum):
    squares = lax.optimization_barrier(jnp.sum(momentum * momentum, axis=(1, 2)))
    current = momentum * lax.rsqrt(squares + 1e-07)[:, None, None]
    for sweep_index in range(NS_ITERS):
        gram_matrix = jnp.einsum('mrk,mrl->mkl', current, current, precision=HIGHEST)
        square = jnp.einsum('mkj,mjl->mkl', gram_matrix, gram_matrix, precision=HIGHEST)
        mixing = NS_COEFFS[1] * gram_matrix + NS_COEFFS[2] * square
        current = NS_COEFFS[0] * current + jnp.einsum('mrk,mkl->mrl', current, mixing, precision=HIGHEST)
    return current

def adam_update(weight, gradient, first_moment, second_moment, step_rate, decay_rate):
    first_new = BETA_ONE * first_moment + (1.0 - BETA_ONE) * gradient
    second_new = BETA_TWO * second_moment + (1.0 - BETA_TWO) * gradient * gradient
    unbiased_one = first_new / (1.0 - BETA_ONE ** STEP)
    unbiased_two = second_new / (1.0 - BETA_TWO ** STEP)
    weight_new = weight * (1.0 - step_rate * decay_rate) - step_rate * unbiased_one / (jnp.sqrt(unbiased_two) + 1e-08)
    return (weight_new, first_new, second_new)

def reference(inputs, targets, valid_steps, var_weights, grid_to_mesh, mesh_edges, send_rows, mesh_to_grid, date_index, matrices, matrices_momentum, in_proj, in_first, in_second, out_proj, out_first, out_second, norm_gains, gains_first, gains_second, date_table, date_first, date_second):
    graph = (grid_to_mesh, mesh_edges, send_rows, mesh_to_grid)
    valid_count = jnp.sum(valid_steps.astype(jnp.float32))
    params = (matrices, in_proj, out_proj, norm_gains, date_table)

    def total(weights):
        rounded = jax.tree.map(low, weights)
        checked = jax.checkpoint(member_loss)

        def member_step(running, member):
            data_in, data_out, mask_row, date_row = member
            term = checked(rounded, data_in.astype(jnp.float32), data_out.astype(jnp.float32), mask_row.astype(jnp.float32), date_row, var_weights, graph)
            return (running + term, None)
        result, unused = lax.scan(member_step, jnp.zeros((), jnp.float32), (inputs, targets, valid_steps, date_index))
        return result
    loss_sum, pullback = jax.vjp(total, params)
    gradients, = pullback(1.0 / valid_count)
    g_matrices, g_in, g_out, g_gains, g_dates = gradients
    new_momentum = MUON_MOMENTUM * matrices_momentum + g_matrices
    new_matrices = matrices * (1.0 - MUON_RATE * WEIGHT_DECAY) - MUON_RATE * orthogonal(new_momentum)
    new_in = adam_update(in_proj, g_in, in_first, in_second, MATRIX_RATE, WEIGHT_DECAY)
    new_out = adam_update(out_proj, g_out, out_first, out_second, MATRIX_RATE, WEIGHT_DECAY)
    new_gain = adam_update(norm_gains, g_gains, gains_first, gains_second, VECTOR_RATE, 0.0)
    new_date = adam_update(date_table, g_dates, date_first, date_second, VECTOR_RATE, 0.0)
    return (new_matrices, new_momentum, new_in[0], new_in[1], new_in[2], new_out[0], new_out[1], new_out[2], new_gain[0], new_gain[1], new_gain[2], new_date[0], new_date[1], new_date[2], loss_sum, valid_count)
```

```python
from functools import partial

import jax
import jax.numpy as jnp
from jax import lax
from jax.experimental import pallas as pl
from jax.experimental.pallas import tpu as pltpu
from jax.sharding import PartitionSpec as P

NS_ITERS = 2
STEP = 10
NS_COEFFS = (3.4445, -4.775, 2.0315)
MUON_RATE = 0.8
MUON_MOMENTUM = 0.95
MATRIX_RATE = 0.05
VECTOR_RATE = 0.2
BETA_ONE = 0.9
BETA_TWO = 0.95
WEIGHT_DECAY = 0.01

F32 = jnp.float32
BF16 = jnp.bfloat16
HIGHEST = lax.Precision.HIGHEST
LATENT = 512
BLOCK = 512
T_TYPE = F32
VMEM_BYTES = 60 * 1024 * 1024


def dot(left, right):
    return jnp.dot(left, right, preferred_element_type=F32)


def dot_nt(left, right):
    return lax.dot_general(left, right, (((1,), (1,)), ((), ())), preferred_element_type=F32)


def dot_tn(left, right):
    return lax.dot_general(left, right, (((0,), (0,)), ((), ())), preferred_element_type=F32)


def split_two(values):
    high = values.astype(BF16)
    return high, (values - high.astype(F32)).astype(BF16)


def sigmoid(values):
    return 0.5 * jnp.tanh(0.5 * values) + 0.5


def normalise(values):
    centred = values - jnp.mean(values, axis=-1, keepdims=True)
    spread = jnp.mean(centred * centred, axis=-1, keepdims=True)
    scale = lax.rsqrt(spread + 1e-05)
    return centred * scale, scale


def norm_back(grad, gain, unit, scale):
    scaled = gain * grad
    mean_one = jnp.mean(scaled, axis=-1, keepdims=True)
    mean_two = jnp.mean(scaled * unit, axis=-1, keepdims=True)
    return scale * (scaled - mean_one - unit * mean_two)


def count_columns(index, width, count):
    lanes = lax.broadcasted_iota(jnp.int32, (index.shape[0], width), 1)
    total = None
    for k in range(count):
        one = jnp.where(lanes == index[:, k : k + 1], 1.0, 0.0)
        total = one if total is None else total + one
    return total.astype(BF16)


def columns_of(index):
    short = 8 - index.shape[0]
    if short > 0:
        index = jnp.concatenate([index, jnp.zeros((short, index.shape[1]), index.dtype)], axis=0)
    return jnp.transpose(index)


def count_rows(index, height):
    lines = lax.broadcasted_iota(jnp.int32, (height, index.shape[1]), 0)
    total = None
    for k in range(index.shape[0]):
        one = jnp.where(lines == index[k : k + 1, :], 1.0, 0.0)
        total = one if total is None else total + one
    return total.astype(BF16)


def encode_kernel(
    day_ref, x_ref, picks_ref, win_ref, m0_ref, m1_ref, gains_ref, date_ref, send_ref,
    x4_ref, a0_ref, h1_ref, t1_ref, unit_ref, scale_ref, mesh_ref, sent_ref, buf_ref,
    pick_ref, out_ref,
):
    @pl.when(pl.program_id(0) == 0)
    def _():
        count = picks_ref.shape[0]
        pick_ref[...] = count_columns(columns_of(picks_ref[...]), pick_ref.shape[1], count)
        out_ref[...] = count_columns(columns_of(send_ref[...]), out_ref.shape[1], 1)

    x4 = dot_nt(pick_ref[...], x_ref[0]) * (1.0 / picks_ref.shape[0])
    high, low = split_two(x4)
    win = win_ref[...]
    agg = dot(high, win) + dot(low, win) + date_ref[pl.ds(day_ref[pl.program_id(0)], 1), :]
    a0 = agg.astype(BF16)
    pre = dot(a0, m0_ref[...])
    gate = sigmoid(pre)
    hid = pre * gate
    h1 = hid.astype(BF16)
    unit, scale = normalise(dot(h1, m1_ref[...]))
    mesh = agg + unit * gains_ref[0:1, :]
    sent = mesh.astype(BF16)
    x4_ref[0] = high
    a0_ref[0] = a0
    h1_ref[0] = h1
    t1_ref[0] = gate + hid * (1.0 - gate)
    unit_ref[0] = unit
    scale_ref[0] = scale
    mesh_ref[0] = mesh
    sent_ref[0] = sent
    buf_ref[0] = dot(out_ref[...], sent).astype(BF16)


def main_kernel(
    count_ref, day_ref, mesh_ref, sent_ref, left_ref, right_ref, x_ref, y_ref, valid_ref, varw_ref,
    date_ref, edge_ref, pick_row_ref,
    win_ref, wout_ref, m2_ref, m3_ref, m4_ref, m5_ref, m6_ref, gains_ref,
    gm_ref, gout_ref, gxd_ref, dsum_ref, ggain_ref, loss_ref, dmesh_ref, dhalo_ref,
    eh_ref, eht_ref, d_ref, dt_ref, ext_ref, t_ref, mm_ref, acc_ref,
):
    nodes = mesh_ref.shape[1]
    table = ext_ref.shape[0]
    points = x_ref.shape[2]
    k_edge = edge_ref.shape[0]
    k_pick = pick_row_ref.shape[0]
    halo = left_ref.shape[1]

    @pl.when(pl.program_id(0) == 0)
    def _():
        edge_columns = columns_of(edge_ref[...])
        for k in range(k_edge):
            rows = slice(k * nodes, (k + 1) * nodes)
            eh_ref[rows, :] = count_columns(edge_columns[:, k : k + 1], table, 1)
            eht_ref[:, rows] = count_rows(edge_ref[k : k + 1, :], table)

        def build(i, carry):
            rows = pl.ds(pl.multiple_of(i * BLOCK, BLOCK), BLOCK)
            picks = pick_row_ref[:, rows]
            d_ref[rows, :] = count_columns(columns_of(picks), nodes, k_pick)
            dt_ref[:, rows] = count_rows(picks, nodes)
            return carry

        lax.fori_loop(0, points // BLOCK, build, 0)
        gm_ref[...] = jnp.zeros_like(gm_ref)
        gout_ref[...] = jnp.zeros_like(gout_ref)
        gxd_ref[...] = jnp.zeros_like(gxd_ref)
        ggain_ref[...] = jnp.zeros_like(ggain_ref)
        loss_ref[...] = jnp.zeros_like(loss_ref)

    sent = sent_ref[0]
    ext_ref[:nodes, :] = sent
    ext_ref[nodes : nodes + halo, :] = left_ref[0]
    ext_ref[nodes + halo :, :] = right_ref[0]
    receivers = dot(sent, m3_ref[...])

    def edge(k, carry):
        hid_sum, t_sum = carry
        rows = pl.ds(pl.multiple_of(k * nodes, nodes), nodes)
        picked = dot(eh_ref[rows, :], ext_ref[...]).astype(BF16)
        pre = dot(picked, m2_ref[...]) + receivers
        gate = sigmoid(pre)
        hid = pre * gate
        t = gate + hid * (1.0 - gate)
        t_ref[rows, :] = t.astype(t_ref.dtype)
        return hid_sum + hid.astype(BF16).astype(F32), t_sum + t

    zero = jnp.zeros((nodes, LATENT), F32)
    hid_sum, t_sum = lax.fori_loop(0, k_edge, edge, (zero, zero))
    h_high, h_low = split_two(hid_sum * (1.0 / k_edge))
    m4 = m4_ref[...]
    unit2, scale2 = normalise(dot(h_high, m4) + dot(h_low, m4))
    mesh2 = mesh_ref[0] + unit2 * gains_ref[1:2, :]
    m_high, m_low = split_two(mesh2)
    mm_ref[:nodes, :] = m_high
    mm_ref[nodes:, :] = m_low

    acc_ref[...] = jnp.zeros_like(acc_ref)
    dsum_ref[...] = jnp.zeros_like(dsum_ref)
    member = pl.program_id(0)
    date = date_ref[pl.ds(day_ref[member], 1), :]
    gain3 = gains_ref[2:3, :]
    varw = varw_ref[...]

    def grid_block(i, carry):
        rows = pl.ds(pl.multiple_of(i * BLOCK, BLOCK), BLOCK)
        picks = d_ref[rows, :]
        dec = dot(picks, mm_ref[:nodes, :]) + dot(picks, mm_ref[nodes:, :])
        a2 = (dec * (1.0 / k_pick)).astype(BF16)
        pre = dot(a2, m5_ref[...])
        gate = sigmoid(pre)
        hid = pre * gate
        t = gate + hid * (1.0 - gate)
        h2 = hid.astype(BF16)
        unit, scale = normalise(dot(h2, m6_ref[...]))
        x = x_ref[0, :, rows]
        grid = dot_tn(x, win_ref[...]) + date + unit * gain3
        grid = grid.astype(BF16)
        misfit = x.astype(F32) + dot_nt(wout_ref[...], grid) - y_ref[0, :, rows].astype(F32)
        valid = valid_ref[pl.ds(member, 1), rows].astype(F32)
        weighted = valid * varw * misfit
        loss_ref[...] += jnp.sum(weighted * misfit, axis=1, keepdims=True)
        dp = weighted * count_ref[0]
        dsum_ref[0] += jnp.sum(dp, axis=1, keepdims=True)
        dp = dp.astype(BF16)
        gout_ref[...] += dot(dp, grid)
        gxd_ref[...] += dot_nt(x, dp)
        dgrid = dot_tn(dp, wout_ref[...])
        ggain_ref[1:2, :] += jnp.sum(dgrid * unit, axis=0, keepdims=True)
        dc = norm_back(dgrid, gain3, unit, scale).astype(BF16)
        gm_ref[4] += dot_tn(h2, dc)
        du = (dot_nt(dc, m6_ref[...]) * t).astype(BF16)
        gm_ref[3] += dot_tn(a2, du)
        ddec = dot_nt(du, m5_ref[...]).astype(BF16)
        acc_ref[...] += dot(dt_ref[:, rows], ddec)
        return carry

    lax.fori_loop(0, points // BLOCK, grid_block, 0)

    dmesh2 = acc_ref[...] * (1.0 / k_pick)
    ggain_ref[0:1, :] += jnp.sum(dmesh2 * unit2, axis=0, keepdims=True)
    dagg = norm_back(dmesh2, gains_ref[1:2, :], unit2, scale2).astype(BF16)
    gm_ref[2] += dot_tn(h_high, dagg)
    dhid = dot_nt(dagg, m4_ref[...]) * (1.0 / k_edge)
    dr = (dhid * t_sum).astype(BF16)
    gm_ref[1] += dot_tn(sent, dr)

    def edge_back(k, total):
        rows = pl.ds(pl.multiple_of(k * nodes, nodes), nodes)
        dpre = (dhid * t_ref[rows, :].astype(F32)).astype(BF16)
        return total + dot(eht_ref[:, rows], dpre)

    ds = lax.fori_loop(0, k_edge, edge_back, jnp.zeros((table, LATENT), F32)).astype(BF16)
    gm_ref[0] += dot_tn(ext_ref[...], ds)
    dext = dot_nt(ds, m2_ref[...])
    dmesh_ref[0] = dmesh2 + dext[:nodes, :] + dot_nt(dr, m3_ref[...])
    dhalo_ref[0] = dext[nodes:, :].astype(BF16)


def encode_back_kernel(
    dmesh_ref, ret_ref, send_ref, x4_ref, a0_ref, h1_ref, t1_ref, unit_ref, scale_ref, m0_ref, m1_ref,
    gains_ref, wout_ref, gxd_ref, dsum_ref, gm_ref, gin_ref, ggain_ref, gdate_ref, back_ref,
):
    @pl.when(pl.program_id(0) == 0)
    def _():
        back_ref[...] = count_rows(send_ref[...], back_ref.shape[0])
        gm_ref[...] = jnp.zeros_like(gm_ref)
        ggain_ref[...] = jnp.zeros_like(ggain_ref)
        high, low = split_two(gxd_ref[...])
        wout = wout_ref[...]
        gin_ref[...] = dot(high, wout) + dot(low, wout)

    dmesh = dmesh_ref[0] + dot(back_ref[...], ret_ref[0])
    unit = unit_ref[0]
    ggain_ref[...] += jnp.sum(dmesh * unit, axis=0, keepdims=True)
    dc = norm_back(dmesh, gains_ref[0:1, :], unit, scale_ref[0]).astype(BF16)
    gm_ref[1] += dot_tn(h1_ref[0], dc)
    du = (dot_nt(dc, m1_ref[...]) * t1_ref[0]).astype(BF16)
    gm_ref[0] += dot_tn(a0_ref[0], du)
    dagg = dmesh + dot_nt(du, m0_ref[...])
    gin_ref[...] += dot_tn(x4_ref[0], dagg.astype(BF16))
    high, low = split_two(dsum_ref[0])
    wout = wout_ref[...]
    gdate_ref[0] = jnp.sum(dagg, axis=0, keepdims=True) + dot_tn(high, wout) + dot_tn(low, wout)


def whole(shape):
    return pl.BlockSpec(shape, lambda m: (0,) * len(shape))


def per_member(shape):
    return pl.BlockSpec((1,) + shape, lambda m: (m, 0, 0))


def call(kernel, members, in_specs, out_shapes, out_specs, scratch, cost):
    return pl.pallas_call(
        kernel,
        grid=(members,),
        in_specs=in_specs,
        out_shape=out_shapes,
        out_specs=out_specs,
        scratch_shapes=scratch,
        compiler_params=pltpu.CompilerParams(
            dimension_semantics=("arbitrary",), vmem_limit_bytes=VMEM_BYTES
        ),
        cost_estimate=pl.CostEstimate(flops=cost, bytes_accessed=32 << 20, transcendentals=0),
    )


def shape_of(shape, dtype):
    return jax.ShapeDtypeStruct(shape, dtype)


def cyclic(block, halo):
    count = lax.axis_size("region")
    forward = [(i, (i + 1) % count) for i in range(count)]
    backward = [(target, source) for source, target in forward]
    low = lax.ppermute(block[:, -halo:], "region", forward)
    high = lax.ppermute(block[:, :halo], "region", backward)
    return low, high


def gram_sum(block):
    return lax.psum(
        jnp.einsum("mrk,mrl->mkl", block, block, precision=HIGHEST).astype(BF16), "row"
    ).astype(F32)


def sweep_step(current, gram_matrix):
    square = jnp.einsum("mkj,mjl->mkl", gram_matrix, gram_matrix, precision=HIGHEST)
    mixing = NS_COEFFS[1] * gram_matrix + NS_COEFFS[2] * square
    return NS_COEFFS[0] * current + jnp.einsum("mrk,mkl->mrl", current, mixing, precision=HIGHEST)


def adam_update(weight, gradient, first_moment, second_moment, step_rate, decay_rate):
    first_new = BETA_ONE * first_moment + (1.0 - BETA_ONE) * gradient
    second_new = BETA_TWO * second_moment + (1.0 - BETA_TWO) * gradient * gradient
    unbiased_one = first_new / (1.0 - BETA_ONE**STEP)
    unbiased_two = second_new / (1.0 - BETA_TWO**STEP)
    weight_new = weight * (1.0 - step_rate * decay_rate) - step_rate * unbiased_one / (
        jnp.sqrt(unbiased_two) + 1e-08
    )
    return (weight_new, first_new, second_new)


def body(
    inputs,
    targets,
    valid_steps,
    var_weights,
    grid_to_mesh,
    mesh_edges,
    send_rows,
    mesh_to_grid,
    date_index,
    matrices,
    matrices_momentum,
    in_proj,
    in_first,
    in_second,
    out_proj,
    out_first,
    out_second,
    norm_gains,
    gains_first,
    gains_second,
    date_table,
    date_first,
    date_second,
):
    inputs = jnp.swapaxes(inputs, 1, 2)
    targets = jnp.swapaxes(targets, 1, 2)
    members, variables, points = inputs.shape
    nodes = grid_to_mesh.shape[0]
    halo = send_rows.shape[0] // 2
    table = nodes + 2 * halo
    k_edge = mesh_edges.shape[1]
    k_pick = mesh_to_grid.shape[1]
    dates = date_table.shape[0]

    masks = valid_steps.astype(F32)
    valid_count = lax.psum(jnp.sum(masks), ("region", "row"))
    full_m = lax.all_gather(matrices.astype(BF16), "row", axis=1, tiled=True)
    full_in = lax.all_gather(in_proj.astype(BF16), "row", axis=1, tiled=True)
    full_out = lax.all_gather(out_proj.T.astype(BF16), "row", axis=1, tiled=True)
    full_gains = lax.all_gather(norm_gains.astype(BF16), "row", axis=1, tiled=True).astype(F32)
    full_dates = lax.all_gather(date_table.astype(BF16), "row", axis=1, tiled=True).astype(F32)
    scalars = pl.BlockSpec(memory_space=pltpu.SMEM)

    node_block = per_member((nodes, LATENT))
    matrix = whole((LATENT, LATENT))
    x4, a0, h1, t1, unit1, scale1, mesh1, sent, buf = call(
        encode_kernel,
        members,
        [
            scalars,
            per_member((variables, points)),
            whole((grid_to_mesh.shape[1], nodes)),
            whole(full_in.shape),
            matrix,
            matrix,
            whole(full_gains.shape),
            whole(full_dates.shape),
            whole((1, 2 * halo)),
        ],
        [
            shape_of((members, nodes, variables), BF16),
            shape_of((members, nodes, LATENT), BF16),
            shape_of((members, nodes, LATENT), BF16),
            shape_of((members, nodes, LATENT), F32),
            shape_of((members, nodes, LATENT), F32),
            shape_of((members, nodes, 1), F32),
            shape_of((members, nodes, LATENT), F32),
            shape_of((members, nodes, LATENT), BF16),
            shape_of((members, 2 * halo, LATENT), BF16),
        ],
        [
            per_member((nodes, variables)),
            node_block,
            node_block,
            node_block,
            node_block,
            per_member((nodes, 1)),
            node_block,
            node_block,
            per_member((2 * halo, LATENT)),
        ],
        [pltpu.VMEM((nodes, points), BF16), pltpu.VMEM((2 * halo, nodes), BF16)],
        6_000_000_000,
    )(
        date_index, inputs, grid_to_mesh.T, full_in, full_m[0], full_m[1], full_gains, full_dates,
        send_rows[None, :],
    )
    left, right = cyclic(buf, halo)

    out_shape = (variables, LATENT)
    gm_late, gout, gxd, dsum, ggain_late, loss_row, dmesh, dhalo = call(
        main_kernel,
        members,
        [
            scalars,
            scalars,
            node_block,
            node_block,
            per_member((halo, LATENT)),
            per_member((halo, LATENT)),
            per_member((variables, points)),
            per_member((variables, points)),
            whole((members, points)),
            whole((variables, 1)),
            whole(full_dates.shape),
            whole((k_edge, nodes)),
            whole((k_pick, points)),
            whole(full_in.shape),
            whole(full_out.shape),
            matrix,
            matrix,
            matrix,
            matrix,
            matrix,
            whole(full_gains.shape),
        ],
        [
            shape_of((5, LATENT, LATENT), F32),
            shape_of(out_shape, F32),
            shape_of((variables, variables), F32),
            shape_of((members, variables, 1), F32),
            shape_of((2, LATENT), F32),
            shape_of((variables, 1), F32),
            shape_of((members, nodes, LATENT), F32),
            shape_of((members, 2 * halo, LATENT), BF16),
        ],
        [
            whole((5, LATENT, LATENT)),
            whole(out_shape),
            whole((variables, variables)),
            per_member((variables, 1)),
            whole((2, LATENT)),
            whole((variables, 1)),
            node_block,
            per_member((2 * halo, LATENT)),
        ],
        [
            pltpu.VMEM((k_edge * nodes, table), BF16),
            pltpu.VMEM((table, k_edge * nodes), BF16),
            pltpu.VMEM((points, nodes), BF16),
            pltpu.VMEM((nodes, points), BF16),
            pltpu.VMEM((table, LATENT), BF16),
            pltpu.VMEM((k_edge * nodes, LATENT), T_TYPE),
            pltpu.VMEM((2 * nodes, LATENT), BF16),
            pltpu.VMEM((nodes, LATENT), F32),
        ],
        60_000_000_000,
    )(
        (2.0 / valid_count).reshape(1),
        date_index,
        mesh1,
        sent,
        left,
        right,
        inputs,
        targets,
        valid_steps,
        var_weights[:, None],
        full_dates,
        mesh_edges.T,
        mesh_to_grid.T,
        full_in,
        full_out,
        full_m[2],
        full_m[3],
        full_m[4],
        full_m[5],
        full_m[6],
        full_gains,
    )

    from_previous, from_next = cyclic(
        jnp.concatenate([dhalo[:, :halo], dhalo[:, halo:]], axis=1), halo
    )
    returned = jnp.concatenate([from_previous, from_next], axis=1)
    gm_early, gin, ggain_early, gdate = call(
        encode_back_kernel,
        members,
        [
            node_block,
            per_member((2 * halo, LATENT)),
            whole((1, 2 * halo)),
            per_member((nodes, variables)),
            node_block,
            node_block,
            node_block,
            node_block,
            per_member((nodes, 1)),
            matrix,
            matrix,
            whole(full_gains.shape),
            whole(full_out.shape),
            whole((variables, variables)),
            per_member((variables, 1)),
        ],
        [
            shape_of((2, LATENT, LATENT), F32),
            shape_of((variables, LATENT), F32),
            shape_of((1, LATENT), F32),
            shape_of((members, 1, LATENT), F32),
        ],
        [
            whole((2, LATENT, LATENT)),
            whole((variables, LATENT)),
            whole((1, LATENT)),
            per_member((1, LATENT)),
        ],
        [pltpu.VMEM((nodes, 2 * halo), BF16)],
        4_000_000_000,
    )(
        dmesh, returned, send_rows[None, :], x4, a0, h1, t1, unit1, scale1, full_m[0], full_m[1],
        full_gains, full_out, gxd, dsum,
    )

    chosen = (date_index[None, :] == jnp.arange(dates)[:, None]).astype(F32)
    totals = (
        jnp.concatenate([gm_early, gm_late], axis=0),
        gin,
        gout,
        jnp.concatenate([ggain_early, ggain_late], axis=0),
        jnp.dot(chosen, gdate[:, 0, :], precision=HIGHEST),
    )
    reduced = (
        lax.psum_scatter(totals[0], "row", scatter_dimension=1, tiled=True),
        lax.psum_scatter(totals[1], "row", scatter_dimension=1, tiled=True),
        lax.psum_scatter(totals[2], "row", scatter_dimension=1, tiled=True),
        lax.psum_scatter(totals[3], "row", scatter_dimension=1, tiled=True),
        lax.psum_scatter(totals[4], "row", scatter_dimension=1, tiled=True),
    )
    reduced = lax.psum(reduced, "region")
    loss_sum = lax.psum(jnp.sum(loss_row), ("region", "row"))
    g_matrices, g_in, g_out, g_gains, g_dates = reduced
    new_momentum = MUON_MOMENTUM * matrices_momentum + g_matrices
    squares = lax.psum(jnp.sum(new_momentum * new_momentum, axis=(1, 2)), "row")
    current = new_momentum * lax.rsqrt(squares + 1e-07)[:, None, None]
    gram_matrix = gram_sum(current)
    for sweep_index in range(NS_ITERS):
        if sweep_index > 0:
            gram_matrix = gram_sum(current)
        current = sweep_step(current, gram_matrix)
    new_matrices = matrices * (1.0 - MUON_RATE * WEIGHT_DECAY) - MUON_RATE * current
    new_in = adam_update(in_proj, g_in, in_first, in_second, MATRIX_RATE, WEIGHT_DECAY)
    new_out = adam_update(out_proj, g_out.T, out_first, out_second, MATRIX_RATE, WEIGHT_DECAY)
    new_gain = adam_update(norm_gains, g_gains, gains_first, gains_second, VECTOR_RATE, 0.0)
    new_date = adam_update(date_table, g_dates, date_first, date_second, VECTOR_RATE, 0.0)
    return (
        new_matrices,
        new_momentum,
        new_in[0],
        new_in[1],
        new_in[2],
        new_out[0],
        new_out[1],
        new_out[2],
        new_gain[0],
        new_gain[1],
        new_gain[2],
        new_date[0],
        new_date[1],
        new_date[2],
        loss_sum,
        valid_count,
    )


def solution(mesh):
    in_specs = (
        P("row", "region", None),
        P("row", "region", None),
        P("row", "region"),
        P(),
        P("region", None),
        P("region", None),
        P("region"),
        P("region", None),
        P("row"),
        P(None, "row", None),
        P(None, "row", None),
        P(None, "row"),
        P(None, "row"),
        P(None, "row"),
        P("row", None),
        P("row", None),
        P("row", None),
        P(None, "row"),
        P(None, "row"),
        P(None, "row"),
        P(None, "row"),
        P(None, "row"),
        P(None, "row"),
    )
    out_specs = (
        P(None, "row", None),
        P(None, "row", None),
        P(None, "row"),
        P(None, "row"),
        P(None, "row"),
        P("row", None),
        P("row", None),
        P("row", None),
        P(None, "row"),
        P(None, "row"),
        P(None, "row"),
        P(None, "row"),
        P(None, "row"),
        P(None, "row"),
        P(),
        P(),
    )
    return jax.shard_map(body, mesh=mesh, in_specs=in_specs, out_specs=out_specs, check_vma=False)
```

```python
from functools import partial

import jax
import jax.numpy as jnp
from jax import lax
from jax.experimental import pallas as pl
from jax.experimental.pallas import tpu as pltpu
from jax.sharding import PartitionSpec as P

NS_ITERS = 2
STEP = 10
NS_COEFFS = (3.4445, -4.775, 2.0315)
MUON_RATE = 0.8
MUON_MOMENTUM = 0.95
MATRIX_RATE = 0.05
VECTOR_RATE = 0.2
BETA_ONE = 0.9
BETA_TWO = 0.95
WEIGHT_DECAY = 0.01

F32 = jnp.float32
BF16 = jnp.bfloat16
LATENT = 512
BLOCK = 512
T_TYPE = F32
VMEM_BYTES = 60 * 1024 * 1024
MESH = pl.DeviceIdType.MESH
SLOTS = 8
IN_ROW, OUT_ROW, GAIN_ROW, DATE_ROW, LOSS_ROW = 0, 240, 480, 496, 504


def dot(left, right):
    return jnp.dot(left, right, preferred_element_type=F32)


def dot_nt(left, right):
    return lax.dot_general(left, right, (((1,), (1,)), ((), ())), preferred_element_type=F32)


def dot_tn(left, right):
    return lax.dot_general(left, right, (((0,), (0,)), ((), ())), preferred_element_type=F32)


def split_two(values):
    high = values.astype(BF16)
    return high, (values - high.astype(F32)).astype(BF16)


def sigmoid(values):
    return 0.5 * jnp.tanh(0.5 * values) + 0.5


def normalise(values):
    centred = values - jnp.mean(values, axis=-1, keepdims=True)
    spread = jnp.mean(centred * centred, axis=-1, keepdims=True)
    scale = lax.rsqrt(spread + 1e-05)
    return centred * scale, scale


def norm_back(grad, gain, unit, scale):
    scaled = gain * grad
    mean_one = jnp.mean(scaled, axis=-1, keepdims=True)
    mean_two = jnp.mean(scaled * unit, axis=-1, keepdims=True)
    return scale * (scaled - mean_one - unit * mean_two)


def count_columns(index, width, count):
    lanes = lax.broadcasted_iota(jnp.int32, (index.shape[0], width), 1)
    total = None
    for k in range(count):
        one = jnp.where(lanes == index[:, k : k + 1], 1.0, 0.0)
        total = one if total is None else total + one
    return total.astype(BF16)


def gain_row(small_ref, k):
    return small_ref[GAIN_ROW : GAIN_ROW + 16, :].astype(F32)[k : k + 1, :]


def date_row(small_ref, day_ref):
    table = small_ref[DATE_ROW : DATE_ROW + 16, :].astype(F32)
    lines = lax.broadcasted_iota(jnp.int32, table.shape, 0)
    return jnp.sum(jnp.where(lines == day_ref[pl.program_id(0)], table, 0.0), axis=0, keepdims=True)


def columns_of(index):
    short = 8 - index.shape[0]
    if short > 0:
        index = jnp.concatenate([index, jnp.zeros((short, index.shape[1]), index.dtype)], axis=0)
    return jnp.transpose(index)


def count_rows(index, height):
    lines = lax.broadcasted_iota(jnp.int32, (height, index.shape[1]), 0)
    total = None
    for k in range(index.shape[0]):
        one = jnp.where(lines == index[k : k + 1, :], 1.0, 0.0)
        total = one if total is None else total + one
    return total.astype(BF16)


def encode_kernel(
    day_ref, x_ref, picks_ref, small_ref, m0_ref, m1_ref, send_ref,
    x4_ref, a0_ref, h1_ref, t1_ref, unit_ref, scale_ref, mesh_ref, sent_ref, buf_ref,
    pick_ref, out_ref,
):
    @pl.when(pl.program_id(0) == 0)
    def _():
        count = picks_ref.shape[0]
        pick_ref[...] = count_columns(columns_of(picks_ref[...]), pick_ref.shape[1], count)
        out_ref[...] = count_columns(columns_of(send_ref[...]), out_ref.shape[1], 1)

    x4 = dot_nt(pick_ref[...], x_ref[0]) * (1.0 / picks_ref.shape[0])
    high, low = split_two(x4)
    win = small_ref[IN_ROW : IN_ROW + x_ref.shape[1], :]
    agg = dot(high, win) + dot(low, win) + date_row(small_ref, day_ref)
    a0 = agg.astype(BF16)
    pre = dot(a0, m0_ref[0])
    gate = sigmoid(pre)
    hid = pre * gate
    h1 = hid.astype(BF16)
    unit, scale = normalise(dot(h1, m1_ref[0]))
    mesh = agg + unit * gain_row(small_ref, 0)
    sent = mesh.astype(BF16)
    x4_ref[0] = high
    a0_ref[0] = a0
    h1_ref[0] = h1
    t1_ref[0] = gate + hid * (1.0 - gate)
    unit_ref[0] = unit
    scale_ref[0] = scale
    mesh_ref[0] = mesh
    sent_ref[0] = sent
    buf_ref[0] = dot(out_ref[...], sent).astype(BF16)


def main_kernel(
    day_ref, mesh_ref, sent_ref, left_ref, right_ref, x_ref, y_ref, valid_ref, varw_ref,
    edge_ref, pick_row_ref, small_ref, m2_ref, m3_ref, m4_ref, m5_ref, m6_ref,
    slots_ref, gout_ref, gxd_ref, dsum_ref, ggain_ref, loss_ref, dmesh_ref, dhalo_ref,
    gm_ref, out_sem, eh_ref, eht_ref, d_ref, dt_ref, ext_ref, t_ref, mm_ref, acc_ref,
):
    nodes = mesh_ref.shape[1]
    table = ext_ref.shape[0]
    variables, points = x_ref.shape[1:]
    k_edge = edge_ref.shape[0]
    k_pick = pick_row_ref.shape[0]
    halo = left_ref.shape[1]

    @pl.when(pl.program_id(0) == 0)
    def _():
        edge_columns = columns_of(edge_ref[...])
        for k in range(k_edge):
            rows = slice(k * nodes, (k + 1) * nodes)
            eh_ref[rows, :] = count_columns(edge_columns[:, k : k + 1], table, 1)
            eht_ref[:, rows] = count_rows(edge_ref[k : k + 1, :], table)

        def build(i, carry):
            rows = pl.ds(pl.multiple_of(i * BLOCK, BLOCK), BLOCK)
            picks = pick_row_ref[:, rows]
            d_ref[rows, :] = count_columns(columns_of(picks), nodes, k_pick)
            dt_ref[:, rows] = count_rows(picks, nodes)
            return carry

        lax.fori_loop(0, points // BLOCK, build, 0)
        gm_ref[...] = jnp.zeros_like(gm_ref)
        gout_ref[...] = jnp.zeros_like(gout_ref)
        gxd_ref[...] = jnp.zeros_like(gxd_ref)
        ggain_ref[...] = jnp.zeros_like(ggain_ref)
        loss_ref[...] = jnp.zeros_like(loss_ref)

    sent = sent_ref[0]
    ext_ref[:nodes, :] = sent
    ext_ref[nodes : nodes + halo, :] = left_ref[0]
    ext_ref[nodes + halo :, :] = right_ref[0]
    receivers = dot(sent, m3_ref[0])

    def edge(k, carry):
        hid_sum, t_sum = carry
        rows = pl.ds(pl.multiple_of(k * nodes, nodes), nodes)
        picked = dot(eh_ref[rows, :], ext_ref[...]).astype(BF16)
        pre = dot(picked, m2_ref[0]) + receivers
        gate = sigmoid(pre)
        hid = pre * gate
        t = gate + hid * (1.0 - gate)
        t_ref[rows, :] = t.astype(t_ref.dtype)
        return hid_sum + hid.astype(BF16).astype(F32), t_sum + t

    zero = jnp.zeros((nodes, LATENT), F32)
    hid_sum, t_sum = lax.fori_loop(0, k_edge, edge, (zero, zero))
    h_high, h_low = split_two(hid_sum * (1.0 / k_edge))
    m4 = m4_ref[0]
    gain2 = gain_row(small_ref, 1)
    unit2, scale2 = normalise(dot(h_high, m4) + dot(h_low, m4))
    mesh2 = mesh_ref[0] + unit2 * gain2
    m_high, m_low = split_two(mesh2)
    mm_ref[:nodes, :] = m_high
    mm_ref[nodes:, :] = m_low

    acc_ref[...] = jnp.zeros_like(acc_ref)
    dsum_ref[...] = jnp.zeros_like(dsum_ref)
    member = pl.program_id(0)
    date = date_row(small_ref, day_ref)
    gain3 = gain_row(small_ref, 2)
    wout = small_ref[OUT_ROW : OUT_ROW + variables, :]
    varw = varw_ref[...]

    def grid_block(i, carry):
        rows = pl.ds(pl.multiple_of(i * BLOCK, BLOCK), BLOCK)
        picks = d_ref[rows, :]
        dec = dot(picks, mm_ref[:nodes, :]) + dot(picks, mm_ref[nodes:, :])
        a2 = (dec * (1.0 / k_pick)).astype(BF16)
        pre = dot(a2, m5_ref[0])
        gate = sigmoid(pre)
        hid = pre * gate
        t = gate + hid * (1.0 - gate)
        h2 = hid.astype(BF16)
        unit, scale = normalise(dot(h2, m6_ref[0]))
        x = x_ref[0, :, rows]
        grid = dot_tn(x, small_ref[IN_ROW : IN_ROW + variables, :]) + date + unit * gain3
        grid = grid.astype(BF16)
        misfit = x.astype(F32) + dot_nt(wout, grid) - y_ref[0, :, rows].astype(F32)
        valid = valid_ref[pl.ds(member, 1), rows].astype(F32)
        weighted = valid * varw * misfit
        loss_ref[...] += jnp.sum(weighted * misfit, axis=1, keepdims=True)
        dsum_ref[0] += jnp.sum(weighted, axis=1, keepdims=True)
        dp = weighted.astype(BF16)
        gout_ref[...] += dot(dp, grid)
        gxd_ref[...] += dot_nt(x, dp)
        dgrid = dot_tn(dp, wout)
        ggain_ref[1:2, :] += jnp.sum(dgrid * unit, axis=0, keepdims=True)
        dc = norm_back(dgrid, gain3, unit, scale).astype(BF16)
        gm_ref[4] += dot_tn(h2, dc)
        du = (dot_nt(dc, m6_ref[0]) * t).astype(BF16)
        gm_ref[3] += dot_tn(a2, du)
        ddec = dot_nt(du, m5_ref[0]).astype(BF16)
        acc_ref[...] += dot(dt_ref[:, rows], ddec)
        return carry

    lax.fori_loop(0, points // BLOCK, grid_block, 0)

    dmesh2 = acc_ref[...] * (1.0 / k_pick)
    ggain_ref[0:1, :] += jnp.sum(dmesh2 * unit2, axis=0, keepdims=True)
    dagg = norm_back(dmesh2, gain2, unit2, scale2).astype(BF16)
    gm_ref[2] += dot_tn(h_high, dagg)
    dhid = dot_nt(dagg, m4_ref[0]) * (1.0 / k_edge)
    dr = (dhid * t_sum).astype(BF16)
    gm_ref[1] += dot_tn(sent, dr)

    def edge_back(k, total):
        rows = pl.ds(pl.multiple_of(k * nodes, nodes), nodes)
        dpre = (dhid * t_ref[rows, :].astype(F32)).astype(BF16)
        return total + dot(eht_ref[:, rows], dpre)

    ds = lax.fori_loop(0, k_edge, edge_back, jnp.zeros((table, LATENT), F32)).astype(BF16)
    gm_ref[0] += dot_tn(ext_ref[...], ds)
    dext = dot_nt(ds, m2_ref[0])
    dmesh_ref[0] = dmesh2 + dext[:nodes, :] + dot_nt(dr, m3_ref[0])
    dhalo_ref[0] = dext[nodes:, :].astype(BF16)

    @pl.when(member == pl.num_programs(0) - 1)
    def _():
        copy = pltpu.make_async_copy(gm_ref, slots_ref.at[2:7], out_sem)
        copy.start()
        copy.wait()


def encode_back_kernel(
    day_ref, slots_in_ref, dmesh_ref, ret_ref, send_ref, x4_ref, a0_ref, h1_ref, t1_ref, unit_ref,
    scale_ref, m0_ref, m1_ref, small_ref, gxd_ref, dsum_ref, gout_ref, ggain_ref, loss_ref,
    slots_ref, gm_ref, pack_ref, back_ref, out_sem,
):
    variables = gxd_ref.shape[0]
    wout = small_ref[OUT_ROW : OUT_ROW + variables, :]
    member = pl.program_id(0)

    @pl.when(member == 0)
    def _():
        back_ref[...] = count_rows(send_ref[...], back_ref.shape[0])
        gm_ref[...] = jnp.zeros_like(gm_ref)
        pack_ref[...] = jnp.zeros_like(pack_ref)
        high, low = split_two(gxd_ref[...])
        pack_ref[IN_ROW : IN_ROW + variables, :] = dot(high, wout) + dot(low, wout)
        pack_ref[OUT_ROW : OUT_ROW + variables, :] = gout_ref[...]
        pack_ref[GAIN_ROW + 1 : GAIN_ROW + 3, :] = ggain_ref[...]
        loss = jnp.sum(loss_ref[...], axis=0, keepdims=True)
        pack_ref[LOSS_ROW : LOSS_ROW + 1, :] = jnp.broadcast_to(loss, (1, pack_ref.shape[1]))

    dmesh = dmesh_ref[0] + dot(back_ref[...], ret_ref[0])
    unit = unit_ref[0]
    pack_ref[GAIN_ROW : GAIN_ROW + 1, :] += jnp.sum(dmesh * unit, axis=0, keepdims=True)
    dc = norm_back(dmesh, gain_row(small_ref, 0), unit, scale_ref[0]).astype(BF16)
    gm_ref[1] += dot_tn(h1_ref[0], dc)
    du = (dot_nt(dc, m1_ref[0]) * t1_ref[0]).astype(BF16)
    gm_ref[0] += dot_tn(a0_ref[0], du)
    dagg = dmesh + dot_nt(du, m0_ref[0])
    pack_ref[IN_ROW : IN_ROW + variables, :] += dot_tn(x4_ref[0], dagg.astype(BF16))
    high, low = split_two(dsum_ref[0])
    date = jnp.sum(dagg, axis=0, keepdims=True) + dot_tn(high, wout) + dot_tn(low, wout)
    pack_ref[pl.ds(DATE_ROW + day_ref[member], 1), :] += date

    @pl.when(member == pl.num_programs(0) - 1)
    def _():
        pack_ref[...] = jnp.transpose(pack_ref[...])
        first = pltpu.make_async_copy(gm_ref, slots_ref.at[0:2], out_sem.at[0])
        second = pltpu.make_async_copy(pack_ref, slots_ref.at[7], out_sem.at[1])
        first.start()
        second.start()
        first.wait()
        second.wait()


def whole(shape):
    return pl.BlockSpec(shape, lambda m: (0,) * len(shape))


def per_member(shape):
    return pl.BlockSpec((1,) + shape, lambda m: (m, 0, 0))


def call(kernel, members, in_specs, out_shapes, out_specs, scratch, cost, aliases=None):
    return pl.pallas_call(
        kernel,
        grid=(members,),
        in_specs=in_specs,
        out_shape=out_shapes,
        out_specs=out_specs,
        scratch_shapes=scratch,
        input_output_aliases=aliases or {},
        compiler_params=pltpu.CompilerParams(
            dimension_semantics=("arbitrary",), vmem_limit_bytes=VMEM_BYTES
        ),
        cost_estimate=pl.CostEstimate(flops=cost, bytes_accessed=32 << 20, transcendentals=0),
    )


def shape_of(shape, dtype):
    return jax.ShapeDtypeStruct(shape, dtype)


def neighbours():
    region = lax.axis_index("region")
    slot = lax.rem(region, SLOTS)
    base = region - slot
    one = lax.rem(slot, 2)
    two = lax.rem(slot // 2, 2)
    four = slot // 4
    core = slot + 1 - 2 * one
    side = slot + 2 - 4 * two
    up = slot + 4 - 8 * four
    far = side + 4 - 8 * four
    return base, slot, core, side, up, far


def remote(source, target, send, receive, where):
    return pltpu.make_async_remote_copy(
        src_ref=source, dst_ref=target, send_sem=send, recv_sem=receive,
        device_id=where, device_id_type=MESH,
    )


def greet(places):
    barrier = pltpu.get_barrier_semaphore()
    for place in places:
        pl.semaphore_signal(barrier, inc=1, device_id=place, device_id_type=MESH)
    pl.semaphore_wait(barrier, len(places))


def gather_kernel(
    depth, block_ref, count_ref, full_ref, total_ref, counts_ref, sums_ref, heard_ref,
    local_sem, z_send, z_recv, p_send, p_recv, d_send, d_recv, c_send, c_recv, n_send, n_recv,
    s_send, s_recv,
):
    base, slot, core, side, up, far = neighbours()
    z = lax.axis_index("row")
    half = block_ref.shape[1] // 2
    low, high = pl.ds(0, half), pl.ds(half, half)
    to_core, to_side, to_up = ({"region": base + place} for place in (core, side, up))
    to_z = [None] + [{"row": lax.rem(z + d, depth)} for d in range(1, depth)]
    source = [z] + [lax.rem(z + depth - d, depth) for d in range(1, depth)]
    steps = range(1, depth)
    greet(to_z[1:] + [to_core, to_side, to_up])

    own = pltpu.make_async_copy(block_ref, full_ref.at[:, z], local_sem)
    sent = []

    def send(*args):
        copy = remote(*args)
        copy.start()
        sent.append(copy)

    def arrived(target, receive):
        remote(target, target, receive, receive, to_core).wait_recv()

    for d in steps:
        send(block_ref.at[slot], full_ref.at[slot, z], z_send.at[d], z_recv.at[d], to_z[d])
    own.start()
    for d in steps:
        send(count_ref, counts_ref.at[d], n_send.at[d], n_recv.at[d], to_z[d])
    for d in steps:
        chunk = full_ref.at[slot, source[d]]
        arrived(chunk, z_recv.at[d])
        send(chunk, chunk, p_send.at[0, d], p_recv.at[0, d], to_side)
        send(chunk, chunk, p_send.at[1, d], p_recv.at[1, d], to_up)
        send(chunk, chunk, c_send.at[0, d], c_recv.at[0, d], to_core)

    total = count_ref[...]
    for d in steps:
        arrived(counts_ref.at[d], n_recv.at[d])
        total = total + counts_ref[d]
    sums_ref[0] = total
    send(sums_ref.at[0], heard_ref.at[0], s_send.at[0], s_recv.at[0], to_core)

    for d in steps:
        chunk = full_ref.at[side, source[d]]
        arrived(chunk, p_recv.at[0, d])
        part = full_ref.at[side, source[d], low]
        send(part, part, d_send.at[0, d], d_recv.at[0, d], to_up)
        send(chunk, chunk, c_send.at[1, d], c_recv.at[1, d], to_core)
        chunk = full_ref.at[up, source[d]]
        arrived(chunk, p_recv.at[1, d])
        part = full_ref.at[up, source[d], high]
        send(part, part, d_send.at[1, d], d_recv.at[1, d], to_side)
        send(chunk, chunk, c_send.at[2, d], c_recv.at[2, d], to_core)

    for step, place in ((1, to_side), (2, to_up)):
        arrived(heard_ref.at[step - 1], s_recv.at[step - 1])
        total = total + heard_ref[step - 1]
        sums_ref[step] = total
        send(sums_ref.at[step], heard_ref.at[step], s_send.at[step], s_recv.at[step], place)

    for d in steps:
        arrived(full_ref.at[far, source[d], low], d_recv.at[0, d])
        arrived(full_ref.at[far, source[d], high], d_recv.at[1, d])
        chunk = full_ref.at[far, source[d]]
        send(chunk, chunk, c_send.at[3, d], c_recv.at[3, d], to_core)
    arrived(heard_ref.at[2], s_recv.at[2])
    total_ref[...] = total + heard_ref[2]
    for d in steps:
        for k in range(4):
            arrived(full_ref.at[core, source[d]], c_recv.at[k, d])
    for copy in sent:
        copy.wait_send()
    own.wait()


def gather_weights(block, count, depth):
    hbm = pl.BlockSpec(memory_space=pl.ANY)
    vmem = pl.BlockSpec(memory_space=pltpu.VMEM)
    dma = pltpu.SemaphoreType.DMA
    rows, width = block.shape[1:]
    return pl.pallas_call(
        partial(gather_kernel, depth),
        in_specs=[vmem, vmem],
        out_shape=[
            shape_of((SLOTS, depth, rows, width), BF16),
            shape_of(count.shape, F32),
        ],
        out_specs=[hbm, vmem],
        scratch_shapes=[
            pltpu.VMEM((depth,) + count.shape, F32),
            pltpu.VMEM((3,) + count.shape, F32),
            pltpu.VMEM((3,) + count.shape, F32),
            dma,
            dma((depth,)),
            dma((depth,)),
            dma((2, depth)),
            dma((2, depth)),
            dma((2, depth)),
            dma((2, depth)),
            dma((4, depth)),
            dma((4, depth)),
            dma((depth,)),
            dma((depth,)),
            dma((3,)),
            dma((3,)),
        ],
        compiler_params=pltpu.CompilerParams(
            collective_id=0, has_side_effects=True, vmem_limit_bytes=VMEM_BYTES
        ),
    )(block, count)


def reduce_kernel(
    depth, slots_ref, momentum_ref, count_ref, g_ref, x_ref,
    own_ref, heard_ref, snd_ref, rcv_ref, snd_low_ref, rcv_low_ref, acc_ref, zr_ref, g_own_ref,
    mb_ref, x_own_ref,
    l_sem, h_send, h_recv, p_send, p_recv, q_send, q_recv, z_send, z_recv, m_send, m_recv,
    g_local, g_send, g_recv, x_local, x_send, x_recv,
):
    base, slot, core, side, up, far = neighbours()
    z = lax.axis_index("row")
    rows = acc_ref.shape[0] // depth
    places = (far, side, up, slot)
    to_core, to_side, to_up, to_far = ({"region": base + place} for place in (core, side, up, far))
    to_place = (to_far, to_side, to_up)
    to_z = [None] + [{"row": lax.rem(z + d, depth)} for d in range(1, depth)]
    greet(to_z[1:] + [to_core, to_side, to_up, to_far])
    shift = core - slot
    last = SLOTS - 1
    sent = []

    def send(*args):
        copy = remote(*args)
        copy.start()
        sent.append(copy)

    def arrived(target, receive):
        remote(target, target, receive, receive, to_core).wait_recv()

    loads = []
    for b in range(depth):
        part = pl.ds(b * rows, rows)
        for k, place in enumerate(places):
            send(
                slots_ref.at[place + shift, part], heard_ref.at[k, part],
                h_send.at[k, b], h_recv.at[k, b], to_core,
            )
            copy = pltpu.make_async_copy(
                slots_ref.at[place, part], own_ref.at[k, part], l_sem.at[k, b]
            )
            copy.start()
            loads.append(copy)

    for b in range(depth):
        part = pl.ds(b * rows, rows)
        for k in range(4):
            loads[b * 4 + k].wait()
            arrived(heard_ref.at[k, part], h_recv.at[k, b])
            total = own_ref[k, part, :] + heard_ref[k, part, :]
            if k == 3:
                acc_ref[part, :] = total
                continue
            snd_ref[k, part, :] = total.astype(BF16)
            send(
                snd_ref.at[k, part], rcv_ref.at[k, part], p_send.at[k, b], p_recv.at[k, b],
                to_place[k],
            )

            @pl.when(places[k] == last)
            def _():
                snd_low_ref[part, :] = (total - total.astype(BF16).astype(F32)).astype(BF16)
                remote(
                    snd_low_ref.at[part], rcv_low_ref.at[k, part], q_send.at[b], q_recv.at[k, b],
                    to_place[k],
                ).start()

    for b in range(depth):
        part = pl.ds(b * rows, rows)
        total = acc_ref[part, :]
        for k in range(3):
            arrived(rcv_ref.at[k, part], p_recv.at[k, b])
            total = total + rcv_ref[k, part, :].astype(F32)
        acc_ref[part, :] = total

        @pl.when(slot == last)
        def _():
            low = acc_ref[part, :]
            for k in range(3):
                arrived(rcv_low_ref.at[k, part], q_recv.at[k, b])
                low = low + rcv_low_ref[k, part, :].astype(F32)
            acc_ref[part, :] = low

        @pl.when(z != b)
        def _():
            d = lax.rem(b - z + depth, depth)
            remote(
                acc_ref.at[part], zr_ref.at[d], z_send.at[b], z_recv.at[d], {"row": b + 0 * z}
            ).start()

    g_own = acc_ref[pl.ds(pl.multiple_of(z * rows, rows), rows), :]
    for d in range(1, depth):
        arrived(zr_ref.at[d], z_recv.at[d])
        g_own = g_own + zr_ref[d]
    g_own_ref[...] = g_own
    momentum = MUON_MOMENTUM * momentum_ref[slot - slot // last] + (2.0 / count_ref[0:1, 0:1]) * g_own
    mb_ref[0] = momentum.astype(BF16)
    for d in range(1, depth):
        send(mb_ref.at[0], mb_ref.at[d], m_send.at[d], m_recv.at[d], to_z[d])
    g_copy = pltpu.make_async_copy(g_own_ref, g_ref.at[slot], g_local)
    g_copy.start()
    for k in range(3):
        send(g_own_ref, g_ref.at[slot], g_send.at[k], g_recv.at[k], to_place[k])
    send(g_own_ref, g_ref.at[slot], g_send.at[3], g_recv.at[3], to_core)

    for d in range(1, depth):
        arrived(mb_ref.at[d], m_recv.at[d])
    everything = jnp.concatenate([mb_ref[d] for d in range(depth)], axis=0)
    wide = everything.astype(F32)
    squares = jnp.sum(jnp.sum(wide * wide, axis=1, keepdims=True), axis=0, keepdims=True)
    inverse = lax.rsqrt(squares + 1e-07)
    mine = momentum * inverse
    current = (wide * inverse).astype(BF16)
    mine_low = mine.astype(BF16)
    for sweep in range(NS_ITERS):
        gram = dot_tn(current, current)
        gram_low = gram.astype(BF16)
        mixing = NS_COEFFS[1] * gram + NS_COEFFS[2] * dot(gram_low, gram_low)
        mixing = mixing.astype(BF16)
        mine = NS_COEFFS[0] * mine + dot(mine_low, mixing)
        mine_low = mine.astype(BF16)
        if sweep < NS_ITERS - 1:
            current = (NS_COEFFS[0] * current.astype(F32) + dot(current, mixing)).astype(BF16)
    x_own_ref[...] = mine_low
    x_copy = pltpu.make_async_copy(x_own_ref, x_ref.at[slot], x_local)
    x_copy.start()
    for k in range(3):
        send(x_own_ref, x_ref.at[slot], x_send.at[k], x_recv.at[k], to_place[k])
    send(x_own_ref, x_ref.at[slot], x_send.at[3], x_recv.at[3], to_core)

    for target, send_sem, recv_sem in ((g_ref, g_send, g_recv), (x_ref, x_send, x_recv)):
        for k in range(3):
            chunk = target.at[places[k]]
            arrived(chunk, recv_sem.at[k])
            send(chunk, chunk, send_sem.at[4 + k], recv_sem.at[4 + k], to_core)
    for target, recv_sem in ((g_ref, g_recv), (x_ref, x_recv)):
        for k in range(3, 7):
            arrived(target.at[core], recv_sem.at[k])
    for copy in sent:
        copy.wait_send()
    for b in range(depth):
        part = pl.ds(b * rows, rows)
        for k in range(3):

            @pl.when(places[k] == last)
            def _():
                remote(
                    snd_low_ref.at[part], rcv_low_ref.at[k, part], q_send.at[b], q_recv.at[k, b],
                    to_place[k],
                ).wait_send()

        @pl.when(z != b)
        def _():
            remote(
                acc_ref.at[part], acc_ref.at[part], z_send.at[b], z_send.at[b], to_core
            ).wait_send()

    g_copy.wait()
    x_copy.wait()


def reduce_gradients(slots, momentum, count, depth):
    hbm = pl.BlockSpec(memory_space=pl.ANY)
    vmem = pl.BlockSpec(memory_space=pltpu.VMEM)
    dma = pltpu.SemaphoreType.DMA
    height, width = slots.shape[1:]
    rows = height // depth
    return pl.pallas_call(
        partial(reduce_kernel, depth),
        in_specs=[hbm, vmem, vmem],
        out_shape=[
            shape_of((SLOTS, rows, width), F32),
            shape_of((SLOTS, rows, width), BF16),
        ],
        out_specs=[hbm, hbm],
        scratch_shapes=[
            pltpu.VMEM((4, height, width), F32),
            pltpu.VMEM((4, height, width), F32),
            pltpu.VMEM((3, height, width), BF16),
            pltpu.VMEM((3, height, width), BF16),
            pltpu.VMEM((height, width), BF16),
            pltpu.VMEM((3, height, width), BF16),
            pltpu.VMEM((height, width), F32),
            pltpu.VMEM((depth, rows, width), F32),
            pltpu.VMEM((rows, width), F32),
            pltpu.VMEM((depth, rows, width), BF16),
            pltpu.VMEM((rows, width), BF16),
            dma((4, depth)),
            dma((4, depth)),
            dma((4, depth)),
            dma((3, depth)),
            dma((3, depth)),
            dma((depth,)),
            dma((3, depth)),
            dma((depth,)),
            dma((depth,)),
            dma((depth,)),
            dma((depth,)),
            dma,
            dma((7,)),
            dma((7,)),
            dma,
            dma((7,)),
            dma((7,)),
        ],
        compiler_params=pltpu.CompilerParams(
            collective_id=1, has_side_effects=True, vmem_limit_bytes=VMEM_BYTES
        ),
    )(slots, momentum, count)


def cyclic(block, halo):
    count = lax.axis_size("region")
    forward = [(i, (i + 1) % count) for i in range(count)]
    backward = [(target, source) for source, target in forward]
    low = lax.ppermute(block[:, -halo:], "region", forward)
    high = lax.ppermute(block[:, :halo], "region", backward)
    return low, high


def adam_update(weight, gradient, first_moment, second_moment, step_rate, decay_rate):
    first_new = BETA_ONE * first_moment + (1.0 - BETA_ONE) * gradient
    second_new = BETA_TWO * second_moment + (1.0 - BETA_TWO) * gradient * gradient
    unbiased_one = first_new / (1.0 - BETA_ONE**STEP)
    unbiased_two = second_new / (1.0 - BETA_TWO**STEP)
    weight_new = weight * (1.0 - step_rate * decay_rate) - step_rate * unbiased_one / (
        jnp.sqrt(unbiased_two) + 1e-08
    )
    return (weight_new, first_new, second_new)


def body(
    inputs,
    targets,
    valid_steps,
    var_weights,
    grid_to_mesh,
    mesh_edges,
    send_rows,
    mesh_to_grid,
    date_index,
    matrices,
    matrices_momentum,
    in_proj,
    in_first,
    in_second,
    out_proj,
    out_first,
    out_second,
    norm_gains,
    gains_first,
    gains_second,
    date_table,
    date_first,
    date_second,
):
    inputs = jnp.swapaxes(inputs, 1, 2)
    targets = jnp.swapaxes(targets, 1, 2)
    members, variables, points = inputs.shape
    nodes = grid_to_mesh.shape[0]
    halo = send_rows.shape[0] // 2
    table = nodes + 2 * halo
    k_edge = mesh_edges.shape[1]
    k_pick = mesh_to_grid.shape[1]
    dates = date_table.shape[0]

    depth = lax.axis_size("row")
    regions = lax.axis_size("region")
    groups = [[g * SLOTS + q for g in range(regions // SLOTS)] for q in range(SLOTS)]
    scalars = pl.BlockSpec(memory_space=pltpu.SMEM)
    hbm = pl.BlockSpec(memory_space=pl.ANY)
    share = matrices.shape[1]

    def stacked(in_part, out_part, gain_part, date_part):
        blank = lambda rows: jnp.zeros((rows, share), in_part.dtype)
        return jnp.concatenate(
            [
                in_part, blank(OUT_ROW - variables),
                out_part, blank(GAIN_ROW - OUT_ROW - variables),
                gain_part, blank(DATE_ROW - GAIN_ROW - gain_part.shape[0]),
                date_part, blank(LATENT - DATE_ROW - dates),
            ],
            axis=0,
        )

    small = stacked(in_proj, out_proj.T, norm_gains, date_table)
    block = jnp.concatenate([matrices, small.T[None]], axis=0).astype(BF16)
    local_count = jnp.full((8, 128), jnp.sum(valid_steps).astype(F32))
    gathered, count = gather_weights(block, local_count, depth)
    if regions > SLOTS:
        count = lax.psum(count, "region", axis_index_groups=groups)
    valid_count = count[0, 0]
    weights = gathered.reshape(SLOTS, LATENT, LATENT)
    small = weights[SLOTS - 1].T

    node_block = per_member((nodes, LATENT))
    full_slot = whole((LATENT, LATENT))

    def matrix(j):
        return pl.BlockSpec((1, LATENT, LATENT), lambda m: (j, 0, 0))

    x4, a0, h1, t1, unit1, scale1, mesh1, sent, buf = call(
        encode_kernel,
        members,
        [
            scalars,
            per_member((variables, points)),
            whole((grid_to_mesh.shape[1], nodes)),
            full_slot,
            matrix(0),
            matrix(1),
            whole((1, 2 * halo)),
        ],
        [
            shape_of((members, nodes, variables), BF16),
            shape_of((members, nodes, LATENT), BF16),
            shape_of((members, nodes, LATENT), BF16),
            shape_of((members, nodes, LATENT), F32),
            shape_of((members, nodes, LATENT), F32),
            shape_of((members, nodes, 1), F32),
            shape_of((members, nodes, LATENT), F32),
            shape_of((members, nodes, LATENT), BF16),
            shape_of((members, 2 * halo, LATENT), BF16),
        ],
        [
            per_member((nodes, variables)),
            node_block,
            node_block,
            node_block,
            node_block,
            per_member((nodes, 1)),
            node_block,
            node_block,
            per_member((2 * halo, LATENT)),
        ],
        [pltpu.VMEM((nodes, points), BF16), pltpu.VMEM((2 * halo, nodes), BF16)],
        6_000_000_000,
    )(
        date_index, inputs, grid_to_mesh.T, small, weights, weights, send_rows[None, :],
    )
    left, right = cyclic(buf, halo)

    out_shape = (variables, LATENT)
    slots, gout, gxd, dsum, ggain_late, loss_row, dmesh, dhalo = call(
        main_kernel,
        members,
        [
            scalars,
            node_block,
            node_block,
            per_member((halo, LATENT)),
            per_member((halo, LATENT)),
            per_member((variables, points)),
            per_member((variables, points)),
            whole((members, points)),
            whole((variables, 1)),
            whole((k_edge, nodes)),
            whole((k_pick, points)),
            full_slot,
            matrix(2),
            matrix(3),
            matrix(4),
            matrix(5),
            matrix(6),
        ],
        [
            shape_of((SLOTS, LATENT, LATENT), F32),
            shape_of(out_shape, F32),
            shape_of((variables, variables), F32),
            shape_of((members, variables, 1), F32),
            shape_of((2, LATENT), F32),
            shape_of((variables, 1), F32),
            shape_of((members, nodes, LATENT), F32),
            shape_of((members, 2 * halo, LATENT), BF16),
        ],
        [
            hbm,
            whole(out_shape),
            whole((variables, variables)),
            per_member((variables, 1)),
            whole((2, LATENT)),
            whole((variables, 1)),
            node_block,
            per_member((2 * halo, LATENT)),
        ],
        [
            pltpu.VMEM((5, LATENT, LATENT), F32),
            pltpu.SemaphoreType.DMA,
            pltpu.VMEM((k_edge * nodes, table), BF16),
            pltpu.VMEM((table, k_edge * nodes), BF16),
            pltpu.VMEM((points, nodes), BF16),
            pltpu.VMEM((nodes, points), BF16),
            pltpu.VMEM((table, LATENT), BF16),
            pltpu.VMEM((k_edge * nodes, LATENT), T_TYPE),
            pltpu.VMEM((2 * nodes, LATENT), BF16),
            pltpu.VMEM((nodes, LATENT), F32),
        ],
        60_000_000_000,
    )(
        date_index,
        mesh1,
        sent,
        left,
        right,
        inputs,
        targets,
        valid_steps,
        var_weights[:, None],
        mesh_edges.T,
        mesh_to_grid.T,
        small,
        weights,
        weights,
        weights,
        weights,
        weights,
    )

    from_previous, from_next = cyclic(
        jnp.concatenate([dhalo[:, :halo], dhalo[:, halo:]], axis=1), halo
    )
    returned = jnp.concatenate([from_previous, from_next], axis=1)
    (slots,) = call(
        encode_back_kernel,
        members,
        [
            scalars,
            hbm,
            node_block,
            per_member((2 * halo, LATENT)),
            whole((1, 2 * halo)),
            per_member((nodes, variables)),
            node_block,
            node_block,
            node_block,
            node_block,
            per_member((nodes, 1)),
            matrix(0),
            matrix(1),
            full_slot,
            whole((variables, variables)),
            per_member((variables, 1)),
            whole(out_shape),
            whole((2, LATENT)),
            whole((variables, 1)),
        ],
        [shape_of(slots.shape, F32)],
        [hbm],
        [
            pltpu.VMEM((2, LATENT, LATENT), F32),
            pltpu.VMEM((LATENT, LATENT), F32),
            pltpu.VMEM((nodes, 2 * halo), BF16),
            pltpu.SemaphoreType.DMA((2,)),
        ],
        4_000_000_000,
        {1: 0},
    )(
        date_index, slots, dmesh, returned, send_rows[None, :], x4, a0, h1, t1, unit1, scale1, weights,
        weights, small, gxd, dsum, gout, ggain_late, loss_row,
    )
    if regions > SLOTS:
        slots = lax.psum(slots, "region", axis_index_groups=groups)
    sums, turned = reduce_gradients(slots, matrices_momentum, count, depth)
    rest = sums[SLOTS - 1].T
    loss_sum = rest[LOSS_ROW, 0]
    rest = rest * (2.0 / valid_count)
    g_matrices = sums[: SLOTS - 1] * (2.0 / valid_count)
    g_in = rest[IN_ROW : IN_ROW + variables]
    g_out = rest[OUT_ROW : OUT_ROW + variables]
    g_gains = rest[GAIN_ROW : GAIN_ROW + norm_gains.shape[0]]
    g_dates = rest[DATE_ROW : DATE_ROW + dates]
    current = turned[: SLOTS - 1].astype(F32)
    new_momentum = MUON_MOMENTUM * matrices_momentum + g_matrices
    new_matrices = matrices * (1.0 - MUON_RATE * WEIGHT_DECAY) - MUON_RATE * current
    new_in = adam_update(in_proj, g_in, in_first, in_second, MATRIX_RATE, WEIGHT_DECAY)
    new_out = adam_update(out_proj, g_out.T, out_first, out_second, MATRIX_RATE, WEIGHT_DECAY)
    new_gain = adam_update(norm_gains, g_gains, gains_first, gains_second, VECTOR_RATE, 0.0)
    new_date = adam_update(date_table, g_dates, date_first, date_second, VECTOR_RATE, 0.0)
    return (
        new_matrices,
        new_momentum,
        new_in[0],
        new_in[1],
        new_in[2],
        new_out[0],
        new_out[1],
        new_out[2],
        new_gain[0],
        new_gain[1],
        new_gain[2],
        new_date[0],
        new_date[1],
        new_date[2],
        loss_sum,
        valid_count,
    )


def solution(mesh):
    in_specs = (
        P("row", "region", None),
        P("row", "region", None),
        P("row", "region"),
        P(),
        P("region", None),
        P("region", None),
        P("region"),
        P("region", None),
        P("row"),
        P(None, "row", None),
        P(None, "row", None),
        P(None, "row"),
        P(None, "row"),
        P(None, "row"),
        P("row", None),
        P("row", None),
        P("row", None),
        P(None, "row"),
        P(None, "row"),
        P(None, "row"),
        P(None, "row"),
        P(None, "row"),
        P(None, "row"),
    )
    out_specs = (
        P(None, "row", None),
        P(None, "row", None),
        P(None, "row"),
        P(None, "row"),
        P(None, "row"),
        P("row", None),
        P("row", None),
        P("row", None),
        P(None, "row"),
        P(None, "row"),
        P(None, "row"),
        P(None, "row"),
        P(None, "row"),
        P(None, "row"),
        P(),
        P(),
    )
    return jax.shard_map(body, mesh=mesh, in_specs=in_specs, out_specs=out_specs, check_vma=False)
```

```python
from functools import partial

import jax
import jax.numpy as jnp
from jax import lax
from jax.experimental import pallas as pl
from jax.experimental.pallas import tpu as pltpu
from jax.sharding import PartitionSpec as P

NS_ITERS = 2
STEP = 10
NS_COEFFS = (3.4445, -4.775, 2.0315)
MUON_RATE = 0.8
MUON_MOMENTUM = 0.95
MATRIX_RATE = 0.05
VECTOR_RATE = 0.2
BETA_ONE = 0.9
BETA_TWO = 0.95
WEIGHT_DECAY = 0.01

F32 = jnp.float32
BF16 = jnp.bfloat16
LATENT = 512
BLOCK = 1024
T_TYPE = BF16
VMEM_BYTES = 60 * 1024 * 1024
MESH = pl.DeviceIdType.MESH
SLOTS = 8
SMALL = 3
IN_ROW, OUT_ROW, GAIN_ROW, DATE_ROW, LOSS_ROW = 0, 240, 480, 496, 504


def dot(left, right):
    return jnp.dot(left, right, preferred_element_type=F32)


def dot_nt(left, right):
    return lax.dot_general(left, right, (((1,), (1,)), ((), ())), preferred_element_type=F32)


def dot_tn(left, right):
    return lax.dot_general(left, right, (((0,), (0,)), ((), ())), preferred_element_type=F32)


def split_two(values):
    high = values.astype(BF16)
    return high, (values - high.astype(F32)).astype(BF16)


def silu_parts(half):
    bend = jnp.tanh(half)
    gate = 0.5 * bend + 0.5
    hid = half * bend + half
    return hid, gate + hid * (1.0 - gate)


def normalise(values):
    centred = values - jnp.mean(values, axis=-1, keepdims=True)
    spread = jnp.mean(centred * centred, axis=-1, keepdims=True)
    scale = lax.rsqrt(spread + 1e-05)
    return centred * scale, scale


def norm_back(grad, gain, unit, scale):
    scaled = gain * grad
    mean_one = jnp.mean(scaled, axis=-1, keepdims=True)
    mean_two = jnp.mean(scaled * unit, axis=-1, keepdims=True)
    return scale * (scaled - mean_one - unit * mean_two)


def count_columns(index, width, count):
    lanes = lax.broadcasted_iota(jnp.int32, (index.shape[0], width), 1)
    total = None
    for k in range(count):
        one = jnp.where(lanes == index[:, k : k + 1], 1.0, 0.0)
        total = one if total is None else total + one
    return total.astype(BF16)


def gain_row(small_ref, k):
    return small_ref[GAIN_ROW : GAIN_ROW + 16, :].astype(F32)[k : k + 1, :]


def date_row(small_ref, day):
    table = small_ref[DATE_ROW : DATE_ROW + 16, :].astype(F32)
    lines = lax.broadcasted_iota(jnp.int32, table.shape, 0)
    return jnp.sum(jnp.where(lines == day, table, 0.0), axis=0, keepdims=True)


def columns_of(index):
    short = 8 - index.shape[0]
    if short > 0:
        index = jnp.concatenate([index, jnp.zeros((short, index.shape[1]), index.dtype)], axis=0)
    return jnp.transpose(index)


def count_rows(index, height):
    lines = lax.broadcasted_iota(jnp.int32, (height, index.shape[1]), 0)
    total = None
    for k in range(index.shape[0]):
        one = jnp.where(lines == index[k : k + 1, :], 1.0, 0.0)
        total = one if total is None else total + one
    return total.astype(BF16)


def main_kernel(
    day_ref, mesh_ref, sent_ref, left_ref, right_ref, x_ref, y_ref, valid_ref, varw_ref,
    edge_ref, pick_row_ref, small_ref, m2_ref, m3_ref, m4_ref, m5_ref, m6_ref,
    slots_ref, gout_ref, gxd_ref, dsum_ref, ggain_ref, loss_ref, dmesh_ref, dhalo_ref,
    gm_ref, out_sem, eh_ref, eht_ref, d_ref, dt_ref, ext_ref, t_ref, mm_ref, acc_ref,
):
    nodes = mesh_ref.shape[1]
    table = ext_ref.shape[0]
    variables, points = x_ref.shape[1:]
    k_edge = edge_ref.shape[0]
    k_pick = pick_row_ref.shape[0]
    halo = left_ref.shape[1]

    @pl.when(pl.program_id(0) == 0)
    def _():
        edge_columns = columns_of(edge_ref[...])
        for k in range(k_edge):
            rows = slice(k * nodes, (k + 1) * nodes)
            eh_ref[rows, :] = count_columns(edge_columns[:, k : k + 1], table, 1)
            eht_ref[:, rows] = count_rows(edge_ref[k : k + 1, :], table)

        def build(i, carry):
            rows = pl.ds(pl.multiple_of(i * BLOCK, BLOCK), BLOCK)
            picks = pick_row_ref[:, rows]
            d_ref[rows, :] = count_columns(columns_of(picks), nodes, k_pick)
            dt_ref[:, rows] = count_rows(picks, nodes)
            return carry

        lax.fori_loop(0, points // BLOCK, build, 0)
        gm_ref[...] = jnp.zeros_like(gm_ref)
        gout_ref[...] = jnp.zeros_like(gout_ref)
        gxd_ref[...] = jnp.zeros_like(gxd_ref)
        ggain_ref[...] = jnp.zeros_like(ggain_ref)
        loss_ref[...] = jnp.zeros_like(loss_ref)

    sent = sent_ref[0]
    ext_ref[:nodes, :] = sent
    ext_ref[nodes : nodes + halo, :] = left_ref[0]
    ext_ref[nodes + halo :, :] = right_ref[0]
    receivers = 0.5 * dot(sent, m3_ref[0])

    def edge(k, carry):
        hid_sum, t_sum = carry
        rows = pl.ds(pl.multiple_of(k * nodes, nodes), nodes)
        picked = dot(eh_ref[rows, :], ext_ref[...]).astype(BF16)
        hid, t = silu_parts(0.5 * dot(picked, m2_ref[0]) + receivers)
        t_ref[rows, :] = t.astype(t_ref.dtype)
        return hid_sum + hid.astype(BF16).astype(F32), t_sum + t

    zero = jnp.zeros((nodes, LATENT), F32)
    hid_sum, t_sum = lax.fori_loop(0, k_edge, edge, (zero, zero), unroll=k_edge)
    h_high, h_low = split_two(hid_sum * (1.0 / k_edge))
    m4 = m4_ref[0]
    gain2 = gain_row(small_ref, 1)
    unit2, scale2 = normalise(dot(h_high, m4) + dot(h_low, m4))
    mesh2 = mesh_ref[0] + unit2 * gain2
    mm_ref[...] = mesh2.astype(BF16)

    acc_ref[...] = jnp.zeros_like(acc_ref)
    dsum_ref[...] = jnp.zeros_like(dsum_ref)
    member = pl.program_id(0)
    date = date_row(small_ref, day_ref[member])
    gain3 = gain_row(small_ref, 2)
    wout = small_ref[OUT_ROW : OUT_ROW + variables, :]
    varw = varw_ref[...]

    def grid_block(i, carry):
        rows = pl.ds(pl.multiple_of(i * BLOCK, BLOCK), BLOCK)
        picks = d_ref[rows, :]
        dec = dot(picks, mm_ref[...])
        a2 = (dec * (1.0 / k_pick)).astype(BF16)
        hid, t = silu_parts(0.5 * dot(a2, m5_ref[0]))
        h2 = hid.astype(BF16)
        unit, scale = normalise(dot(h2, m6_ref[0]))
        x = x_ref[0, :, rows]
        grid = dot_tn(x, small_ref[IN_ROW : IN_ROW + variables, :]) + date + unit * gain3
        grid = grid.astype(BF16)
        misfit = x.astype(F32) + dot_nt(wout, grid) - y_ref[0, :, rows].astype(F32)
        valid = valid_ref[pl.ds(member, 1), rows].astype(F32)
        weighted = valid * varw * misfit
        loss_ref[...] += jnp.sum(weighted * misfit, axis=1, keepdims=True)
        dsum_ref[0] += jnp.sum(weighted, axis=1, keepdims=True)
        dp = weighted.astype(BF16)
        gout_ref[...] += dot(dp, grid)
        gxd_ref[...] += dot_nt(x, dp)
        dgrid = dot_tn(dp, wout)
        ggain_ref[1:2, :] += jnp.sum(dgrid * unit, axis=0, keepdims=True)
        dc = norm_back(dgrid, gain3, unit, scale).astype(BF16)
        gm_ref[4] += dot_tn(h2, dc)
        du = (dot_nt(dc, m6_ref[0]) * t).astype(BF16)
        gm_ref[3] += dot_tn(a2, du)
        ddec = dot_nt(du, m5_ref[0]).astype(BF16)
        acc_ref[...] += dot(dt_ref[:, rows], ddec)
        return carry

    lax.fori_loop(0, points // BLOCK, grid_block, 0)

    dmesh2 = acc_ref[...] * (1.0 / k_pick)
    ggain_ref[0:1, :] += jnp.sum(dmesh2 * unit2, axis=0, keepdims=True)
    dagg = norm_back(dmesh2, gain2, unit2, scale2).astype(BF16)
    gm_ref[2] += dot_tn(h_high, dagg)
    dhid = dot_nt(dagg, m4_ref[0]) * (1.0 / k_edge)
    dr = (dhid * t_sum).astype(BF16)
    gm_ref[1] += dot_tn(sent, dr)

    def edge_back(k, total):
        rows = pl.ds(pl.multiple_of(k * nodes, nodes), nodes)
        dpre = (dhid * t_ref[rows, :].astype(F32)).astype(BF16)
        return total + dot(eht_ref[:, rows], dpre)

    ds = lax.fori_loop(
        0, k_edge, edge_back, jnp.zeros((table, LATENT), F32), unroll=k_edge
    ).astype(BF16)
    gm_ref[0] += dot_tn(ext_ref[...], ds)
    dext = dot_nt(ds, m2_ref[0])
    dmesh_ref[0] = dmesh2 + dext[:nodes, :] + dot_nt(dr, m3_ref[0])
    dhalo_ref[0] = dext[nodes:, :].astype(BF16)

    @pl.when(member == pl.num_programs(0) - 1)
    def _():
        copy = pltpu.make_async_copy(gm_ref, slots_ref, out_sem)
        copy.start()
        copy.wait()


def main_scratch(k_edge, nodes, points, table):
    return [
        pltpu.VMEM((5, LATENT, LATENT), F32),
        pltpu.SemaphoreType.DMA,
        pltpu.VMEM((k_edge * nodes, table), BF16),
        pltpu.VMEM((table, k_edge * nodes), BF16),
        pltpu.VMEM((points, nodes), BF16),
        pltpu.VMEM((nodes, points), BF16),
        pltpu.VMEM((table, LATENT), BF16),
        pltpu.VMEM((k_edge * nodes, LATENT), T_TYPE),
        pltpu.VMEM((nodes, LATENT), BF16),
        pltpu.VMEM((nodes, LATENT), F32),
    ]


def whole(shape):
    return pl.BlockSpec(shape, lambda m: (0,) * len(shape))


def per_member(shape):
    return pl.BlockSpec((1,) + shape, lambda m: (m, 0, 0))


def call(kernel, members, in_specs, out_shapes, out_specs, scratch, cost, aliases=None):
    return pl.pallas_call(
        kernel,
        grid=(members,),
        in_specs=in_specs,
        out_shape=out_shapes,
        out_specs=out_specs,
        scratch_shapes=scratch,
        input_output_aliases=aliases or {},
        compiler_params=pltpu.CompilerParams(
            dimension_semantics=("arbitrary",), vmem_limit_bytes=VMEM_BYTES
        ),
        cost_estimate=pl.CostEstimate(flops=cost, bytes_accessed=32 << 20, transcendentals=0),
    )


def shape_of(shape, dtype):
    return jax.ShapeDtypeStruct(shape, dtype)


def neighbours():
    region = lax.axis_index("region")
    slot = lax.rem(region, SLOTS)
    base = region - slot
    one = lax.rem(slot, 2)
    two = lax.rem(slot // 2, 2)
    four = slot // 4
    core = slot + 1 - 2 * one
    side = slot + 2 - 4 * two
    up = slot + 4 - 8 * four
    far = side + 4 - 8 * four
    return base, slot, core, side, up, far


def remote(source, target, send, receive, where):
    return pltpu.make_async_remote_copy(
        src_ref=source, dst_ref=target, send_sem=send, recv_sem=receive,
        device_id=where, device_id_type=MESH,
    )


def greet(places):
    barrier = pltpu.get_barrier_semaphore()
    for place in places:
        pl.semaphore_signal(barrier, inc=1, device_id=place, device_id_type=MESH)
    pl.semaphore_wait(barrier, len(places))


def around():
    region, count = lax.axis_index("region"), lax.axis_size("region")
    following, previous = lax.rem(region + 1, count), lax.rem(region + count - 1, count)
    return {"region": following}, {"region": previous}


def encode_kernel(
    depth, day_ref, matrices_ref, in_ref, outp_ref, gains_ref, dates_ref, valid_ref, x_ref, picks_ref,
    rows_ref,
    full_ref, small_out_ref, total_ref, x4_out, a0_out, h1_out, t1_out, unit_out, scale_out, mesh_out,
    sent_out, left_ref, right_ref,
    block_ref, pack_ref, pick_ref, out_ref, x4_ref, xl_ref, a0_ref, h1_ref, t1_ref, unit_ref, scale_ref,
    mesh_ref, sent_ref, buf_ref, w_ref, small_ref, count_ref, counts_ref, sums_ref, heard_ref,
    local_sem, z_send, z_recv, p_send, p_recv, d_send, d_recv, c_send, c_recv, n_send, n_recv,
    s_send, s_recv, w_sem, o_sem, e_send, e_recv, q_sem,
):
    base, slot, core, side, up, far = neighbours()
    z = lax.axis_index("row")
    half = block_ref.shape[1] // 2
    low, high = pl.ds(0, half), pl.ds(half, half)
    to_core, to_side, to_up = ({"region": base + place} for place in (core, side, up))
    to_next, to_previous = around()
    to_z = [None] + [{"row": lax.rem(z + d, depth)} for d in range(1, depth)]
    source = [z] + [lax.rem(z + depth - d, depth) for d in range(1, depth)]
    steps = range(1, depth)
    members, variables, points = x_ref.shape
    nodes = a0_ref.shape[1]
    halo = left_ref.shape[1]
    greet(to_z[1:] + [to_core, to_side, to_up, to_next, to_previous])
    sent = []
    local = []

    def send(*args):
        copy = remote(*args)
        copy.start()
        sent.append(copy)

    def arrived(target, receive):
        remote(target, target, receive, receive, to_core).wait_recv()

    def keep(*args):
        copy = pltpu.make_async_copy(*args)
        copy.start()
        local.append(copy)

    for k in range(SLOTS - 1):
        block_ref[k + (k + 1) // (SMALL + 1)] = matrices_ref[k].astype(BF16)
    pack_ref[...] = jnp.zeros_like(pack_ref)
    pack_ref[IN_ROW : IN_ROW + variables, :] = in_ref[...]
    pack_ref[OUT_ROW : OUT_ROW + variables, :] = outp_ref[...]
    pack_ref[GAIN_ROW : GAIN_ROW + gains_ref.shape[0], :] = gains_ref[...]
    pack_ref[DATE_ROW : DATE_ROW + dates_ref.shape[0], :] = dates_ref[...]
    block_ref[SMALL] = jnp.transpose(pack_ref[...]).astype(BF16)
    for d in steps:
        send(block_ref.at[slot], full_ref.at[slot, z], z_send.at[d], z_recv.at[d], to_z[d])
    keep(block_ref, full_ref.at[:, z], local_sem)
    valid = jnp.sum(valid_ref[...].astype(F32), axis=1, keepdims=True)
    valid = jnp.sum(valid, axis=0, keepdims=True)
    count_ref[...] = jnp.broadcast_to(valid, count_ref.shape)
    for d in steps:
        send(count_ref, counts_ref.at[d], n_send.at[d], n_recv.at[d], to_z[d])

    def gather_inputs(m):
        x4 = dot_nt(pick_ref[...], x_ref[m]) * (1.0 / picks_ref.shape[0])
        top, rest = split_two(x4)
        x4_ref[m] = top
        xl_ref[m] = rest
        keep(x4_ref.at[m], x4_out.at[m], o_sem.at[0, m])

    pick_ref[...] = count_columns(columns_of(picks_ref[...]), points, picks_ref.shape[0])
    out_ref[...] = count_columns(columns_of(rows_ref[...]), nodes, 1)
    for d in steps:
        chunk = full_ref.at[slot, source[d]]
        arrived(chunk, z_recv.at[d])
        send(chunk, chunk, p_send.at[0, d], p_recv.at[0, d], to_side)
        send(chunk, chunk, p_send.at[1, d], p_recv.at[1, d], to_up)
        send(chunk, chunk, c_send.at[0, d], c_recv.at[0, d], to_core)
        if d <= members:
            gather_inputs(d - 1)
    for m in range(depth - 1, members):
        gather_inputs(m)

    total = count_ref[...]
    for d in steps:
        arrived(counts_ref.at[d], n_recv.at[d])
        total = total + counts_ref[d]
    sums_ref[0] = total
    send(sums_ref.at[0], heard_ref.at[0], s_send.at[0], s_recv.at[0], to_core)

    for d in steps:
        chunk = full_ref.at[side, source[d]]
        arrived(chunk, p_recv.at[0, d])
        part = full_ref.at[side, source[d], low]
        send(part, part, d_send.at[0, d], d_recv.at[0, d], to_up)
        send(chunk, chunk, c_send.at[1, d], c_recv.at[1, d], to_core)
        chunk = full_ref.at[up, source[d]]
        arrived(chunk, p_recv.at[1, d])
        part = full_ref.at[up, source[d], high]
        send(part, part, d_send.at[1, d], d_recv.at[1, d], to_side)
        send(chunk, chunk, c_send.at[2, d], c_recv.at[2, d], to_core)

    for step, place in ((1, to_side), (2, to_up)):
        arrived(heard_ref.at[step - 1], s_recv.at[step - 1])
        total = total + heard_ref[step - 1]
        sums_ref[step] = total
        send(sums_ref.at[step], heard_ref.at[step], s_send.at[step], s_recv.at[step], place)

    for d in steps:
        arrived(full_ref.at[far, source[d], low], d_recv.at[0, d])
        arrived(full_ref.at[far, source[d], high], d_recv.at[1, d])
        chunk = full_ref.at[far, source[d]]
        send(chunk, chunk, c_send.at[3, d], c_recv.at[3, d], to_core)
    arrived(heard_ref.at[2], s_recv.at[2])
    total_ref[...] = total + heard_ref[2]
    for k in range(4):
        for d in steps:
            arrived(full_ref.at[core, source[d]], c_recv.at[k, d])
    local[0].wait()

    loads = []
    for k, j in enumerate((SMALL, 0, 1)):
        copy = pltpu.make_async_copy(full_ref.at[j], w_ref.at[k], w_sem.at[k])
        copy.start()
        loads.append(copy)
    for copy in loads:
        copy.wait()
    small_ref[...] = jnp.transpose(w_ref[0].reshape(LATENT, LATENT))
    keep(small_ref, small_out_ref, q_sem)
    win = small_ref[IN_ROW : IN_ROW + variables, :]
    m0 = w_ref[1].reshape(LATENT, LATENT)
    m1 = w_ref[2].reshape(LATENT, LATENT)
    for m in range(members):
        agg = dot(x4_ref[m], win) + dot(xl_ref[m], win) + date_row(small_ref, day_ref[m])
        a0 = agg.astype(BF16)
        hid, t1 = silu_parts(0.5 * dot(a0, m0))
        h1 = hid.astype(BF16)
        unit, scale = normalise(dot(h1, m1))
        mesh = agg + unit * gain_row(small_ref, 0)
        low_mesh = mesh.astype(BF16)
        a0_ref[m] = a0
        h1_ref[m] = h1
        t1_ref[m] = t1.astype(BF16)
        unit_ref[m] = unit
        scale_ref[m] = scale
        mesh_ref[m] = mesh
        sent_ref[m] = low_mesh
        buf_ref[m] = dot(out_ref[...], low_mesh).astype(BF16)
        send(buf_ref.at[m, halo:], left_ref.at[m], e_send.at[0, m], e_recv.at[0, m], to_next)
        send(buf_ref.at[m, :halo], right_ref.at[m], e_send.at[1, m], e_recv.at[1, m], to_previous)
        for k, (ref, target) in enumerate(
            (
                (a0_ref, a0_out), (h1_ref, h1_out), (t1_ref, t1_out), (unit_ref, unit_out),
                (scale_ref, scale_out), (mesh_ref, mesh_out), (sent_ref, sent_out),
            )
        ):
            keep(ref.at[m], target.at[m], o_sem.at[k + 1, m])
    for m in range(members):
        arrived(left_ref.at[m], e_recv.at[0, m])
        arrived(right_ref.at[m], e_recv.at[1, m])
    for copy in sent:
        copy.wait_send()
    for copy in local[1:]:
        copy.wait()


def encode(day, matrices, in_proj, out_proj, gains, dates, valid, inputs, picks, rows, depth):
    hbm = pl.BlockSpec(memory_space=pl.ANY)
    vmem = pl.BlockSpec(memory_space=pltpu.VMEM)
    dma = pltpu.SemaphoreType.DMA
    members, variables, points = inputs.shape
    nodes = picks.shape[1]
    halo = rows.shape[1] // 2
    share = matrices.shape[1]
    nodes_of = (members, nodes, LATENT)
    kept = [
        ((members, nodes, variables), BF16),
        (nodes_of, BF16),
        (nodes_of, BF16),
        (nodes_of, BF16),
        (nodes_of, F32),
        ((members, nodes, 1), F32),
        (nodes_of, F32),
        (nodes_of, BF16),
    ]
    return pl.pallas_call(
        partial(encode_kernel, depth),
        in_specs=[pl.BlockSpec(memory_space=pltpu.SMEM)] + [vmem] * 9,
        out_shape=[
            shape_of((SLOTS, depth, share, LATENT), BF16),
            shape_of((LATENT, LATENT), BF16),
            shape_of((8, 128), F32),
            *(shape_of(*one) for one in kept),
            shape_of((members, halo, LATENT), BF16),
            shape_of((members, halo, LATENT), BF16),
        ],
        out_specs=[hbm, hbm, vmem] + [hbm] * (len(kept) + 2),
        scratch_shapes=[
            pltpu.VMEM((SLOTS, share, LATENT), BF16),
            pltpu.VMEM((LATENT, share), F32),
            pltpu.VMEM((nodes, points), BF16),
            pltpu.VMEM((2 * halo, nodes), BF16),
            pltpu.VMEM(*kept[0]),
            *(pltpu.VMEM(*one) for one in kept),
            pltpu.VMEM((members, 2 * halo, LATENT), BF16),
            pltpu.VMEM((3, depth, share, LATENT), BF16),
            pltpu.VMEM((LATENT, LATENT), BF16),
            pltpu.VMEM((8, 128), F32),
            pltpu.VMEM((depth, 8, 128), F32),
            pltpu.VMEM((3, 8, 128), F32),
            pltpu.VMEM((3, 8, 128), F32),
            dma,
            dma((depth,)),
            dma((depth,)),
            dma((2, depth)),
            dma((2, depth)),
            dma((2, depth)),
            dma((2, depth)),
            dma((4, depth)),
            dma((4, depth)),
            dma((depth,)),
            dma((depth,)),
            dma((3,)),
            dma((3,)),
            dma((3,)),
            dma((len(kept), members)),
            dma((2, members)),
            dma((2, members)),
            dma,
        ],
        compiler_params=pltpu.CompilerParams(
            collective_id=0, has_side_effects=True, vmem_limit_bytes=VMEM_BYTES
        ),
    )(day, matrices, in_proj, out_proj, gains, dates, valid, inputs, picks, rows)


def reduce_kernel(
    depth, day_ref, late_ref, momentum_ref, count_ref, dmesh_in, dhalo_ref, rows_ref, x4_in, a0_in,
    h1_in, t1_in, unit_in, scale_in, weights_ref, small_ref, gxd_ref, dsum_ref, gout_ref, ggain_ref,
    loss_ref,
    g_ref, x_ref,
    dmesh_ref, ret_ref, x4_ref, a0_ref, h1_ref, t1_ref, unit_ref, scale_ref, m_ref, back_ref, pack_ref,
    early_ref, own_ref, heard_ref, snd_ref, rcv_ref, snd_low_ref, rcv_low_ref, acc_ref, zr_ref,
    g_own_ref, mb_ref, x_own_ref,
    i_sem, e_send, e_recv, l_sem, h_send, h_recv, p_send, p_recv, q_send, q_recv, z_send, z_recv,
    m_send, m_recv, g_local, g_send, g_recv, x_local, x_send, x_recv,
):
    base, slot, core, side, up, far = neighbours()
    z = lax.axis_index("row")
    rows = acc_ref.shape[0] // depth
    chips = SLOTS // 2
    mine = slot // 2
    parity = lax.rem(slot, 2)
    members, variables = x4_ref.shape[0], x4_ref.shape[2]
    halo = dhalo_ref.shape[1] // 2
    to_core, to_side, to_up, to_far = ({"region": base + place} for place in (core, side, up, far))
    to_next, to_previous = around()
    to_place = (to_far, to_side, to_up)
    places = (far, side, up)
    to_z = [None] + [{"row": lax.rem(z + d, depth)} for d in range(1, depth)]
    greet(to_z[1:] + [to_core, to_side, to_up, to_far, to_next, to_previous])
    parts = [pl.ds(b * rows, rows) for b in range(depth)]
    sent = []

    def send(*args):
        copy = remote(*args)
        copy.start()
        sent.append(copy)

    def arrived(target, receive):
        remote(target, target, receive, receive, to_core).wait_recv()

    def load(*args):
        copy = pltpu.make_async_copy(*args)
        copy.start()
        return copy

    for m in range(members):
        send(dhalo_ref.at[m, halo:], ret_ref.at[m, :halo], e_send.at[0, m], e_recv.at[0, m], to_next)
        send(dhalo_ref.at[m, :halo], ret_ref.at[m, halo:], e_send.at[1, m], e_recv.at[1, m], to_previous)
    inner = ((dmesh_in, dmesh_ref), (x4_in, x4_ref), (a0_in, a0_ref), (h1_in, h1_ref), (t1_in, t1_ref),
             (unit_in, unit_ref), (scale_in, scale_ref))
    ready = [
        [load(ref.at[m], target.at[m], i_sem.at[k, m]) for k, (ref, target) in enumerate(inner)]
        for m in range(members)
    ]
    first = load(late_ref.at[0], early_ref.at[2], i_sem.at[len(inner), 0])
    ready[0].append(load(weights_ref.at[0:2], m_ref, i_sem.at[len(inner), 1]))

    loads = {}

    def share(chip):
        for b, part in enumerate(parts):
            if chip < 2:
                ref = early_ref.at[2 * chip + 1 - parity, part]
            else:
                ref = late_ref.at[2 * chip - SMALL + 1 - parity, part]
            send(ref, heard_ref.at[chip, part], h_send.at[chip, b], h_recv.at[chip, b], to_core)
            if chip >= 2:
                loads[chip, b] = load(
                    late_ref.at[2 * chip - SMALL + parity, part], own_ref.at[chip - 2, part],
                    l_sem.at[chip - 2, b],
                )

    def low_copy(b):
        return remote(
            snd_low_ref.at[parts[b]], rcv_low_ref.at[mine, parts[b]], q_send.at[b], q_recv.at[mine, b],
            {"region": base + SMALL},
        )

    def chip_copy(chip, b):
        return remote(
            snd_ref.at[chip, parts[b]], rcv_ref.at[mine, parts[b]], p_send.at[chip, b],
            p_recv.at[mine, b], {"region": base + 2 * chip + parity},
        )

    def pass_on(chip, b):
        part = parts[b]
        arrived(heard_ref.at[chip, part], h_recv.at[chip, b])
        if chip < 2:
            total = early_ref[2 * chip + parity, part, :]
        else:
            loads[chip, b].wait()
            total = own_ref[chip - 2, part, :]
        total = total + heard_ref[chip, part, :]

        @pl.when(mine == chip)
        def _():
            acc_ref[part, :] = total

        @pl.when(mine != chip)
        def _():
            snd_ref[chip, part, :] = total.astype(BF16)
            chip_copy(chip, b).start()

        if chip == SMALL // 2:

            @pl.when((mine != chip) & (parity == SMALL % 2))
            def _():
                snd_low_ref[part, :] = (total - total.astype(BF16).astype(F32)).astype(BF16)
                low_copy(b).start()

    share(3)
    share(2)

    lines = lax.broadcasted_iota(jnp.int32, (16, LATENT), 0)
    back_ref[...] = count_rows(rows_ref[...], back_ref.shape[0])
    wout = small_ref[OUT_ROW : OUT_ROW + variables, :]
    pack_ref[...] = jnp.zeros_like(pack_ref)
    top, rest = split_two(gxd_ref[...])
    pack_ref[IN_ROW : IN_ROW + variables, :] = dot(top, wout) + dot(rest, wout)
    pack_ref[OUT_ROW : OUT_ROW + variables, :] = gout_ref[...]
    pack_ref[GAIN_ROW + 1 : GAIN_ROW + 3, :] = ggain_ref[...]
    loss = jnp.sum(loss_ref[...], axis=0, keepdims=True)
    pack_ref[LOSS_ROW : LOSS_ROW + 1, :] = jnp.broadcast_to(loss, (1, LATENT))
    early_ref[0:2] = jnp.zeros((2, LATENT, LATENT), F32)
    late = [(chip, b) for chip in (3, 2) for b in range(depth)]
    for m in range(members):
        for copy in ready[m]:
            copy.wait()
        arrived(ret_ref.at[m, :halo], e_recv.at[0, m])
        arrived(ret_ref.at[m, halo:], e_recv.at[1, m])
        dmesh = dmesh_ref[m] + dot(back_ref[...], ret_ref[m])
        unit = unit_ref[m]
        pack_ref[GAIN_ROW : GAIN_ROW + 1, :] += jnp.sum(dmesh * unit, axis=0, keepdims=True)
        dc = norm_back(dmesh, gain_row(small_ref, 0), unit, scale_ref[m]).astype(BF16)
        early_ref[1] += dot_tn(h1_ref[m], dc)
        du = (dot_nt(dc, m_ref[1]) * t1_ref[m].astype(F32)).astype(BF16)
        early_ref[0] += dot_tn(a0_ref[m], du)
        dagg = dmesh + dot_nt(du, m_ref[0])
        pack_ref[IN_ROW : IN_ROW + variables, :] += dot_tn(x4_ref[m], dagg.astype(BF16))
        top, rest = split_two(dsum_ref[m])
        date = jnp.sum(dagg, axis=0, keepdims=True) + dot_tn(top, wout) + dot_tn(rest, wout)
        pack_ref[DATE_ROW : DATE_ROW + 16, :] += jnp.where(lines == day_ref[m], date, 0.0)
        for chip, b in late[m * len(late) // members : (m + 1) * len(late) // members]:
            pass_on(chip, b)
    early_ref[SMALL] = jnp.transpose(pack_ref[...])
    first.wait()
    share(0)
    share(1)
    for b in range(depth):
        for chip in range(2):
            pass_on(chip, b)

    sources = [lax.rem(mine + i, chips) for i in range(1, chips)]
    for b, part in enumerate(parts):
        total = acc_ref[part, :]
        for c in sources:
            arrived(rcv_ref.at[c, part], p_recv.at[c, b])
            total = total + rcv_ref[c, part, :].astype(F32)
        acc_ref[part, :] = total

        @pl.when(slot == SMALL)
        def _():
            low = acc_ref[part, :]
            for c in sources:
                arrived(rcv_low_ref.at[c, part], q_recv.at[c, b])
                low = low + rcv_low_ref[c, part, :].astype(F32)
            acc_ref[part, :] = low

        @pl.when(z != b)
        def _():
            d = lax.rem(b - z + depth, depth)
            remote(
                acc_ref.at[part], zr_ref.at[d], z_send.at[b], z_recv.at[d], {"row": b + 0 * z}
            ).start()

    zr_ref[0] = acc_ref[pl.ds(pl.multiple_of(z * rows, rows), rows), :]
    for d in range(1, depth):
        arrived(zr_ref.at[d], z_recv.at[d])
    g_own = zr_ref[z]
    for place in range(1, depth):
        g_own = g_own + zr_ref[lax.rem(z + depth - place, depth)]
    g_own_ref[...] = g_own
    momentum = (
        MUON_MOMENTUM * momentum_ref[slot - (slot + SMALL + 1) // SLOTS]
        + (2.0 / count_ref[0:1, 0:1]) * g_own
    )
    mb_ref[0] = momentum.astype(BF16)
    for d in range(1, depth):
        send(mb_ref.at[0], mb_ref.at[d], m_send.at[d], m_recv.at[d], to_z[d])
    g_copy = load(g_own_ref, g_ref.at[slot], g_local)
    for k in range(3):
        send(g_own_ref, g_ref.at[slot], g_send.at[k], g_recv.at[k], to_place[k])
    send(g_own_ref, g_ref.at[slot], g_send.at[3], g_recv.at[3], to_core)

    for d in range(1, depth):
        arrived(mb_ref.at[d], m_recv.at[d])
    everything = jnp.concatenate([mb_ref[d] for d in range(depth)], axis=0)
    wide = everything.astype(F32)
    squares = jnp.sum(jnp.sum(wide * wide, axis=1, keepdims=True), axis=0, keepdims=True)
    inverse = lax.rsqrt(squares + 1e-07)
    turn = momentum * inverse
    current = (wide * inverse).astype(BF16)
    turn_low = turn.astype(BF16)
    for sweep in range(NS_ITERS):
        gram = dot_tn(current, current)
        gram_low = gram.astype(BF16)
        mixing = NS_COEFFS[1] * gram + NS_COEFFS[2] * dot(gram_low, gram_low)
        mixing = mixing.astype(BF16)
        turn = NS_COEFFS[0] * turn + dot(turn_low, mixing)
        turn_low = turn.astype(BF16)
        if sweep < NS_ITERS - 1:
            current = (NS_COEFFS[0] * current.astype(F32) + dot(current, mixing)).astype(BF16)
    x_own_ref[...] = turn_low
    x_copy = pltpu.make_async_copy(x_own_ref, x_ref.at[slot], x_local)
    x_copy.start()
    for k in range(3):
        send(x_own_ref, x_ref.at[slot], x_send.at[k], x_recv.at[k], to_place[k])
    send(x_own_ref, x_ref.at[slot], x_send.at[3], x_recv.at[3], to_core)

    for target, send_sem, recv_sem in ((g_ref, g_send, g_recv), (x_ref, x_send, x_recv)):
        for k in range(3):
            chunk = target.at[places[k]]
            arrived(chunk, recv_sem.at[k])
            send(chunk, chunk, send_sem.at[4 + k], recv_sem.at[4 + k], to_core)
    for target, recv_sem in ((g_ref, g_recv), (x_ref, x_recv)):
        for k in range(3, 7):
            arrived(target.at[core], recv_sem.at[k])
    for copy in sent:
        copy.wait_send()
    for b in range(depth):
        for chip in range(chips):

            @pl.when(mine != chip)
            def _():
                chip_copy(chip, b).wait_send()

        @pl.when((mine != SMALL // 2) & (parity == SMALL % 2))
        def _():
            low_copy(b).wait_send()

        @pl.when(z != b)
        def _():
            remote(
                acc_ref.at[parts[b]], acc_ref.at[parts[b]], z_send.at[b], z_send.at[b], to_core
            ).wait_send()

    g_copy.wait()
    x_copy.wait()


def reduce_gradients(
    day, late, momentum, count, dmesh, dhalo, rows, kept, weights, small, gxd, dsum, gout, ggain, loss,
    depth,
):
    hbm = pl.BlockSpec(memory_space=pl.ANY)
    vmem = pl.BlockSpec(memory_space=pltpu.VMEM)
    dma = pltpu.SemaphoreType.DMA
    members, nodes, width = dmesh.shape
    height = LATENT
    share = height // depth
    halo = dhalo.shape[1]
    chips = SLOTS // 2

    return pl.pallas_call(
        partial(reduce_kernel, depth),
        in_specs=[pl.BlockSpec(memory_space=pltpu.SMEM), hbm, vmem, vmem, hbm, vmem, vmem]
        + [hbm] * len(kept)
        + [hbm]
        + [vmem] * 6,
        out_shape=[
            shape_of((SLOTS, share, width), F32),
            shape_of((SLOTS, share, width), BF16),
        ],
        out_specs=[hbm, hbm],
        scratch_shapes=[
            pltpu.VMEM(dmesh.shape, F32),
            pltpu.VMEM(dhalo.shape, BF16),
            *(pltpu.VMEM(one.shape, one.dtype) for one in kept),
            pltpu.VMEM((2, height, width), BF16),
            pltpu.VMEM((nodes, halo), BF16),
            pltpu.VMEM((height, width), F32),
            pltpu.VMEM((4, height, width), F32),
            pltpu.VMEM((2, height, width), F32),
            pltpu.VMEM((chips, height, width), F32),
            pltpu.VMEM((chips, height, width), BF16),
            pltpu.VMEM((chips, height, width), BF16),
            pltpu.VMEM((height, width), BF16),
            pltpu.VMEM((chips, height, width), BF16),
            pltpu.VMEM((height, width), F32),
            pltpu.VMEM((depth, share, width), F32),
            pltpu.VMEM((share, width), F32),
            pltpu.VMEM((depth, share, width), BF16),
            pltpu.VMEM((share, width), BF16),
            dma((len(kept) + 2, members)),
            dma((2, members)),
            dma((2, members)),
            dma((2, depth)),
            dma((chips, depth)),
            dma((chips, depth)),
            dma((chips, depth)),
            dma((chips, depth)),
            dma((depth,)),
            dma((chips, depth)),
            dma((depth,)),
            dma((depth,)),
            dma((depth,)),
            dma((depth,)),
            dma,
            dma((7,)),
            dma((7,)),
            dma,
            dma((7,)),
            dma((7,)),
        ],
        compiler_params=pltpu.CompilerParams(
            collective_id=1, has_side_effects=True, vmem_limit_bytes=VMEM_BYTES
        ),
    )(
        day, late, momentum, count, dmesh, dhalo, rows, *kept, weights, small, gxd, dsum, gout,
        ggain, loss,
    )


def turn_whole(sums, count, momentum):
    blocks = jnp.concatenate([sums[:SMALL], sums[SMALL + 1 :]], axis=0)
    blocks = MUON_MOMENTUM * momentum + (2.0 / count[0, 0]) * blocks
    squares = lax.psum(jnp.sum(blocks * blocks, axis=(1, 2)), "row")
    current = blocks * lax.rsqrt(squares + 1e-07)[:, None, None]

    def product(expression, left, right):
        return jnp.einsum(expression, left, right, precision=lax.Precision.HIGHEST)

    for _ in range(NS_ITERS):
        gram = lax.psum(product("mrk,mrl->mkl", current, current), "row")
        mixing = NS_COEFFS[1] * gram + NS_COEFFS[2] * product("mkj,mjl->mkl", gram, gram)
        current = NS_COEFFS[0] * current + product("mrk,mkl->mrl", current, mixing)
    current = current.astype(BF16)
    return jnp.concatenate([current[:SMALL], current[SMALL - 1 :]], axis=0)


def finish_kernel(
    g_ref, rest_ref, x_ref, count_ref, matrix_ref, momentum_ref,
    in_ref, in1_ref, in2_ref, out_ref, out1_ref, out2_ref, gain_ref, gain1_ref, gain2_ref,
    date_ref, date1_ref, date2_ref,
    new_matrix_ref, new_momentum_ref,
    nin_ref, nin1_ref, nin2_ref, nout_ref, nout1_ref, nout2_ref, ngain_ref, ngain1_ref, ngain2_ref,
    ndate_ref, ndate1_ref, ndate2_ref, loss_ref,
):
    scale = 2.0 / count_ref[0:1, 0:1]
    new_momentum_ref[...] = MUON_MOMENTUM * momentum_ref[...] + scale * g_ref[...]
    new_matrix_ref[...] = (
        matrix_ref[...] * (1.0 - MUON_RATE * WEIGHT_DECAY) - MUON_RATE * x_ref[...].astype(F32)
    )

    @pl.when(pl.program_id(0) == 0)
    def _():
        rest = jnp.transpose(rest_ref[0])
        loss_ref[...] = rest[LOSS_ROW : LOSS_ROW + 8, :]
        rest = rest * scale
        for row, rate, decay, old, new in (
            (IN_ROW, MATRIX_RATE, WEIGHT_DECAY, (in_ref, in1_ref, in2_ref), (nin_ref, nin1_ref, nin2_ref)),
            (OUT_ROW, MATRIX_RATE, WEIGHT_DECAY, (out_ref, out1_ref, out2_ref),
             (nout_ref, nout1_ref, nout2_ref)),
            (GAIN_ROW, VECTOR_RATE, 0.0, (gain_ref, gain1_ref, gain2_ref),
             (ngain_ref, ngain1_ref, ngain2_ref)),
            (DATE_ROW, VECTOR_RATE, 0.0, (date_ref, date1_ref, date2_ref),
             (ndate_ref, ndate1_ref, ndate2_ref)),
        ):
            weight, first, second = (ref[...] for ref in old)
            gradient = rest[row : row + weight.shape[0], :]
            for ref, value in zip(new, adam_update(weight, gradient, first, second, rate, decay)):
                ref[...] = value


def finish(sums, turned, count, matrices, momentum, vectors):
    share, width = sums.shape[1:]

    def slot_block():
        return pl.BlockSpec((1, share, width), lambda m: (m + (m + 1) // (SMALL + 1), 0, 0))

    one = pl.BlockSpec((1, share, width), lambda m: (m, 0, 0))
    return pl.pallas_call(
        finish_kernel,
        grid=(matrices.shape[0],),
        in_specs=[
            slot_block(), pl.BlockSpec((1, share, width), lambda m: (SMALL, 0, 0)), slot_block(),
            whole(count.shape), one, one, *(whole(v.shape) for v in vectors),
        ],
        out_shape=[shape_of(matrices.shape, F32)] * 2
        + [shape_of(v.shape, F32) for v in vectors]
        + [shape_of((8, share), F32)],
        out_specs=[one, one] + [whole(v.shape) for v in vectors] + [whole((8, share))],
        compiler_params=pltpu.CompilerParams(
            dimension_semantics=("arbitrary",), vmem_limit_bytes=VMEM_BYTES
        ),
    )(sums, sums, turned, count, matrices, momentum, *vectors)


def adam_update(weight, gradient, first_moment, second_moment, step_rate, decay_rate):
    first_new = BETA_ONE * first_moment + (1.0 - BETA_ONE) * gradient
    second_new = BETA_TWO * second_moment + (1.0 - BETA_TWO) * gradient * gradient
    unbiased_one = first_new / (1.0 - BETA_ONE**STEP)
    unbiased_two = second_new / (1.0 - BETA_TWO**STEP)
    weight_new = weight * (1.0 - step_rate * decay_rate) - step_rate * unbiased_one / (
        jnp.sqrt(unbiased_two) + 1e-08
    )
    return (weight_new, first_new, second_new)


def body(
    inputs,
    targets,
    valid_steps,
    var_weights,
    grid_to_mesh,
    mesh_edges,
    send_rows,
    mesh_to_grid,
    date_index,
    matrices,
    matrices_momentum,
    in_proj,
    in_first,
    in_second,
    out_proj,
    out_first,
    out_second,
    norm_gains,
    gains_first,
    gains_second,
    date_table,
    date_first,
    date_second,
):
    inputs = jnp.swapaxes(inputs, 1, 2)
    targets = jnp.swapaxes(targets, 1, 2)
    members, variables, points = inputs.shape
    nodes = grid_to_mesh.shape[0]
    halo = send_rows.shape[0] // 2
    table = nodes + 2 * halo
    k_edge = mesh_edges.shape[1]
    k_pick = mesh_to_grid.shape[1]
    dates = date_table.shape[0]

    depth = lax.axis_size("row")
    regions = lax.axis_size("region")
    groups = [[g * SLOTS + q for g in range(regions // SLOTS)] for q in range(SLOTS)]
    scalars = pl.BlockSpec(memory_space=pltpu.SMEM)
    hbm = pl.BlockSpec(memory_space=pl.ANY)
    gathered, small, count, *kept, left, right = encode(
        date_index, matrices, in_proj, out_proj.T, norm_gains, date_table, valid_steps, inputs,
        grid_to_mesh.T, send_rows[None, :], depth,
    )
    mesh1, sent = kept[6:]
    if regions > SLOTS:
        count = lax.psum(count, "region", axis_index_groups=groups)
    weights = gathered.reshape(SLOTS, LATENT, LATENT)
    node_block = per_member((nodes, LATENT))

    def matrix(j):
        place = j + (j + 1) // (SMALL + 1)
        return pl.BlockSpec(
            (1, LATENT, LATENT), lambda m: (place, 0, 0), pipeline_mode=pl.Buffered(1)
        )

    out_shape = (variables, LATENT)
    late, gout, gxd, dsum, ggain_late, loss_row, dmesh, dhalo = call(
        main_kernel,
        members,
        [
            scalars,
            node_block,
            node_block,
            per_member((halo, LATENT)),
            per_member((halo, LATENT)),
            per_member((variables, points)),
            per_member((variables, points)),
            whole((members, points)),
            whole((variables, 1)),
            whole((k_edge, nodes)),
            whole((k_pick, points)),
            whole((LATENT, LATENT)),
            matrix(2),
            matrix(3),
            matrix(4),
            matrix(5),
            matrix(6),
        ],
        [
            shape_of((5, LATENT, LATENT), F32),
            shape_of(out_shape, F32),
            shape_of((variables, variables), F32),
            shape_of((members, variables, 1), F32),
            shape_of((2, LATENT), F32),
            shape_of((variables, 1), F32),
            shape_of((members, nodes, LATENT), F32),
            shape_of((members, 2 * halo, LATENT), BF16),
        ],
        [
            hbm,
            whole(out_shape),
            whole((variables, variables)),
            per_member((variables, 1)),
            whole((2, LATENT)),
            whole((variables, 1)),
            node_block,
            per_member((2 * halo, LATENT)),
        ],
        main_scratch(k_edge, nodes, points, table),
        60_000_000_000,
    )(
        date_index,
        mesh1,
        sent,
        left,
        right,
        inputs,
        targets,
        valid_steps,
        var_weights[:, None],
        mesh_edges.T,
        mesh_to_grid.T,
        small,
        weights,
        weights,
        weights,
        weights,
        weights,
    )

    sums, turned = reduce_gradients(
        date_index, late, matrices_momentum, count, dmesh, dhalo, send_rows[None, :], kept[:6], weights,
        small, gxd, dsum, gout, ggain_late, loss_row, depth,
    )
    if regions > SLOTS:
        sums = lax.psum(sums, "region", axis_index_groups=groups)
        turned = turn_whole(sums, count, matrices_momentum)
    vectors = (
        in_proj, in_first, in_second, out_proj.T, out_first.T, out_second.T,
        norm_gains, gains_first, gains_second, date_table, date_first, date_second,
    )
    new = finish(sums, turned, count, matrices, matrices_momentum, vectors)
    return (
        *new[:5],
        *(part.T for part in new[5:8]),
        *new[8:14],
        new[14][0, 0],
        count[0, 0],
    )


def solution(mesh):
    in_specs = (
        P("row", "region", None),
        P("row", "region", None),
        P("row", "region"),
        P(),
        P("region", None),
        P("region", None),
        P("region"),
        P("region", None),
        P("row"),
        P(None, "row", None),
        P(None, "row", None),
        P(None, "row"),
        P(None, "row"),
        P(None, "row"),
        P("row", None),
        P("row", None),
        P("row", None),
        P(None, "row"),
        P(None, "row"),
        P(None, "row"),
        P(None, "row"),
        P(None, "row"),
        P(None, "row"),
    )
    out_specs = (
        P(None, "row", None),
        P(None, "row", None),
        P(None, "row"),
        P(None, "row"),
        P(None, "row"),
        P("row", None),
        P("row", None),
        P("row", None),
        P(None, "row"),
        P(None, "row"),
        P(None, "row"),
        P(None, "row"),
        P(None, "row"),
        P(None, "row"),
        P(),
        P(),
    )
    return jax.shard_map(body, mesh=mesh, in_specs=in_specs, out_specs=out_specs, check_vma=False)
```

```python
from functools import partial

import jax
import jax.numpy as jnp
from jax import lax
from jax.experimental import pallas as pl
from jax.experimental.pallas import tpu as pltpu
from jax.sharding import PartitionSpec as P

NS_ITERS = 2
STEP = 10
NS_COEFFS = (3.4445, -4.775, 2.0315)
MUON_RATE = 0.8
MUON_MOMENTUM = 0.95
MATRIX_RATE = 0.05
VECTOR_RATE = 0.2
BETA_ONE = 0.9
BETA_TWO = 0.95
WEIGHT_DECAY = 0.01

F32 = jnp.float32
BF16 = jnp.bfloat16
LATENT = 512
BLOCK = 1024
PARTS = 1
T_TYPE = BF16
VMEM_BYTES = 60 * 1024 * 1024
MESH = pl.DeviceIdType.MESH
SLOTS = 8
SMALL = 6
IN_ROW, OUT_ROW, GAIN_ROW, DATE_ROW, LOSS_ROW = 0, 240, 480, 496, 504


def dot(left, right):
    return jnp.dot(left, right, preferred_element_type=F32)


def dot_nt(left, right):
    return lax.dot_general(left, right, (((1,), (1,)), ((), ())), preferred_element_type=F32)


def dot_tn(left, right):
    return lax.dot_general(left, right, (((0,), (0,)), ((), ())), preferred_element_type=F32)


def split_two(values):
    high = values.astype(BF16)
    return high, (values - high.astype(F32)).astype(BF16)


def silu_parts(half):
    bend = jnp.tanh(half)
    gate = 0.5 * bend + 0.5
    hid = half * bend + half
    return hid, gate + hid * (1.0 - gate)


def normalise(values):
    centred = values - jnp.mean(values, axis=-1, keepdims=True)
    spread = jnp.mean(centred * centred, axis=-1, keepdims=True)
    scale = lax.rsqrt(spread + 1e-05)
    return centred * scale, scale


def norm_back(grad, gain, unit, scale):
    scaled = gain * grad
    mean_one = jnp.mean(scaled, axis=-1, keepdims=True)
    mean_two = jnp.mean(scaled * unit, axis=-1, keepdims=True)
    return scale * (scaled - mean_one - unit * mean_two)


def in_turn(parts):
    parts = list(parts)
    while parts:
        parts = [part for part in parts if next(part, None) is not None]


def count_columns(index, width, count):
    lanes = lax.broadcasted_iota(jnp.int32, (index.shape[0], width), 1)
    total = None
    for k in range(count):
        one = jnp.where(lanes == index[:, k : k + 1], 1.0, 0.0)
        total = one if total is None else total + one
    return total.astype(BF16)


def gain_row(small_ref, k):
    return small_ref[GAIN_ROW : GAIN_ROW + 16, :].astype(F32)[k : k + 1, :]


def date_row(small_ref, day):
    table = small_ref[DATE_ROW : DATE_ROW + 16, :].astype(F32)
    lines = lax.broadcasted_iota(jnp.int32, table.shape, 0)
    return jnp.sum(jnp.where(lines == day, table, 0.0), axis=0, keepdims=True)


def columns_of(index):
    short = 8 - index.shape[0]
    if short > 0:
        index = jnp.concatenate([index, jnp.zeros((short, index.shape[1]), index.dtype)], axis=0)
    return jnp.transpose(index)


def count_rows(index, height):
    lines = lax.broadcasted_iota(jnp.int32, (height, index.shape[1]), 0)
    total = None
    for k in range(index.shape[0]):
        one = jnp.where(lines == index[k : k + 1, :], 1.0, 0.0)
        total = one if total is None else total + one
    return total.astype(BF16)


def main_kernel(
    k_pick, day_ref, mesh_ref, sent_ref, left_ref, right_ref, x_ref, y_ref, valid_ref, varw_ref,
    eh_in, eht_in, d_in, dt_in, small_ref, m2_ref, m3_ref, m4_ref, m5_ref, m6_ref,
    slots_ref, gout_ref, gxd_ref, dsum_ref, ggain_ref, loss_ref, dmesh_ref, dhalo_ref,
    gm_ref, out_sem, in_sem, eh_ref, eht_ref, d_ref, dt_ref, ext_ref, t_ref, mm_ref, acc_ref, sender_ref,
):
    nodes = mesh_ref.shape[1]
    table = ext_ref.shape[0]
    variables, points = x_ref.shape[1:]
    k_edge = eh_ref.shape[0] // nodes
    counts = [
        pltpu.make_async_copy(source, target, in_sem.at[k])
        for k, (source, target) in enumerate(
            ((eh_in, eh_ref), (d_in, d_ref), (dt_in, dt_ref), (eht_in, eht_ref))
        )
    ]

    def counts_ready(*which):
        @pl.when(pl.program_id(0) == 0)
        def _():
            for k in which:
                counts[k].wait()

    halo = left_ref.shape[1]

    @pl.when(pl.program_id(0) == 0)
    def _():
        for copy in counts:
            copy.start()
        gm_ref[...] = jnp.zeros_like(gm_ref)
        gout_ref[...] = jnp.zeros_like(gout_ref)
        gxd_ref[...] = jnp.zeros_like(gxd_ref)
        ggain_ref[...] = jnp.zeros_like(ggain_ref)
        loss_ref[...] = jnp.zeros_like(loss_ref)

    sent = sent_ref[0]
    ext_ref[:nodes, :] = sent
    ext_ref[nodes : nodes + halo, :] = left_ref[0]
    ext_ref[nodes + halo :, :] = right_ref[0]
    receivers = 0.5 * dot(sent, m3_ref[0])
    sender_ref[...] = (0.5 * dot(ext_ref[...], m2_ref[0])).astype(BF16)

    counts_ready(0)

    def edge(k, carry):
        hid_sum, t_sum = carry
        rows = pl.ds(pl.multiple_of(k * nodes, nodes), nodes)
        hid, t = silu_parts(1.0 * dot(eh_ref[rows, :], sender_ref[...]) + receivers)
        t_ref[rows, :] = t.astype(t_ref.dtype)
        return hid_sum + hid.astype(BF16).astype(F32), t_sum + t

    zero = jnp.zeros((nodes, LATENT), F32)
    hid_sum, t_sum = lax.fori_loop(0, k_edge, edge, (zero, zero), unroll=k_edge)
    h_high = (hid_sum * (1.0 / k_edge)).astype(BF16)
    gain2 = gain_row(small_ref, 1)
    unit2, scale2 = normalise(dot(h_high, m4_ref[0]))
    mesh2 = mesh_ref[0] + unit2 * gain2
    mm_ref[...] = mesh2.astype(BF16)

    counts_ready(1, 2)
    acc_ref[...] = jnp.zeros_like(acc_ref)
    dsum_ref[...] = jnp.zeros_like(dsum_ref)
    member = pl.program_id(0)
    date = date_row(small_ref, day_ref[member])
    gain3 = gain_row(small_ref, 2)
    wout = small_ref[OUT_ROW : OUT_ROW + variables, :]
    square = (variables, variables)
    same = lax.broadcasted_iota(jnp.int32, square, 0) == lax.broadcasted_iota(jnp.int32, square, 1)
    varw = jnp.sum(jnp.where(same, varw_ref[...], 0.0), axis=1, keepdims=True)

    def decode_part(rows):
        dec = dot(d_ref[rows, :], mm_ref[...])
        a2 = (dec * (1.0 / k_pick)).astype(BF16)
        yield True
        hid, t = silu_parts(0.5 * dot(a2, m5_ref[0]))
        h2 = hid.astype(BF16)
        yield True
        unit, scale = normalise(dot(h2, m6_ref[0]))
        yield True
        x = x_ref[0, :, rows]
        grid = dot_tn(x, small_ref[IN_ROW : IN_ROW + variables, :]) + date + unit * gain3
        grid = grid.astype(BF16)
        yield True
        misfit = x.astype(F32) + dot_nt(wout, grid) - y_ref[0, :, rows].astype(F32)
        valid = valid_ref[pl.ds(member, 1), rows].astype(F32)
        weighted = valid * varw * misfit
        loss_ref[...] += jnp.sum(weighted * misfit, axis=1, keepdims=True)
        dsum_ref[0] += jnp.sum(weighted, axis=1, keepdims=True)
        dp = weighted.astype(BF16)
        gout_ref[...] += dot(dp, grid)
        gxd_ref[...] += dot_nt(x, dp)
        yield True
        dgrid = dot_tn(dp, wout)
        ggain_ref[1:2, :] += jnp.sum(dgrid * unit, axis=0, keepdims=True)
        dc = norm_back(dgrid, gain3, unit, scale).astype(BF16)
        gm_ref[4] += dot_tn(h2, dc)
        yield True
        du = (dot_nt(dc, m6_ref[0]) * t).astype(BF16)
        gm_ref[3] += dot_tn(a2, du)
        yield True
        ddec = dot_nt(du, m5_ref[0]).astype(BF16)
        acc_ref[...] += dot(dt_ref[:, rows], ddec)
        yield True

    def grid_block(i, carry):
        part = BLOCK // PARTS
        in_turn(
            decode_part(pl.ds(pl.multiple_of(i * BLOCK + k * part, part), part)) for k in range(PARTS)
        )
        return carry

    lax.fori_loop(0, points // BLOCK, grid_block, 0)

    counts_ready(3)
    dmesh2 = acc_ref[...] * (1.0 / k_pick)
    ggain_ref[0:1, :] += jnp.sum(dmesh2 * unit2, axis=0, keepdims=True)
    dagg = norm_back(dmesh2, gain2, unit2, scale2).astype(BF16)
    gm_ref[2] += dot_tn(h_high, dagg)
    dhid = dot_nt(dagg, m4_ref[0]) * (1.0 / k_edge)
    dr = (dhid * t_sum).astype(BF16)
    gm_ref[1] += dot_tn(sent, dr)

    def edge_back(k, total):
        rows = pl.ds(pl.multiple_of(k * nodes, nodes), nodes)
        dpre = (dhid * t_ref[rows, :].astype(F32)).astype(BF16)
        return total + dot(eht_ref[:, rows], dpre)

    ds = lax.fori_loop(
        0, k_edge, edge_back, jnp.zeros((table, LATENT), F32), unroll=k_edge
    ).astype(BF16)
    gm_ref[0] += dot_tn(ext_ref[...], ds)
    dext = dot_nt(ds, m2_ref[0])
    dmesh_ref[0] = dmesh2 + dext[:nodes, :] + dot_nt(dr, m3_ref[0])
    dhalo_ref[0] = dext[nodes:, :].astype(BF16)

    @pl.when(member == pl.num_programs(0) - 1)
    def _():
        copy = pltpu.make_async_copy(gm_ref, slots_ref, out_sem)
        copy.start()
        copy.wait()


def main_scratch(k_edge, nodes, points, table):
    return [
        pltpu.VMEM((5, LATENT, LATENT), F32),
        pltpu.SemaphoreType.DMA,
        pltpu.SemaphoreType.DMA((4,)),
        pltpu.VMEM((k_edge * nodes, table), BF16),
        pltpu.VMEM((table, k_edge * nodes), BF16),
        pltpu.VMEM((points, nodes), BF16),
        pltpu.VMEM((nodes, points), BF16),
        pltpu.VMEM((table, LATENT), BF16),
        pltpu.VMEM((k_edge * nodes, LATENT), T_TYPE),
        pltpu.VMEM((nodes, LATENT), BF16),
        pltpu.VMEM((nodes, LATENT), F32),
        pltpu.VMEM((table, LATENT), BF16),
    ]


def whole(shape):
    return pl.BlockSpec(shape, lambda m: (0,) * len(shape))


def per_member(shape):
    return pl.BlockSpec((1,) + shape, lambda m: (m, 0, 0))


def call(kernel, members, in_specs, out_shapes, out_specs, scratch, cost, aliases=None):
    return pl.pallas_call(
        kernel,
        grid=(members,),
        in_specs=in_specs,
        out_shape=out_shapes,
        out_specs=out_specs,
        scratch_shapes=scratch,
        input_output_aliases=aliases or {},
        compiler_params=pltpu.CompilerParams(
            dimension_semantics=("arbitrary",), vmem_limit_bytes=VMEM_BYTES
        ),
        cost_estimate=pl.CostEstimate(flops=cost, bytes_accessed=32 << 20, transcendentals=0),
    )


def shape_of(shape, dtype):
    return jax.ShapeDtypeStruct(shape, dtype)


def slot_of(matrix):
    return 2 * matrix - 5 * ((matrix + 1) // 4)


def neighbours():
    region = lax.axis_index("region")
    slot = lax.rem(region, SLOTS)
    base = region - slot
    one = lax.rem(slot, 2)
    two = lax.rem(slot // 2, 2)
    four = slot // 4
    core = slot + 1 - 2 * one
    side = slot + 2 - 4 * two
    up = slot + 4 - 8 * four
    far = side + 4 - 8 * four
    return base, slot, core, side, up, far


def remote(source, target, send, receive, where):
    return pltpu.make_async_remote_copy(
        src_ref=source, dst_ref=target, send_sem=send, recv_sem=receive,
        device_id=where, device_id_type=MESH,
    )


def greet(places):
    barrier = pltpu.get_barrier_semaphore()
    for place in places:
        pl.semaphore_signal(barrier, inc=1, device_id=place, device_id_type=MESH)
    pl.semaphore_wait(barrier, len(places))


def around():
    region, count = lax.axis_index("region"), lax.axis_size("region")
    following, previous = lax.rem(region + 1, count), lax.rem(region + count - 1, count)
    return {"region": following}, {"region": previous}


def encode_kernel(
    depth, day_ref, matrices_ref, in_ref, outp_ref, gains_ref, dates_ref, valid_ref, x_ref, picks_ref,
    rows_ref, edge_ref, near_ref,
    full_ref, small_out_ref, total_ref, x4_out, a0_out, h1_out, t1_out, unit_out, scale_out, mesh_out,
    sent_out, left_ref, right_ref, eh_out, eht_out, d_out, dt_out,
    edge_cols_ref, grid_cols_ref, eh_ref, eht_ref, d_ref, dt_ref, block_ref, pack_ref, pick_ref, out_ref, x4_ref, xl_ref, a0_ref, h1_ref, t1_ref, unit_ref, scale_ref,
    mesh_ref, sent_ref, buf_ref, w_ref, small_ref, count_ref, counts_ref, sums_ref, heard_ref,
    local_sem, z_send, z_recv, p_send, p_recv, d_send, d_recv, c_send, c_recv, n_send, n_recv,
    s_send, s_recv, w_sem, o_sem, e_send, e_recv, q_sem, b_sem,
):
    base, slot, core, side, up, far = neighbours()
    z = lax.axis_index("row")
    half = block_ref.shape[1] // 2
    low, high = pl.ds(0, half), pl.ds(half, half)
    to_core, to_side, to_up = ({"region": base + place} for place in (core, side, up))
    to_next, to_previous = around()
    to_z = [None] + [{"row": lax.rem(z + d, depth)} for d in range(1, depth)]
    steps = range(1, depth)
    members, variables, points = x_ref.shape
    nodes = a0_ref.shape[1]
    halo = left_ref.shape[1]
    greet(to_z[1:] + [to_core, to_side, to_up, to_next, to_previous])

    def at(d):
        return lax.rem(z + depth - d, depth)

    def arrived(target, receive):
        remote(target, target, receive, receive, to_core).wait_recv()

    def gone(origin, receive):
        remote(origin, origin, receive, receive, to_core).wait_send()

    for k in range(SLOTS - 1):
        block_ref[slot_of(k)] = matrices_ref[k].astype(BF16)
    pack_ref[...] = jnp.zeros_like(pack_ref)
    pack_ref[IN_ROW : IN_ROW + variables, :] = in_ref[...]
    pack_ref[OUT_ROW : OUT_ROW + variables, :] = outp_ref[...]
    pack_ref[GAIN_ROW : GAIN_ROW + gains_ref.shape[0], :] = gains_ref[...]
    pack_ref[DATE_ROW : DATE_ROW + dates_ref.shape[0], :] = dates_ref[...]
    block_ref[SMALL] = jnp.transpose(pack_ref[...]).astype(BF16)
    for d in steps:
        remote(
            block_ref.at[slot], full_ref.at[slot, z], z_send.at[d], z_recv.at[d], to_z[d]
        ).start()
    own = pltpu.make_async_copy(block_ref, full_ref.at[:, z], local_sem)
    own.start()
    valid = jnp.sum(valid_ref[...].astype(F32), axis=1, keepdims=True)
    valid = jnp.sum(valid, axis=0, keepdims=True)
    count_ref[...] = jnp.broadcast_to(valid, count_ref.shape)
    for d in steps:
        remote(count_ref, counts_ref.at[d], n_send.at[d], n_recv.at[d], to_z[d]).start()

    table, k_edge, k_near = eht_ref.shape[0], edge_ref.shape[0], near_ref.shape[0]
    k_grid = picks_ref.shape[0]
    wide = 128
    pieces = nodes // wide
    edge_cols_ref[...] = columns_of(edge_ref[...])
    grid_cols_ref[...] = columns_of(picks_ref[...])

    def build_edges(i, carry):
        k, piece = i // pieces, lax.rem(i, pieces)
        inside = pl.ds(pl.multiple_of(piece * wide, wide), wide)
        across = pl.ds(pl.multiple_of(i * wide, wide), wide)
        columns = edge_cols_ref[inside, :].astype(F32)
        chosen = lax.broadcasted_iota(jnp.int32, columns.shape, 1) == k
        column = jnp.sum(jnp.where(chosen, columns, 0.0), axis=1, keepdims=True).astype(jnp.int32)
        eh_ref[across, :] = count_columns(column, table, 1)
        lines = edge_ref[:, inside].astype(F32)
        chosen = lax.broadcasted_iota(jnp.int32, lines.shape, 0) == k
        line = jnp.sum(jnp.where(chosen, lines, 0.0), axis=0, keepdims=True).astype(jnp.int32)
        eht_ref[:, across] = count_rows(line, table)
        return carry

    def build_near(i, carry):
        inside = pl.ds(pl.multiple_of(i * wide, wide), wide)
        near = near_ref[:, inside]
        d_ref[inside, :] = count_columns(columns_of(near), nodes, k_near)
        dt_ref[:, inside] = count_rows(near, nodes)
        return carry

    def build_grid(i, carry):
        inside = pl.ds(pl.multiple_of(i * 64, 64), 64)
        pick_ref[inside, :] = count_columns(grid_cols_ref[inside, :], points, k_grid)
        return carry

    lax.fori_loop(0, nodes // 64, build_grid, 0)
    out_ref[...] = count_columns(columns_of(rows_ref[...]), nodes, 1)
    edges, nears = k_edge * pieces, points // wide
    share = -(-edges // (depth - 1))

    def from_z(d, carry):
        chunk = full_ref.at[slot, at(d)]
        arrived(chunk, z_recv.at[d])
        remote(chunk, chunk, p_send.at[0, d], p_recv.at[0, d], to_side).start()
        remote(chunk, chunk, p_send.at[1, d], p_recv.at[1, d], to_up).start()
        remote(chunk, chunk, c_send.at[0, d], c_recv.at[0, d], to_core).start()
        lax.fori_loop((d - 1) * share, jnp.minimum(d * share, edges), build_edges, 0)
        return carry

    lax.fori_loop(1, depth, from_z, 0)
    builds = [
        pltpu.make_async_copy(ref, target, b_sem.at[k])
        for k, (ref, target) in enumerate(
            ((eh_ref, eh_out), (eht_ref, eht_out), (d_ref, d_out), (dt_ref, dt_out))
        )
    ]
    builds[0].start()
    builds[1].start()

    total = count_ref[...]
    for d in steps:
        arrived(counts_ref.at[d], n_recv.at[d])
        total = total + counts_ref[d]
    sums_ref[0] = total
    partners = (to_core, to_side, to_up)

    def count_copy(step):
        return remote(
            sums_ref.at[step], heard_ref.at[step], s_send.at[step], s_recv.at[step], partners[step]
        )

    count_copy(0).start()

    def from_sides(d, carry):
        chunk = full_ref.at[side, at(d)]
        arrived(chunk, p_recv.at[0, d])
        part = full_ref.at[side, at(d), low]
        remote(part, part, d_send.at[0, d], d_recv.at[0, d], to_up).start()
        remote(chunk, chunk, c_send.at[1, d], c_recv.at[1, d], to_core).start()
        chunk = full_ref.at[up, at(d)]
        arrived(chunk, p_recv.at[1, d])
        part = full_ref.at[up, at(d), high]
        remote(part, part, d_send.at[1, d], d_recv.at[1, d], to_side).start()
        remote(chunk, chunk, c_send.at[2, d], c_recv.at[2, d], to_core).start()
        return carry

    lax.fori_loop(1, depth, from_sides, 0)

    def gather_inputs(m, carry):
        x4 = dot_nt(pick_ref[...], x_ref[m]) * (1.0 / k_grid)
        top, rest = split_two(x4)
        x4_ref[m] = top
        xl_ref[m] = rest
        return carry

    lax.fori_loop(0, members, gather_inputs, 0)
    for step in (1, 2):
        count_copy(step - 1).wait_recv()
        total = total + heard_ref[step - 1]
        sums_ref[step] = total
        count_copy(step).start()

    def from_far(d, carry):
        arrived(full_ref.at[far, at(d), low], d_recv.at[0, d])
        arrived(full_ref.at[far, at(d), high], d_recv.at[1, d])
        chunk = full_ref.at[far, at(d)]
        remote(chunk, chunk, c_send.at[3, d], c_recv.at[3, d], to_core).start()
        return carry

    lax.fori_loop(1, depth, from_far, 0)
    lax.fori_loop(0, nears, build_near, 0)
    builds[2].start()
    builds[3].start()
    count_copy(2).wait_recv()
    total_ref[...] = total + heard_ref[2]

    def from_core(d, carry):
        for k in range(4):
            arrived(full_ref.at[core, at(d)], c_recv.at[k, d])
        return carry

    lax.fori_loop(1, depth, from_core, 0)
    own.wait()

    loads = [
        pltpu.make_async_copy(full_ref.at[j], w_ref.at[k], w_sem.at[k])
        for k, j in enumerate((SMALL, slot_of(0), slot_of(1)))
    ]
    for copy in loads:
        copy.start()
    for copy in loads:
        copy.wait()
    small_ref[...] = jnp.transpose(w_ref[0].reshape(LATENT, LATENT))
    small_copy = pltpu.make_async_copy(small_ref, small_out_ref, q_sem)
    small_copy.start()
    kept = (
        (x4_ref, x4_out), (a0_ref, a0_out), (h1_ref, h1_out), (t1_ref, t1_out), (unit_ref, unit_out),
        (scale_ref, scale_out), (mesh_ref, mesh_out), (sent_ref, sent_out),
    )

    def kept_copies(m):
        return [
            pltpu.make_async_copy(ref.at[m], target.at[m], o_sem.at[k, m])
            for k, (ref, target) in enumerate(kept)
        ]

    def halo_copies(m):
        return [
            remote(buf_ref.at[m, halo:], left_ref.at[m], e_send.at[0, m], e_recv.at[0, m], to_next),
            remote(buf_ref.at[m, :halo], right_ref.at[m], e_send.at[1, m], e_recv.at[1, m], to_previous),
        ]

    def encode_member(m, carry):
        win = small_ref[IN_ROW : IN_ROW + variables, :]
        agg = dot(x4_ref[m], win) + dot(xl_ref[m], win) + date_row(small_ref, day_ref[m])
        a0 = agg.astype(BF16)
        hid, t1 = silu_parts(0.5 * dot(a0, w_ref[1].reshape(LATENT, LATENT)))
        h1 = hid.astype(BF16)
        unit, scale = normalise(dot(h1, w_ref[2].reshape(LATENT, LATENT)))
        mesh = agg + unit * gain_row(small_ref, 0)
        low_mesh = mesh.astype(BF16)
        buf_ref[m] = dot(out_ref[...], low_mesh).astype(BF16)
        for copy in halo_copies(m):
            copy.start()
        a0_ref[m] = a0
        h1_ref[m] = h1
        t1_ref[m] = t1.astype(BF16)
        unit_ref[m] = unit
        scale_ref[m] = scale
        mesh_ref[m] = mesh
        sent_ref[m] = low_mesh
        for copy in kept_copies(m):
            copy.start()
        return carry

    lax.fori_loop(0, members, encode_member, 0)

    def finish_member(m, carry):
        for copy in halo_copies(m) + kept_copies(m):
            copy.wait()
        return carry

    def finish_row(d, carry):
        gone(block_ref.at[slot], z_send.at[d])
        gone(count_ref, n_send.at[d])
        chunk = full_ref.at[slot, at(d)]
        for k in range(2):
            gone(chunk, p_send.at[k, d])
            gone(full_ref.at[slot, at(d), low], d_send.at[k, d])
        for k in range(4):
            gone(chunk, c_send.at[k, d])
        return carry

    lax.fori_loop(0, members, finish_member, 0)
    lax.fori_loop(1, depth, finish_row, 0)
    for step in range(3):
        count_copy(step).wait_send()
    for copy in builds:
        copy.wait()
    small_copy.wait()


def encode(
    day, matrices, in_proj, out_proj, gains, dates, valid, inputs, picks, rows, edges, near, depth
):
    hbm = pl.BlockSpec(memory_space=pl.ANY)
    vmem = pl.BlockSpec(memory_space=pltpu.VMEM)
    dma = pltpu.SemaphoreType.DMA
    members, variables, points = inputs.shape
    nodes = picks.shape[1]
    halo = rows.shape[1] // 2
    share = matrices.shape[1]
    nodes_of = (members, nodes, LATENT)
    table, pairs = nodes + 2 * halo, edges.shape[0] * nodes
    counts = ((pairs, table), (table, pairs), (points, nodes), (nodes, points))
    kept = [
        ((members, nodes, variables), BF16),
        (nodes_of, BF16),
        (nodes_of, BF16),
        (nodes_of, BF16),
        (nodes_of, F32),
        ((members, nodes, 1), F32),
        (nodes_of, F32),
        (nodes_of, BF16),
    ]
    return pl.pallas_call(
        partial(encode_kernel, depth),
        in_specs=[pl.BlockSpec(memory_space=pltpu.SMEM)] + [vmem] * 11,
        out_shape=[
            shape_of((SLOTS, depth, share, LATENT), BF16),
            shape_of((LATENT, LATENT), BF16),
            shape_of((8, 128), F32),
            *(shape_of(*one) for one in kept),
            shape_of((members, halo, LATENT), BF16),
            shape_of((members, halo, LATENT), BF16),
            *(shape_of(one, BF16) for one in counts),
        ],
        out_specs=[hbm, hbm, vmem] + [hbm] * (len(kept) + 2 + len(counts)),
        scratch_shapes=[
            pltpu.VMEM((nodes, 8), jnp.int32),
            pltpu.VMEM((nodes, 8), jnp.int32),
            *(pltpu.VMEM(one, BF16) for one in counts),
            pltpu.VMEM((SLOTS, share, LATENT), BF16),
            pltpu.VMEM((LATENT, share), F32),
            pltpu.VMEM((nodes, points), BF16),
            pltpu.VMEM((2 * halo, nodes), BF16),
            pltpu.VMEM(*kept[0]),
            *(pltpu.VMEM(*one) for one in kept),
            pltpu.VMEM((members, 2 * halo, LATENT), BF16),
            pltpu.VMEM((3, depth, share, LATENT), BF16),
            pltpu.VMEM((LATENT, LATENT), BF16),
            pltpu.VMEM((8, 128), F32),
            pltpu.VMEM((depth, 8, 128), F32),
            pltpu.VMEM((3, 8, 128), F32),
            pltpu.VMEM((3, 8, 128), F32),
            dma,
            dma((depth,)),
            dma((depth,)),
            dma((2, depth)),
            dma((2, depth)),
            dma((2, depth)),
            dma((2, depth)),
            dma((4, depth)),
            dma((4, depth)),
            dma((depth,)),
            dma((depth,)),
            dma((3,)),
            dma((3,)),
            dma((3,)),
            dma((len(kept), members)),
            dma((2, members)),
            dma((2, members)),
            dma,
            dma((len(counts),)),
        ],
        compiler_params=pltpu.CompilerParams(
            collective_id=0, has_side_effects=True, vmem_limit_bytes=VMEM_BYTES
        ),
    )(
        day, matrices, in_proj, out_proj, gains, dates, valid, inputs, picks, rows, edges, near
    )


def reduce_kernel(
    depth, day_ref, late_ref, momentum_ref, count_ref, dmesh_in, dhalo_ref, rows_ref, x4_in, a0_in,
    h1_in, t1_in, unit_in, scale_in, weights_ref, small_ref, gxd_ref, dsum_ref, gout_ref, ggain_ref,
    loss_ref,
    g_ref, x_ref,
    dmesh_ref, ret_ref, x4_ref, a0_ref, h1_ref, t1_ref, unit_ref, scale_ref, m_ref, back_ref, pack_ref,
    early_ref, own_ref, heard_ref, snd_ref, rcv_ref, snd_low_ref, rcv_low_ref, acc_ref, zr_ref,
    g_own_ref, mb_ref, x_own_ref,
    i_sem, e_send, e_recv, l_sem, h_send, h_recv, p_send, p_recv, q_send, q_recv, z_send, z_recv,
    m_send, m_recv, g_local, g_send, g_recv, x_local, x_send, x_recv,
):
    base, slot, core, side, up, far = neighbours()
    z = lax.axis_index("row")
    rows = acc_ref.shape[0] // depth
    chips = SLOTS // 2
    mine = slot // 2
    parity = lax.rem(slot, 2)
    members, variables = x4_ref.shape[0], x4_ref.shape[2]
    halo = dhalo_ref.shape[1] // 2
    to_core, to_side, to_up, to_far = ({"region": base + place} for place in (core, side, up, far))
    to_next, to_previous = around()
    to_place = (to_far, to_side, to_up)
    places = (far, side, up)
    to_z = [None] + [{"row": lax.rem(z + d, depth)} for d in range(1, depth)]
    greet(to_z[1:] + [to_core, to_side, to_up, to_far, to_next, to_previous])
    sent = []

    def part_of(b):
        return pl.ds(pl.multiple_of(b * rows, rows), rows)

    def send(*args):
        copy = remote(*args)
        copy.start()
        sent.append(copy)

    def arrived(target, receive):
        remote(target, target, receive, receive, to_core).wait_recv()

    def load(*args):
        copy = pltpu.make_async_copy(*args)
        copy.start()
        return copy

    def halo_copies(m):
        return [
            remote(dhalo_ref.at[m, halo:], ret_ref.at[m, :halo], e_send.at[0, m], e_recv.at[0, m], to_next),
            remote(
                dhalo_ref.at[m, :halo], ret_ref.at[m, halo:], e_send.at[1, m], e_recv.at[1, m], to_previous
            ),
        ]

    inner = ((dmesh_in, dmesh_ref), (x4_in, x4_ref), (a0_in, a0_ref), (h1_in, h1_ref), (t1_in, t1_ref),
             (unit_in, unit_ref), (scale_in, scale_ref))

    def inner_loads(m):
        return [
            pltpu.make_async_copy(ref.at[m], target.at[m], i_sem.at[k, m])
            for k, (ref, target) in enumerate(inner)
        ]

    for m in range(members):
        for copy in halo_copies(m):
            copy.start()
    for m in range(members):
        for copy in inner_loads(m):
            copy.start()
    m_loads = []
    first = load(late_ref.at[0], early_ref.at[2], i_sem.at[len(inner), 0])
    for k in range(2):
        m_loads.append(load(weights_ref.at[slot_of(k)], m_ref.at[k], i_sem.at[len(inner), 1 + k]))

    def late_copy(chip):
        return remote(
            late_ref.at[1 + chip], heard_ref.at[chip], h_send.at[chip, 0], h_recv.at[chip, 0], to_core
        )

    def late_load(chip):
        return pltpu.make_async_copy(late_ref.at[1 + chip], own_ref.at[chip], l_sem.at[chip])

    def early_copy(chip, b):
        return remote(
            early_ref.at[chip, part_of(b)], heard_ref.at[chip, part_of(b)], h_send.at[chip, b],
            h_recv.at[chip, b], to_core,
        )

    def low_copy(b):
        return remote(
            snd_low_ref.at[part_of(b)], rcv_low_ref.at[mine, part_of(b)], q_send.at[b], q_recv.at[mine, b],
            {"region": base + SMALL},
        )

    def chip_copy(chip, b):
        return remote(
            snd_ref.at[chip, part_of(b)], rcv_ref.at[mine, part_of(b)], p_send.at[chip, b],
            p_recv.at[mine, b], {"region": base + 2 * chip + parity},
        )

    def pass_on(chip, b, own):
        part = part_of(b)
        total = own[chip, part, :] + heard_ref[chip, part, :]

        @pl.when(mine == chip)
        def _():
            acc_ref[part, :] = total

        @pl.when(mine != chip)
        def _():
            snd_ref[chip, part, :] = total.astype(BF16)
            chip_copy(chip, b).start()

    def pass_late(chip):
        @pl.when(parity == 1)
        def _():
            late_load(chip).wait()
            late_copy(chip).wait_recv()

            def piece(b, carry):
                pass_on(chip, b, own_ref)
                return carry

            lax.fori_loop(0, depth, piece, 0)

    def pass_early(b, carry):
        @pl.when(parity == 0)
        def _():
            def piece(chip, carry):
                early_copy(chip, b).wait_recv()
                pass_on(chip, b, early_ref)
                return carry

            lax.fori_loop(0, chips, piece, 0)
            part = part_of(b)

            @pl.when(mine != SMALL // 2)
            def _():
                total = early_ref[SMALL // 2, part, :] + heard_ref[SMALL // 2, part, :]
                snd_low_ref[part, :] = (total - total.astype(BF16).astype(F32)).astype(BF16)
                low_copy(b).start()

        return carry

    @pl.when(parity == 0)
    def _():
        for chip in range(chips):
            late_copy(chip).start()

    @pl.when(parity == 1)
    def _():
        for chip in range(chips):
            late_load(chip).start()

    lines = lax.broadcasted_iota(jnp.int32, (16, LATENT), 0)
    back_ref[...] = count_rows(rows_ref[...], back_ref.shape[0])
    wout = small_ref[OUT_ROW : OUT_ROW + variables, :]
    pack_ref[...] = jnp.zeros_like(pack_ref)
    top, rest = split_two(gxd_ref[...])
    pack_ref[IN_ROW : IN_ROW + variables, :] = dot(top, wout) + dot(rest, wout)
    pack_ref[OUT_ROW : OUT_ROW + variables, :] = gout_ref[...]
    pack_ref[GAIN_ROW + 1 : GAIN_ROW + 3, :] = ggain_ref[...]
    loss = jnp.sum(loss_ref[...], axis=0, keepdims=True)
    pack_ref[LOSS_ROW : LOSS_ROW + 1, :] = jnp.broadcast_to(loss, (1, LATENT))
    early_ref[0:2] = jnp.zeros((2, LATENT, LATENT), F32)
    for copy in m_loads:
        copy.wait()

    def member_back(m, carry):
        for copy in inner_loads(m):
            copy.wait()
        for copy in halo_copies(m):
            copy.wait()
        dmesh = dmesh_ref[m] + dot(back_ref[...], ret_ref[m])
        unit = unit_ref[m]
        pack_ref[GAIN_ROW : GAIN_ROW + 1, :] += jnp.sum(dmesh * unit, axis=0, keepdims=True)
        dc = norm_back(dmesh, gain_row(small_ref, 0), unit, scale_ref[m]).astype(BF16)
        early_ref[1] += dot_tn(h1_ref[m], dc)
        du = (dot_nt(dc, m_ref[1]) * t1_ref[m].astype(F32)).astype(BF16)
        early_ref[0] += dot_tn(a0_ref[m], du)
        dagg = dmesh + dot_nt(du, m_ref[0])
        pack_ref[IN_ROW : IN_ROW + variables, :] += dot_tn(x4_ref[m], dagg.astype(BF16))
        top, rest = split_two(dsum_ref[m])
        date = jnp.sum(dagg, axis=0, keepdims=True) + dot_tn(top, wout) + dot_tn(rest, wout)
        pack_ref[DATE_ROW : DATE_ROW + 16, :] += jnp.where(lines == day_ref[m], date, 0.0)

        @pl.when(m < chips)
        def _():
            pass_late(m)

        return carry

    lax.fori_loop(0, members, member_back, 0)
    for chip in range(members, chips):
        pass_late(chip)
    early_ref[SMALL // 2] = jnp.transpose(pack_ref[...])
    first.wait()

    @pl.when(parity == 1)
    def _():
        for b in range(depth):
            for chip in range(chips):
                early_copy(chip, b).start()

    lax.fori_loop(0, depth, pass_early, 0)

    sources = [lax.rem(mine + i, chips) for i in range(1, chips)]
    def z_copy(b):
        d = lax.rem(b - z + depth, depth)
        return remote(acc_ref.at[part_of(b)], zr_ref.at[d], z_send.at[b], z_recv.at[d], {"row": b + 0 * z})

    def across_z(b, carry):
        part = part_of(b)
        total = acc_ref[part, :]
        for c in sources:
            arrived(rcv_ref.at[c, part], p_recv.at[c, b])
            total = total + rcv_ref[c, part, :].astype(F32)
        acc_ref[part, :] = total

        @pl.when(slot == SMALL)
        def _():
            low = acc_ref[part, :]
            for c in sources:
                arrived(rcv_low_ref.at[c, part], q_recv.at[c, b])
                low = low + rcv_low_ref[c, part, :].astype(F32)
            acc_ref[part, :] = low

        @pl.when(z != b)
        def _():
            z_copy(b).start()

        return carry

    lax.fori_loop(0, depth, across_z, 0)
    zr_ref[0] = acc_ref[pl.ds(pl.multiple_of(z * rows, rows), rows), :]
    for d in range(1, depth):
        arrived(zr_ref.at[d], z_recv.at[d])
    g_own = zr_ref[z]
    for place in range(1, depth):
        g_own = g_own + zr_ref[lax.rem(z + depth - place, depth)]
    g_own_ref[...] = g_own
    momentum = (
        MUON_MOMENTUM * momentum_ref[mine + (SLOTS // 2 - 1) * parity]
        + (2.0 / count_ref[0:1, 0:1]) * g_own
    )
    mb_ref[0] = momentum.astype(BF16)
    for d in range(1, depth):
        send(mb_ref.at[0], mb_ref.at[d], m_send.at[d], m_recv.at[d], to_z[d])
    g_copy = load(g_own_ref, g_ref.at[slot], g_local)
    for k in range(3):
        send(g_own_ref, g_ref.at[slot], g_send.at[k], g_recv.at[k], to_place[k])
    send(g_own_ref, g_ref.at[slot], g_send.at[3], g_recv.at[3], to_core)

    for d in range(1, depth):
        arrived(mb_ref.at[d], m_recv.at[d])
    everything = jnp.concatenate([mb_ref[d] for d in range(depth)], axis=0)
    wide = everything.astype(F32)
    squares = jnp.sum(jnp.sum(wide * wide, axis=1, keepdims=True), axis=0, keepdims=True)
    inverse = lax.rsqrt(squares + 1e-07)
    turn = momentum * inverse
    current = (wide * inverse).astype(BF16)
    turn_low = turn.astype(BF16)
    for sweep in range(NS_ITERS):
        gram = dot_tn(current, current)
        gram_low = gram.astype(BF16)
        mixing = NS_COEFFS[1] * gram + NS_COEFFS[2] * dot(gram_low, gram_low)
        mixing = mixing.astype(BF16)
        turn = NS_COEFFS[0] * turn + dot(turn_low, mixing)
        turn_low = turn.astype(BF16)
        if sweep < NS_ITERS - 1:
            current = (NS_COEFFS[0] * current.astype(F32) + dot(current, mixing)).astype(BF16)
    x_own_ref[...] = turn_low
    x_copy = pltpu.make_async_copy(x_own_ref, x_ref.at[slot], x_local)
    x_copy.start()
    for k in range(3):
        send(x_own_ref, x_ref.at[slot], x_send.at[k], x_recv.at[k], to_place[k])
    send(x_own_ref, x_ref.at[slot], x_send.at[3], x_recv.at[3], to_core)

    for target, send_sem, recv_sem in ((g_ref, g_send, g_recv), (x_ref, x_send, x_recv)):
        for k in range(3):
            chunk = target.at[places[k]]
            arrived(chunk, recv_sem.at[k])
            send(chunk, chunk, send_sem.at[4 + k], recv_sem.at[4 + k], to_core)
    for target, recv_sem in ((g_ref, g_recv), (x_ref, x_recv)):
        for k in range(3, 7):
            arrived(target.at[core], recv_sem.at[k])
    for copy in sent:
        copy.wait_send()
    @pl.when(parity == 0)
    def _():
        for chip in range(chips):
            late_copy(chip).wait_send()

    @pl.when(parity == 1)
    def _():
        for b in range(depth):
            for chip in range(chips):
                early_copy(chip, b).wait_send()

    for b in range(depth):
        for chip in range(chips):

            @pl.when(mine != chip)
            def _():
                chip_copy(chip, b).wait_send()

        @pl.when((mine != SMALL // 2) & (parity == 0))
        def _():
            low_copy(b).wait_send()

        @pl.when(z != b)
        def _():
            z_copy(b).wait_send()

    g_copy.wait()
    x_copy.wait()


def reduce_gradients(
    day, late, momentum, count, dmesh, dhalo, rows, kept, weights, small, gxd, dsum, gout, ggain, loss,
    depth,
):
    hbm = pl.BlockSpec(memory_space=pl.ANY)
    vmem = pl.BlockSpec(memory_space=pltpu.VMEM)
    dma = pltpu.SemaphoreType.DMA
    members, nodes, width = dmesh.shape
    height = LATENT
    share = height // depth
    halo = dhalo.shape[1]
    chips = SLOTS // 2

    return pl.pallas_call(
        partial(reduce_kernel, depth),
        in_specs=[pl.BlockSpec(memory_space=pltpu.SMEM), hbm, vmem, vmem, hbm, vmem, vmem]
        + [hbm] * len(kept)
        + [hbm]
        + [vmem] * 6,
        out_shape=[
            shape_of((SLOTS, share, width), F32),
            shape_of((SLOTS, share, width), BF16),
        ],
        out_specs=[hbm, hbm],
        scratch_shapes=[
            pltpu.VMEM(dmesh.shape, F32),
            pltpu.VMEM(dhalo.shape, BF16),
            *(pltpu.VMEM(one.shape, one.dtype) for one in kept),
            pltpu.VMEM((2, height, width), BF16),
            pltpu.VMEM((nodes, halo), BF16),
            pltpu.VMEM((height, width), F32),
            pltpu.VMEM((4, height, width), F32),
            pltpu.VMEM((chips, height, width), F32),
            pltpu.VMEM((chips, height, width), F32),
            pltpu.VMEM((chips, height, width), BF16),
            pltpu.VMEM((chips, height, width), BF16),
            pltpu.VMEM((height, width), BF16),
            pltpu.VMEM((chips, height, width), BF16),
            pltpu.VMEM((height, width), F32),
            pltpu.VMEM((depth, share, width), F32),
            pltpu.VMEM((share, width), F32),
            pltpu.VMEM((depth, share, width), BF16),
            pltpu.VMEM((share, width), BF16),
            dma((len(kept) + 2, members)),
            dma((2, members)),
            dma((2, members)),
            dma((chips,)),
            dma((chips, depth)),
            dma((chips, depth)),
            dma((chips, depth)),
            dma((chips, depth)),
            dma((depth,)),
            dma((chips, depth)),
            dma((depth,)),
            dma((depth,)),
            dma((depth,)),
            dma((depth,)),
            dma,
            dma((7,)),
            dma((7,)),
            dma,
            dma((7,)),
            dma((7,)),
        ],
        compiler_params=pltpu.CompilerParams(
            collective_id=1, has_side_effects=True, vmem_limit_bytes=VMEM_BYTES
        ),
    )(
        day, late, momentum, count, dmesh, dhalo, rows, *kept, weights, small, gxd, dsum, gout,
        ggain, loss,
    )


def turn_whole(sums, count, momentum):
    blocks = jnp.stack([sums[slot_of(k)] for k in range(SLOTS - 1)])
    blocks = MUON_MOMENTUM * momentum + (2.0 / count[0, 0]) * blocks
    squares = lax.psum(jnp.sum(blocks * blocks, axis=(1, 2)), "row")
    current = blocks * lax.rsqrt(squares + 1e-07)[:, None, None]

    def product(expression, left, right):
        return jnp.einsum(expression, left, right, precision=lax.Precision.HIGHEST)

    for _ in range(NS_ITERS):
        gram = lax.psum(product("mrk,mrl->mkl", current, current), "row")
        mixing = NS_COEFFS[1] * gram + NS_COEFFS[2] * product("mkj,mjl->mkl", gram, gram)
        current = NS_COEFFS[0] * current + product("mrk,mkl->mrl", current, mixing)
    current = current.astype(BF16)
    by_slot = {slot_of(k): current[k] for k in range(SLOTS - 1)}
    return jnp.stack([by_slot.get(k, current[0]) for k in range(SLOTS)])


def finish_kernel(
    g_ref, rest_ref, x_ref, count_ref, matrix_ref, momentum_ref,
    in_ref, in1_ref, in2_ref, out_ref, out1_ref, out2_ref, gain_ref, gain1_ref, gain2_ref,
    date_ref, date1_ref, date2_ref,
    new_matrix_ref, new_momentum_ref,
    nin_ref, nin1_ref, nin2_ref, nout_ref, nout1_ref, nout2_ref, ngain_ref, ngain1_ref, ngain2_ref,
    ndate_ref, ndate1_ref, ndate2_ref, loss_ref, valid_ref,
):
    scale = 2.0 / count_ref[0:1, 0:1]
    new_momentum_ref[...] = MUON_MOMENTUM * momentum_ref[...] + scale * g_ref[...]
    new_matrix_ref[...] = (
        matrix_ref[...] * (1.0 - MUON_RATE * WEIGHT_DECAY) - MUON_RATE * x_ref[...].astype(F32)
    )

    @pl.when(pl.program_id(0) == 0)
    def _():
        rest = jnp.transpose(rest_ref[0])
        loss_ref[0, 0] = jnp.sum(rest[LOSS_ROW : LOSS_ROW + 1, 0:1])
        valid_ref[0, 0] = jnp.sum(count_ref[0:1, 0:1])
        rest = rest * scale
        for row, rate, decay, old, new in (
            (IN_ROW, MATRIX_RATE, WEIGHT_DECAY, (in_ref, in1_ref, in2_ref), (nin_ref, nin1_ref, nin2_ref)),
            (OUT_ROW, MATRIX_RATE, WEIGHT_DECAY, (out_ref, out1_ref, out2_ref),
             (nout_ref, nout1_ref, nout2_ref)),
            (GAIN_ROW, VECTOR_RATE, 0.0, (gain_ref, gain1_ref, gain2_ref),
             (ngain_ref, ngain1_ref, ngain2_ref)),
            (DATE_ROW, VECTOR_RATE, 0.0, (date_ref, date1_ref, date2_ref),
             (ndate_ref, ndate1_ref, ndate2_ref)),
        ):
            weight, first, second = (ref[...] for ref in old)
            gradient = rest[row : row + weight.shape[0], :]
            for ref, value in zip(new, adam_update(weight, gradient, first, second, rate, decay)):
                ref[...] = value


def finish(sums, turned, count, matrices, momentum, vectors):
    share, width = sums.shape[1:]

    def slot_block():
        return pl.BlockSpec((1, share, width), lambda m: (slot_of(m), 0, 0))

    one = pl.BlockSpec((1, share, width), lambda m: (m, 0, 0))
    return pl.pallas_call(
        finish_kernel,
        grid=(matrices.shape[0],),
        in_specs=[
            slot_block(), pl.BlockSpec((1, share, width), lambda m: (SMALL, 0, 0)), slot_block(),
            whole(count.shape), one, one, *(whole(v.shape) for v in vectors),
        ],
        out_shape=[shape_of(matrices.shape, F32)] * 2
        + [shape_of(v.shape, F32) for v in vectors]
        + [shape_of((1, 1), F32)] * 2,
        out_specs=[one, one] + [whole(v.shape) for v in vectors]
        + [pl.BlockSpec(memory_space=pltpu.SMEM)] * 2,
        compiler_params=pltpu.CompilerParams(
            dimension_semantics=("arbitrary",), vmem_limit_bytes=VMEM_BYTES
        ),
    )(sums, sums, turned, count, matrices, momentum, *vectors)


def adam_update(weight, gradient, first_moment, second_moment, step_rate, decay_rate):
    first_new = BETA_ONE * first_moment + (1.0 - BETA_ONE) * gradient
    second_new = BETA_TWO * second_moment + (1.0 - BETA_TWO) * gradient * gradient
    unbiased_one = first_new / (1.0 - BETA_ONE**STEP)
    unbiased_two = second_new / (1.0 - BETA_TWO**STEP)
    weight_new = weight * (1.0 - step_rate * decay_rate) - step_rate * unbiased_one / (
        jnp.sqrt(unbiased_two) + 1e-08
    )
    return (weight_new, first_new, second_new)


def body(
    inputs,
    targets,
    valid_steps,
    var_weights,
    grid_to_mesh,
    mesh_edges,
    send_rows,
    mesh_to_grid,
    date_index,
    matrices,
    matrices_momentum,
    in_proj,
    in_first,
    in_second,
    out_proj,
    out_first,
    out_second,
    norm_gains,
    gains_first,
    gains_second,
    date_table,
    date_first,
    date_second,
):
    inputs = jnp.swapaxes(inputs, 1, 2)
    targets = jnp.swapaxes(targets, 1, 2)
    members, variables, points = inputs.shape
    nodes = grid_to_mesh.shape[0]
    halo = send_rows.shape[0] // 2
    table = nodes + 2 * halo
    k_edge = mesh_edges.shape[1]
    k_pick = mesh_to_grid.shape[1]
    dates = date_table.shape[0]

    depth = lax.axis_size("row")
    regions = lax.axis_size("region")
    groups = [[g * SLOTS + q for g in range(regions // SLOTS)] for q in range(SLOTS)]
    scalars = pl.BlockSpec(memory_space=pltpu.SMEM)
    hbm = pl.BlockSpec(memory_space=pl.ANY)
    gathered, small, count, *kept, left, right, eh, eht, d, dt = encode(
        date_index, matrices, in_proj, out_proj.T, norm_gains, date_table, valid_steps, inputs,
        grid_to_mesh.T, send_rows[None, :], mesh_edges.T, mesh_to_grid.T, depth,
    )
    mesh1, sent = kept[6:]
    if regions > SLOTS:
        count = lax.psum(count, "region", axis_index_groups=groups)
    weights = gathered.reshape(SLOTS, LATENT, LATENT)
    node_block = per_member((nodes, LATENT))

    def matrix(j):
        place = slot_of(j)
        return pl.BlockSpec(
            (1, LATENT, LATENT), lambda m: (place, 0, 0), pipeline_mode=pl.Buffered(1)
        )

    out_shape = (variables, LATENT)
    late, gout, gxd, dsum, ggain_late, loss_row, dmesh, dhalo = call(
        partial(main_kernel, k_pick),
        members,
        [
            scalars,
            node_block,
            node_block,
            per_member((halo, LATENT)),
            per_member((halo, LATENT)),
            per_member((variables, points)),
            per_member((variables, points)),
            whole((members, points)),
            whole((1, variables)),
            hbm,
            hbm,
            hbm,
            hbm,
            whole((LATENT, LATENT)),
            matrix(2),
            matrix(3),
            matrix(4),
            matrix(5),
            matrix(6),
        ],
        [
            shape_of((5, LATENT, LATENT), F32),
            shape_of(out_shape, F32),
            shape_of((variables, variables), F32),
            shape_of((members, variables, 1), F32),
            shape_of((2, LATENT), F32),
            shape_of((variables, 1), F32),
            shape_of((members, nodes, LATENT), F32),
            shape_of((members, 2 * halo, LATENT), BF16),
        ],
        [
            hbm,
            whole(out_shape),
            whole((variables, variables)),
            per_member((variables, 1)),
            whole((2, LATENT)),
            whole((variables, 1)),
            node_block,
            per_member((2 * halo, LATENT)),
        ],
        main_scratch(k_edge, nodes, points, table),
        60_000_000_000,
    )(
        date_index,
        mesh1,
        sent,
        left,
        right,
        inputs,
        targets,
        valid_steps,
        var_weights[None, :],
        eh,
        eht,
        d,
        dt,
        small,
        weights,
        weights,
        weights,
        weights,
        weights,
    )

    sums, turned = reduce_gradients(
        date_index, late, matrices_momentum, count, dmesh, dhalo, send_rows[None, :], kept[:6], weights,
        small, gxd, dsum, gout, ggain_late, loss_row, depth,
    )
    if regions > SLOTS:
        sums = lax.psum(sums, "region", axis_index_groups=groups)
        turned = turn_whole(sums, count, matrices_momentum)
    vectors = (
        in_proj, in_first, in_second, out_proj.T, out_first.T, out_second.T,
        norm_gains, gains_first, gains_second, date_table, date_first, date_second,
    )
    new = finish(sums, turned, count, matrices, matrices_momentum, vectors)
    return (
        *new[:5],
        *(part.T for part in new[5:8]),
        *new[8:14],
        new[14].reshape(()),
        new[15].reshape(()),
    )


def solution(mesh):
    in_specs = (
        P("row", "region", None),
        P("row", "region", None),
        P("row", "region"),
        P(),
        P("region", None),
        P("region", None),
        P("region"),
        P("region", None),
        P("row"),
        P(None, "row", None),
        P(None, "row", None),
        P(None, "row"),
        P(None, "row"),
        P(None, "row"),
        P("row", None),
        P("row", None),
        P("row", None),
        P(None, "row"),
        P(None, "row"),
        P(None, "row"),
        P(None, "row"),
        P(None, "row"),
        P(None, "row"),
    )
    out_specs = (
        P(None, "row", None),
        P(None, "row", None),
        P(None, "row"),
        P(None, "row"),
        P(None, "row"),
        P("row", None),
        P("row", None),
        P("row", None),
        P(None, "row"),
        P(None, "row"),
        P(None, "row"),
        P(None, "row"),
        P(None, "row"),
        P(None, "row"),
        P(),
        P(),
    )
    return jax.shard_map(body, mesh=mesh, in_specs=in_specs, out_specs=out_specs, check_vma=False)
```

```python
from functools import partial

import jax
import jax.numpy as jnp
from jax import lax
from jax.experimental import pallas as pl
from jax.experimental.pallas import tpu as pltpu
from jax.sharding import PartitionSpec as P

NS_ITERS = 2
STEP = 10
NS_COEFFS = (3.4445, -4.775, 2.0315)
MUON_RATE = 0.8
MUON_MOMENTUM = 0.95
MATRIX_RATE = 0.05
VECTOR_RATE = 0.2
BETA_ONE = 0.9
BETA_TWO = 0.95
WEIGHT_DECAY = 0.01

F32 = jnp.float32
BF16 = jnp.bfloat16
LATENT = 512
BLOCK = 1024
PARTS = 1
T_TYPE = BF16
VMEM_BYTES = 60 * 1024 * 1024
MESH = pl.DeviceIdType.MESH
SLOTS = 8
SMALL = 6
IN_ROW, OUT_ROW, GAIN_ROW, DATE_ROW, LOSS_ROW = 0, 240, 480, 496, 504


def dot(left, right):
    return jnp.dot(left, right, preferred_element_type=F32)


def dot_nt(left, right):
    return lax.dot_general(left, right, (((1,), (1,)), ((), ())), preferred_element_type=F32)


def dot_tn(left, right):
    return lax.dot_general(left, right, (((0,), (0,)), ((), ())), preferred_element_type=F32)


def split_two(values):
    high = values.astype(BF16)
    return high, (values - high.astype(F32)).astype(BF16)


def silu_parts(half):
    bend = jnp.tanh(half)
    gate = 0.5 * bend + 0.5
    hid = half * bend + half
    return hid, gate + hid * (1.0 - gate)


def normalise(values):
    centred = values - jnp.mean(values, axis=-1, keepdims=True)
    spread = jnp.mean(centred * centred, axis=-1, keepdims=True)
    scale = lax.rsqrt(spread + 1e-05)
    return centred * scale, scale


def norm_back(grad, gain, unit, scale):
    scaled = gain * grad
    mean_one = jnp.mean(scaled, axis=-1, keepdims=True)
    mean_two = jnp.mean(scaled * unit, axis=-1, keepdims=True)
    return scale * (scaled - mean_one - unit * mean_two)


def in_turn(parts):
    parts = list(parts)
    while parts:
        parts = [part for part in parts if next(part, None) is not None]


def count_columns(index, width, count):
    lanes = lax.broadcasted_iota(jnp.int32, (index.shape[0], width), 1)
    total = None
    for k in range(count):
        one = jnp.where(lanes == index[:, k : k + 1], 1.0, 0.0)
        total = one if total is None else total + one
    return total.astype(BF16)


def gain_row(small_ref, k):
    return small_ref[GAIN_ROW : GAIN_ROW + 16, :].astype(F32)[k : k + 1, :]


def date_row(small_ref, day):
    table = small_ref[DATE_ROW : DATE_ROW + 16, :].astype(F32)
    lines = lax.broadcasted_iota(jnp.int32, table.shape, 0)
    return jnp.sum(jnp.where(lines == day, table, 0.0), axis=0, keepdims=True)


def columns_of(index):
    short = 8 - index.shape[0]
    if short > 0:
        index = jnp.concatenate([index, jnp.zeros((short, index.shape[1]), index.dtype)], axis=0)
    return jnp.transpose(index)


def count_rows(index, height):
    lines = lax.broadcasted_iota(jnp.int32, (height, index.shape[1]), 0)
    total = None
    for k in range(index.shape[0]):
        one = jnp.where(lines == index[k : k + 1, :], 1.0, 0.0)
        total = one if total is None else total + one
    return total.astype(BF16)


def main_kernel(
    k_pick, day_ref, mesh_ref, sent_ref, left_ref, right_ref, x_ref, y_ref, valid_ref, varw_ref,
    eh_in, eht_in, d_in, dt_in, small_ref, m2_ref, m3_ref, m4_ref, m5_ref, m6_ref,
    slots_ref, gout_ref, gxd_ref, dsum_ref, ggain_ref, loss_ref, dmesh_ref, dhalo_ref,
    gm_ref, out_sem, in_sem, eh_ref, eht_ref, d_ref, dt_ref, ext_ref, t_ref, mm_ref, acc_ref, sender_ref,
):
    nodes = mesh_ref.shape[1]
    table = ext_ref.shape[0]
    variables, points = x_ref.shape[1:]
    k_edge = eh_ref.shape[0] // nodes
    counts = [
        pltpu.make_async_copy(source, target, in_sem.at[k])
        for k, (source, target) in enumerate(
            ((eh_in, eh_ref), (d_in, d_ref), (dt_in, dt_ref), (eht_in, eht_ref))
        )
    ]

    def counts_ready(*which):
        @pl.when(pl.program_id(0) == 0)
        def _():
            for k in which:
                counts[k].wait()

    halo = left_ref.shape[1]

    @pl.when(pl.program_id(0) == 0)
    def _():
        for copy in counts:
            copy.start()
        gm_ref[...] = jnp.zeros_like(gm_ref)
        gout_ref[...] = jnp.zeros_like(gout_ref)
        gxd_ref[...] = jnp.zeros_like(gxd_ref)
        ggain_ref[...] = jnp.zeros_like(ggain_ref)
        loss_ref[...] = jnp.zeros_like(loss_ref)

    sent = sent_ref[0]
    ext_ref[:nodes, :] = sent
    ext_ref[nodes : nodes + halo, :] = left_ref[0]
    ext_ref[nodes + halo :, :] = right_ref[0]
    receivers = 0.5 * dot(sent, m3_ref[0])
    sender_ref[...] = (0.5 * dot(ext_ref[...], m2_ref[0])).astype(BF16)

    counts_ready(0)

    def edge(k, carry):
        hid_sum, t_sum = carry
        rows = pl.ds(pl.multiple_of(k * nodes, nodes), nodes)
        hid, t = silu_parts(1.0 * dot(eh_ref[rows, :], sender_ref[...]) + receivers)
        t_ref[rows, :] = t.astype(t_ref.dtype)
        return hid_sum + hid.astype(BF16).astype(F32), t_sum + t

    zero = jnp.zeros((nodes, LATENT), F32)
    hid_sum, t_sum = lax.fori_loop(0, k_edge, edge, (zero, zero), unroll=k_edge)
    h_high = (hid_sum * (1.0 / k_edge)).astype(BF16)
    gain2 = gain_row(small_ref, 1)
    unit2, scale2 = normalise(dot(h_high, m4_ref[0]))
    mesh2 = mesh_ref[0] + unit2 * gain2
    mm_ref[...] = mesh2.astype(BF16)

    counts_ready(1, 2)
    acc_ref[...] = jnp.zeros_like(acc_ref)
    dsum_ref[...] = jnp.zeros_like(dsum_ref)
    member = pl.program_id(0)
    date = date_row(small_ref, day_ref[member])
    gain3 = gain_row(small_ref, 2)
    wout = small_ref[OUT_ROW : OUT_ROW + variables, :]
    square = (variables, variables)
    same = lax.broadcasted_iota(jnp.int32, square, 0) == lax.broadcasted_iota(jnp.int32, square, 1)
    varw = jnp.sum(jnp.where(same, varw_ref[...], 0.0), axis=1, keepdims=True)

    def decode_part(rows):
        dec = dot(d_ref[rows, :], mm_ref[...])
        a2 = (dec * (1.0 / k_pick)).astype(BF16)
        yield True
        hid, t = silu_parts(0.5 * dot(a2, m5_ref[0]))
        h2 = hid.astype(BF16)
        yield True
        unit, scale = normalise(dot(h2, m6_ref[0]))
        yield True
        x = x_ref[0, :, rows]
        grid = dot_tn(x, small_ref[IN_ROW : IN_ROW + variables, :]) + date + unit * gain3
        grid = grid.astype(BF16)
        yield True
        misfit = x.astype(F32) + dot_nt(wout, grid) - y_ref[0, :, rows].astype(F32)
        valid = valid_ref[pl.ds(member, 1), rows].astype(F32)
        weighted = valid * varw * misfit
        loss_ref[...] += jnp.sum(weighted * misfit, axis=1, keepdims=True)
        dsum_ref[0] += jnp.sum(weighted, axis=1, keepdims=True)
        dp = weighted.astype(BF16)
        gout_ref[...] += dot(dp, grid)
        gxd_ref[...] += dot_nt(x, dp)
        yield True
        dgrid = dot_tn(dp, wout)
        ggain_ref[1:2, :] += jnp.sum(dgrid * unit, axis=0, keepdims=True)
        dc = norm_back(dgrid, gain3, unit, scale).astype(BF16)
        gm_ref[4] += dot_tn(h2, dc)
        yield True
        du = (dot_nt(dc, m6_ref[0]) * t).astype(BF16)
        gm_ref[3] += dot_tn(a2, du)
        yield True
        ddec = dot_nt(du, m5_ref[0]).astype(BF16)
        acc_ref[...] += dot(dt_ref[:, rows], ddec)
        yield True

    def grid_block(i, carry):
        part = BLOCK // PARTS
        in_turn(
            decode_part(pl.ds(pl.multiple_of(i * BLOCK + k * part, part), part)) for k in range(PARTS)
        )
        return carry

    lax.fori_loop(0, points // BLOCK, grid_block, 0)

    counts_ready(3)
    dmesh2 = acc_ref[...] * (1.0 / k_pick)
    ggain_ref[0:1, :] += jnp.sum(dmesh2 * unit2, axis=0, keepdims=True)
    dagg = norm_back(dmesh2, gain2, unit2, scale2).astype(BF16)
    gm_ref[2] += dot_tn(h_high, dagg)
    dhid = dot_nt(dagg, m4_ref[0]) * (1.0 / k_edge)
    dr = (dhid * t_sum).astype(BF16)
    gm_ref[1] += dot_tn(sent, dr)

    def edge_back(k, total):
        rows = pl.ds(pl.multiple_of(k * nodes, nodes), nodes)
        dpre = (dhid * t_ref[rows, :].astype(F32)).astype(BF16)
        return total + dot(eht_ref[:, rows], dpre)

    ds = lax.fori_loop(
        0, k_edge, edge_back, jnp.zeros((table, LATENT), F32), unroll=k_edge
    ).astype(BF16)
    gm_ref[0] += dot_tn(ext_ref[...], ds)
    dext = dot_nt(ds, m2_ref[0])
    dmesh_ref[0] = dmesh2 + dext[:nodes, :] + dot_nt(dr, m3_ref[0])
    dhalo_ref[0] = dext[nodes:, :].astype(BF16)

    @pl.when(member == pl.num_programs(0) - 1)
    def _():
        copy = pltpu.make_async_copy(gm_ref, slots_ref, out_sem)
        copy.start()
        copy.wait()


def main_scratch(k_edge, nodes, points, table):
    return [
        pltpu.VMEM((5, LATENT, LATENT), F32),
        pltpu.SemaphoreType.DMA,
        pltpu.SemaphoreType.DMA((4,)),
        pltpu.VMEM((k_edge * nodes, table), BF16),
        pltpu.VMEM((table, k_edge * nodes), BF16),
        pltpu.VMEM((points, nodes), BF16),
        pltpu.VMEM((nodes, points), BF16),
        pltpu.VMEM((table, LATENT), BF16),
        pltpu.VMEM((k_edge * nodes, LATENT), T_TYPE),
        pltpu.VMEM((nodes, LATENT), BF16),
        pltpu.VMEM((nodes, LATENT), F32),
        pltpu.VMEM((table, LATENT), BF16),
    ]


def whole(shape):
    return pl.BlockSpec(shape, lambda m: (0,) * len(shape))


def per_member(shape):
    return pl.BlockSpec((1,) + shape, lambda m: (m, 0, 0))


def call(kernel, members, in_specs, out_shapes, out_specs, scratch, cost, aliases=None):
    return pl.pallas_call(
        kernel,
        grid=(members,),
        in_specs=in_specs,
        out_shape=out_shapes,
        out_specs=out_specs,
        scratch_shapes=scratch,
        input_output_aliases=aliases or {},
        compiler_params=pltpu.CompilerParams(
            dimension_semantics=("arbitrary",), vmem_limit_bytes=VMEM_BYTES
        ),
        cost_estimate=pl.CostEstimate(flops=cost, bytes_accessed=32 << 20, transcendentals=0),
    )


def shape_of(shape, dtype):
    return jax.ShapeDtypeStruct(shape, dtype)


def slot_of(matrix):
    return 2 * matrix - 5 * ((matrix + 1) // 4)


def neighbours():
    region = lax.axis_index("region")
    slot = lax.rem(region, SLOTS)
    base = region - slot
    one = lax.rem(slot, 2)
    two = lax.rem(slot // 2, 2)
    four = slot // 4
    core = slot + 1 - 2 * one
    side = slot + 2 - 4 * two
    up = slot + 4 - 8 * four
    far = side + 4 - 8 * four
    return base, slot, core, side, up, far


def remote(source, target, send, receive, where):
    return pltpu.make_async_remote_copy(
        src_ref=source, dst_ref=target, send_sem=send, recv_sem=receive,
        device_id=where, device_id_type=MESH,
    )


def greet(places):
    barrier = pltpu.get_barrier_semaphore()
    for place in places:
        pl.semaphore_signal(barrier, inc=1, device_id=place, device_id_type=MESH)


def greeted(places):
    pl.semaphore_wait(pltpu.get_barrier_semaphore(), len(places))


def around():
    region, count = lax.axis_index("region"), lax.axis_size("region")
    following, previous = lax.rem(region + 1, count), lax.rem(region + count - 1, count)
    return {"region": following}, {"region": previous}


def encode_kernel(
    depth, day_ref, matrices_ref, in_ref, outp_ref, gains_ref, dates_ref, valid_ref, x_in, picks_ref,
    rows_ref, edge_ref, near_ref,
    full_ref, small_out_ref, total_ref, x4_out, a0_out, h1_out, t1_out, unit_out, scale_out, mesh_out,
    sent_out, left_ref, right_ref, eh_out, eht_out, d_out, dt_out,
    x_ref, edge_cols_ref, grid_cols_ref, eh_ref, eht_ref, d_ref, dt_ref, block_ref, pack_ref, pick_ref, out_ref, x4_ref, xl_ref, a0_ref, h1_ref, t1_ref, unit_ref, scale_ref,
    mesh_ref, sent_ref, buf_ref, w_ref, small_ref, count_ref, counts_ref, sums_ref, heard_ref,
    local_sem, z_send, z_recv, p_send, p_recv, d_send, d_recv, c_send, c_recv, n_send, n_recv,
    s_send, s_recv, w_sem, o_sem, e_send, e_recv, q_sem, b_sem, x_sem,
):
    base, slot, core, side, up, far = neighbours()
    z = lax.axis_index("row")
    half = block_ref.shape[1] // 2
    low, high = pl.ds(0, half), pl.ds(half, half)
    to_core, to_side, to_up = ({"region": base + place} for place in (core, side, up))
    to_next, to_previous = around()
    to_z = [None] + [{"row": lax.rem(z + d, depth)} for d in range(1, depth)]
    steps = range(1, depth)
    members, variables, points = x_in.shape
    nodes = a0_ref.shape[1]
    halo = left_ref.shape[1]
    peers = to_z[1:] + [to_core, to_side, to_up, to_next, to_previous]
    greet(peers)

    def at(d):
        return lax.rem(z + depth - d, depth)

    def arrived(target, receive):
        remote(target, target, receive, receive, to_core).wait_recv()

    def gone(origin, receive):
        remote(origin, origin, receive, receive, to_core).wait_send()

    x_copy = pltpu.make_async_copy(x_in, x_ref, x_sem)
    x_copy.start()

    for k in range(SLOTS - 1):
        block_ref[slot_of(k)] = matrices_ref[k].astype(BF16)
    pack_ref[...] = jnp.zeros_like(pack_ref)
    pack_ref[IN_ROW : IN_ROW + variables, :] = in_ref[...]
    pack_ref[OUT_ROW : OUT_ROW + variables, :] = outp_ref[...]
    pack_ref[GAIN_ROW : GAIN_ROW + gains_ref.shape[0], :] = gains_ref[...]
    pack_ref[DATE_ROW : DATE_ROW + dates_ref.shape[0], :] = dates_ref[...]
    block_ref[SMALL] = jnp.transpose(pack_ref[...]).astype(BF16)
    own = pltpu.make_async_copy(block_ref, full_ref.at[:, z], local_sem)
    own.start()
    table, k_edge, k_near = eht_ref.shape[0], edge_ref.shape[0], near_ref.shape[0]
    k_grid = picks_ref.shape[0]
    wide = 128
    pieces = nodes // wide
    edge_cols_ref[...] = columns_of(edge_ref[...])
    grid_cols_ref[...] = columns_of(picks_ref[...])

    def build_edges(i, carry):
        k, piece = i // pieces, lax.rem(i, pieces)
        inside = pl.ds(pl.multiple_of(piece * wide, wide), wide)
        across = pl.ds(pl.multiple_of(i * wide, wide), wide)
        columns = edge_cols_ref[inside, :].astype(F32)
        chosen = lax.broadcasted_iota(jnp.int32, columns.shape, 1) == k
        column = jnp.sum(jnp.where(chosen, columns, 0.0), axis=1, keepdims=True).astype(jnp.int32)
        eh_ref[across, :] = count_columns(column, table, 1)
        lines = edge_ref[:, inside].astype(F32)
        chosen = lax.broadcasted_iota(jnp.int32, lines.shape, 0) == k
        line = jnp.sum(jnp.where(chosen, lines, 0.0), axis=0, keepdims=True).astype(jnp.int32)
        eht_ref[:, across] = count_rows(line, table)
        return carry

    def build_near(i, carry):
        inside = pl.ds(pl.multiple_of(i * wide, wide), wide)
        near = near_ref[:, inside]
        d_ref[inside, :] = count_columns(columns_of(near), nodes, k_near)
        dt_ref[:, inside] = count_rows(near, nodes)
        return carry

    def build_grid(i, carry):
        inside = pl.ds(pl.multiple_of(i * 64, 64), 64)
        pick_ref[inside, :] = count_columns(grid_cols_ref[inside, :], points, k_grid)
        return carry

    valid = jnp.sum(valid_ref[...].astype(F32), axis=1, keepdims=True)
    valid = jnp.sum(valid, axis=0, keepdims=True)
    count_ref[...] = jnp.broadcast_to(valid, count_ref.shape)
    out_ref[...] = count_columns(columns_of(rows_ref[...]), nodes, 1)
    greeted(peers)
    for d in steps:
        remote(
            block_ref.at[slot], full_ref.at[slot, z], z_send.at[d], z_recv.at[d], to_z[d]
        ).start()
    for d in steps:
        remote(count_ref, counts_ref.at[d], n_send.at[d], n_recv.at[d], to_z[d]).start()

    lax.fori_loop(0, nodes // 64, build_grid, 0)
    edges, nears = k_edge * pieces, points // wide
    first = edges // 4
    share = -(-(edges - first) // (2 * depth - 2))

    def some_edges(i):
        return lax.fori_loop(
            first + i * share, jnp.minimum(first + (i + 1) * share, edges), build_edges, 0
        )

    lax.fori_loop(0, first, build_edges, 0)

    def from_z(d, carry):
        chunk = full_ref.at[slot, at(d)]
        arrived(chunk, z_recv.at[d])
        remote(chunk, chunk, p_send.at[0, d], p_recv.at[0, d], to_side).start()
        remote(chunk, chunk, p_send.at[1, d], p_recv.at[1, d], to_up).start()
        remote(chunk, chunk, c_send.at[0, d], c_recv.at[0, d], to_core).start()
        some_edges(d - 1)
        return carry

    lax.fori_loop(1, depth, from_z, 0)
    builds = [
        pltpu.make_async_copy(ref, target, b_sem.at[k])
        for k, (ref, target) in enumerate(
            ((eh_ref, eh_out), (eht_ref, eht_out), (d_ref, d_out), (dt_ref, dt_out))
        )
    ]

    total = count_ref[...]
    for d in steps:
        arrived(counts_ref.at[d], n_recv.at[d])
        total = total + counts_ref[d]
    sums_ref[0] = total
    partners = (to_core, to_side, to_up)

    def count_copy(step):
        return remote(
            sums_ref.at[step], heard_ref.at[step], s_send.at[step], s_recv.at[step], partners[step]
        )

    count_copy(0).start()

    def from_sides(d, carry):
        chunk = full_ref.at[side, at(d)]
        arrived(chunk, p_recv.at[0, d])
        part = full_ref.at[side, at(d), low]
        remote(part, part, d_send.at[0, d], d_recv.at[0, d], to_up).start()
        remote(chunk, chunk, c_send.at[1, d], c_recv.at[1, d], to_core).start()
        chunk = full_ref.at[up, at(d)]
        arrived(chunk, p_recv.at[1, d])
        part = full_ref.at[up, at(d), high]
        remote(part, part, d_send.at[1, d], d_recv.at[1, d], to_side).start()
        remote(chunk, chunk, c_send.at[2, d], c_recv.at[2, d], to_core).start()
        some_edges(depth - 2 + d)
        return carry

    lax.fori_loop(1, depth, from_sides, 0)
    builds[0].start()
    builds[1].start()

    def gather_inputs(m, carry):
        x4 = dot_nt(pick_ref[...], x_ref[m]) * (1.0 / k_grid)
        top, rest = split_two(x4)
        x4_ref[m] = top
        xl_ref[m] = rest
        return carry

    x_copy.wait()
    lax.fori_loop(0, members, gather_inputs, 0)
    for step in (1, 2):
        count_copy(step - 1).wait_recv()
        total = total + heard_ref[step - 1]
        sums_ref[step] = total
        count_copy(step).start()

    def from_far(d, carry):
        arrived(full_ref.at[far, at(d), low], d_recv.at[0, d])
        arrived(full_ref.at[far, at(d), high], d_recv.at[1, d])
        chunk = full_ref.at[far, at(d)]
        remote(chunk, chunk, c_send.at[3, d], c_recv.at[3, d], to_core).start()
        return carry

    lax.fori_loop(1, depth, from_far, 0)
    lax.fori_loop(0, nears, build_near, 0)
    builds[2].start()
    builds[3].start()
    count_copy(2).wait_recv()
    total_ref[...] = total + heard_ref[2]

    def from_core(d, carry):
        for k in range(4):
            arrived(full_ref.at[core, at(d)], c_recv.at[k, d])
        return carry

    lax.fori_loop(1, depth, from_core, 0)
    own.wait()

    loads = [
        pltpu.make_async_copy(full_ref.at[j], w_ref.at[k], w_sem.at[k])
        for k, j in enumerate((SMALL, slot_of(0), slot_of(1)))
    ]
    for copy in loads:
        copy.start()
    for copy in loads:
        copy.wait()
    small_ref[...] = jnp.transpose(w_ref[0].reshape(LATENT, LATENT))
    small_copy = pltpu.make_async_copy(small_ref, small_out_ref, q_sem)
    small_copy.start()
    kept = (
        (x4_ref, x4_out), (a0_ref, a0_out), (h1_ref, h1_out), (t1_ref, t1_out), (unit_ref, unit_out),
        (scale_ref, scale_out), (mesh_ref, mesh_out), (sent_ref, sent_out),
    )

    def kept_copies(m):
        return [
            pltpu.make_async_copy(ref.at[m], target.at[m], o_sem.at[k, m])
            for k, (ref, target) in enumerate(kept)
        ]

    def halo_copies(m):
        return [
            remote(buf_ref.at[m, halo:], left_ref.at[m], e_send.at[0, m], e_recv.at[0, m], to_next),
            remote(buf_ref.at[m, :halo], right_ref.at[m], e_send.at[1, m], e_recv.at[1, m], to_previous),
        ]

    def encode_member(m, carry):
        win = small_ref[IN_ROW : IN_ROW + variables, :]
        agg = dot(x4_ref[m], win) + dot(xl_ref[m], win) + date_row(small_ref, day_ref[m])
        a0 = agg.astype(BF16)
        hid, t1 = silu_parts(0.5 * dot(a0, w_ref[1].reshape(LATENT, LATENT)))
        h1 = hid.astype(BF16)
        unit, scale = normalise(dot(h1, w_ref[2].reshape(LATENT, LATENT)))
        mesh = agg + unit * gain_row(small_ref, 0)
        low_mesh = mesh.astype(BF16)
        buf_ref[m] = dot(out_ref[...], low_mesh).astype(BF16)
        for copy in halo_copies(m):
            copy.start()
        a0_ref[m] = a0
        h1_ref[m] = h1
        t1_ref[m] = t1.astype(BF16)
        unit_ref[m] = unit
        scale_ref[m] = scale
        mesh_ref[m] = mesh
        sent_ref[m] = low_mesh
        for copy in kept_copies(m):
            copy.start()
        return carry

    lax.fori_loop(0, members, encode_member, 0)

    def finish_member(m, carry):
        for copy in halo_copies(m) + kept_copies(m):
            copy.wait()
        return carry

    def finish_row(d, carry):
        gone(block_ref.at[slot], z_send.at[d])
        gone(count_ref, n_send.at[d])
        chunk = full_ref.at[slot, at(d)]
        for k in range(2):
            gone(chunk, p_send.at[k, d])
            gone(full_ref.at[slot, at(d), low], d_send.at[k, d])
        for k in range(4):
            gone(chunk, c_send.at[k, d])
        return carry

    lax.fori_loop(0, members, finish_member, 0)
    lax.fori_loop(1, depth, finish_row, 0)
    for step in range(3):
        count_copy(step).wait_send()
    for copy in builds:
        copy.wait()
    small_copy.wait()


def encode(
    day, matrices, in_proj, out_proj, gains, dates, valid, inputs, picks, rows, edges, near, depth
):
    hbm = pl.BlockSpec(memory_space=pl.ANY)
    vmem = pl.BlockSpec(memory_space=pltpu.VMEM)
    dma = pltpu.SemaphoreType.DMA
    members, variables, points = inputs.shape
    nodes = picks.shape[1]
    halo = rows.shape[1] // 2
    share = matrices.shape[1]
    nodes_of = (members, nodes, LATENT)
    table, pairs = nodes + 2 * halo, edges.shape[0] * nodes
    counts = ((pairs, table), (table, pairs), (points, nodes), (nodes, points))
    kept = [
        ((members, nodes, variables), BF16),
        (nodes_of, BF16),
        (nodes_of, BF16),
        (nodes_of, BF16),
        (nodes_of, F32),
        ((members, nodes, 1), F32),
        (nodes_of, F32),
        (nodes_of, BF16),
    ]
    return pl.pallas_call(
        partial(encode_kernel, depth),
        in_specs=[pl.BlockSpec(memory_space=pltpu.SMEM)] + [vmem] * 6 + [hbm] + [vmem] * 4,
        out_shape=[
            shape_of((SLOTS, depth, share, LATENT), BF16),
            shape_of((LATENT, LATENT), BF16),
            shape_of((8, 128), F32),
            *(shape_of(*one) for one in kept),
            shape_of((members, halo, LATENT), BF16),
            shape_of((members, halo, LATENT), BF16),
            *(shape_of(one, BF16) for one in counts),
        ],
        out_specs=[hbm, hbm, vmem] + [hbm] * (len(kept) + 2 + len(counts)),
        scratch_shapes=[
            pltpu.VMEM(inputs.shape, BF16),
            pltpu.VMEM((nodes, 8), jnp.int32),
            pltpu.VMEM((nodes, 8), jnp.int32),
            *(pltpu.VMEM(one, BF16) for one in counts),
            pltpu.VMEM((SLOTS, share, LATENT), BF16),
            pltpu.VMEM((LATENT, share), F32),
            pltpu.VMEM((nodes, points), BF16),
            pltpu.VMEM((2 * halo, nodes), BF16),
            pltpu.VMEM(*kept[0]),
            *(pltpu.VMEM(*one) for one in kept),
            pltpu.VMEM((members, 2 * halo, LATENT), BF16),
            pltpu.VMEM((3, depth, share, LATENT), BF16),
            pltpu.VMEM((LATENT, LATENT), BF16),
            pltpu.VMEM((8, 128), F32),
            pltpu.VMEM((depth, 8, 128), F32),
            pltpu.VMEM((3, 8, 128), F32),
            pltpu.VMEM((3, 8, 128), F32),
            dma,
            dma((depth,)),
            dma((depth,)),
            dma((2, depth)),
            dma((2, depth)),
            dma((2, depth)),
            dma((2, depth)),
            dma((4, depth)),
            dma((4, depth)),
            dma((depth,)),
            dma((depth,)),
            dma((3,)),
            dma((3,)),
            dma((3,)),
            dma((len(kept), members)),
            dma((2, members)),
            dma((2, members)),
            dma,
            dma((len(counts),)),
            dma,
        ],
        compiler_params=pltpu.CompilerParams(
            collective_id=0, has_side_effects=True, vmem_limit_bytes=VMEM_BYTES
        ),
    )(
        day, matrices, in_proj, out_proj, gains, dates, valid, inputs, picks, rows, edges, near
    )


def reduce_kernel(
    depth, day_ref, late_ref, momentum_in, count_ref, dmesh_in, dhalo_ref, rows_ref, x4_in, a0_in,
    h1_in, t1_in, unit_in, scale_in, weights_ref, small_ref, gxd_ref, dsum_ref, gout_ref, ggain_ref,
    loss_ref,
    g_ref, x_ref,
    momentum_ref, dmesh_ref, ret_ref, x4_ref, a0_ref, h1_ref, t1_ref, unit_ref, scale_ref, m_ref, back_ref, pack_ref,
    early_ref, own_ref, heard_ref, snd_ref, rcv_ref, snd_low_ref, rcv_low_ref, acc_ref, zr_ref,
    g_own_ref, mb_ref, x_own_ref,
    i_sem, e_send, e_recv, l_sem, h_send, h_recv, p_send, p_recv, q_send, q_recv, z_send, z_recv,
    m_send, m_recv, g_local, g_send, g_recv, x_local, x_send, x_recv,
):
    base, slot, core, side, up, far = neighbours()
    z = lax.axis_index("row")
    rows = acc_ref.shape[0] // depth
    chips = SLOTS // 2
    mine = slot // 2
    parity = lax.rem(slot, 2)
    members, variables = x4_ref.shape[0], x4_ref.shape[2]
    halo = dhalo_ref.shape[1] // 2
    to_core, to_side, to_up, to_far = ({"region": base + place} for place in (core, side, up, far))
    to_next, to_previous = around()
    to_place = (to_far, to_side, to_up)
    places = (far, side, up)
    to_z = [None] + [{"row": lax.rem(z + d, depth)} for d in range(1, depth)]
    peers = to_z[1:] + [to_core, to_side, to_up, to_far, to_next, to_previous]
    greet(peers)
    sent = []

    def both_ends(i):
        return lax.rem(i * (depth - 1), depth)

    def part_of(b):
        return pl.ds(pl.multiple_of(b * rows, rows), rows)

    def send(*args):
        copy = remote(*args)
        copy.start()
        sent.append(copy)

    def arrived(target, receive):
        remote(target, target, receive, receive, to_core).wait_recv()

    def load(*args):
        copy = pltpu.make_async_copy(*args)
        copy.start()
        return copy

    def halo_copies(m):
        return [
            remote(dhalo_ref.at[m, halo:], ret_ref.at[m, :halo], e_send.at[0, m], e_recv.at[0, m], to_next),
            remote(
                dhalo_ref.at[m, :halo], ret_ref.at[m, halo:], e_send.at[1, m], e_recv.at[1, m], to_previous
            ),
        ]

    inner = ((dmesh_in, dmesh_ref), (x4_in, x4_ref), (a0_in, a0_ref), (h1_in, h1_ref), (t1_in, t1_ref),
             (unit_in, unit_ref), (scale_in, scale_ref))

    def inner_loads(m):
        return [
            pltpu.make_async_copy(ref.at[m], target.at[m], i_sem.at[k, m])
            for k, (ref, target) in enumerate(inner)
        ]

    for m in range(members):
        for copy in inner_loads(m):
            copy.start()
    m_loads = [
        load(momentum_in.at[mine + (SLOTS // 2 - 1) * parity], momentum_ref, i_sem.at[len(inner) + 1, 0])
    ]
    first = load(late_ref.at[0], early_ref.at[2], i_sem.at[len(inner), 0])
    for k in range(2):
        m_loads.append(load(weights_ref.at[slot_of(k)], m_ref.at[k], i_sem.at[len(inner), 1 + k]))

    def late_copy(chip):
        return remote(
            late_ref.at[1 + chip], heard_ref.at[chip], h_send.at[chip, 0], h_recv.at[chip, 0], to_core
        )

    def late_load(chip):
        return pltpu.make_async_copy(late_ref.at[1 + chip], own_ref.at[chip], l_sem.at[chip])

    def early_copy(chip, b):
        return remote(
            early_ref.at[chip, part_of(b)], heard_ref.at[chip, part_of(b)], h_send.at[chip, b],
            h_recv.at[chip, b], to_core,
        )

    def low_copy(b):
        return remote(
            snd_low_ref.at[part_of(b)], rcv_low_ref.at[mine, part_of(b)], q_send.at[b], q_recv.at[mine, b],
            {"region": base + SMALL},
        )

    def chip_copy(chip, b):
        return remote(
            snd_ref.at[chip, part_of(b)], rcv_ref.at[mine, part_of(b)], p_send.at[chip, b],
            p_recv.at[mine, b], {"region": base + 2 * chip + parity},
        )

    def pass_on(chip, b, own):
        part = part_of(b)
        total = own[chip, part, :] + heard_ref[chip, part, :]

        @pl.when(mine == chip)
        def _():
            acc_ref[part, :] = total

        @pl.when(mine != chip)
        def _():
            snd_ref[chip, part, :] = total.astype(BF16)
            chip_copy(chip, b).start()

    def pass_late(chip):
        @pl.when(parity == 1)
        def _():
            late_load(chip).wait()
            late_copy(chip).wait_recv()

            def piece(b, carry):
                pass_on(chip, b, own_ref)
                return carry

            lax.fori_loop(0, depth, piece, 0)

    def pass_early(i, carry):
        b = both_ends(i)

        @pl.when(parity == 0)
        def _():
            def piece(chip, carry):
                early_copy(chip, b).wait_recv()
                pass_on(chip, b, early_ref)
                return carry

            lax.fori_loop(0, chips, piece, 0)

        return carry

    def pass_low(b, carry):
        part = part_of(b)
        total = early_ref[SMALL // 2, part, :] + heard_ref[SMALL // 2, part, :]
        snd_low_ref[part, :] = (total - total.astype(BF16).astype(F32)).astype(BF16)
        low_copy(b).start()
        return carry

    @pl.when(parity == 1)
    def _():
        for chip in range(chips):
            late_load(chip).start()

    lines = lax.broadcasted_iota(jnp.int32, (16, LATENT), 0)
    back_ref[...] = count_rows(rows_ref[...], back_ref.shape[0])
    wout = small_ref[OUT_ROW : OUT_ROW + variables, :]
    pack_ref[...] = jnp.zeros_like(pack_ref)
    top, rest = split_two(gxd_ref[...])
    pack_ref[IN_ROW : IN_ROW + variables, :] = dot(top, wout) + dot(rest, wout)
    pack_ref[OUT_ROW : OUT_ROW + variables, :] = gout_ref[...]
    pack_ref[GAIN_ROW + 1 : GAIN_ROW + 3, :] = ggain_ref[...]
    loss = jnp.sum(loss_ref[...], axis=0, keepdims=True)
    pack_ref[LOSS_ROW : LOSS_ROW + 1, :] = jnp.broadcast_to(loss, (1, LATENT))
    early_ref[0:2] = jnp.zeros((2, LATENT, LATENT), F32)
    greeted(peers)
    for m in range(members):
        for copy in halo_copies(m):
            copy.start()

    @pl.when(parity == 0)
    def _():
        for chip in range(chips):
            late_copy(chip).start()

    for copy in m_loads:
        copy.wait()

    def member_back(m, carry):
        for copy in inner_loads(m):
            copy.wait()
        for copy in halo_copies(m):
            copy.wait()
        dmesh = dmesh_ref[m] + dot(back_ref[...], ret_ref[m])
        unit = unit_ref[m]
        pack_ref[GAIN_ROW : GAIN_ROW + 1, :] += jnp.sum(dmesh * unit, axis=0, keepdims=True)
        dc = norm_back(dmesh, gain_row(small_ref, 0), unit, scale_ref[m]).astype(BF16)
        early_ref[1] += dot_tn(h1_ref[m], dc)
        du = (dot_nt(dc, m_ref[1]) * t1_ref[m].astype(F32)).astype(BF16)
        early_ref[0] += dot_tn(a0_ref[m], du)
        dagg = dmesh + dot_nt(du, m_ref[0])
        pack_ref[IN_ROW : IN_ROW + variables, :] += dot_tn(x4_ref[m], dagg.astype(BF16))
        top, rest = split_two(dsum_ref[m])
        date = jnp.sum(dagg, axis=0, keepdims=True) + dot_tn(top, wout) + dot_tn(rest, wout)
        pack_ref[DATE_ROW : DATE_ROW + 16, :] += jnp.where(lines == day_ref[m], date, 0.0)

        @pl.when(m < chips)
        def _():
            pass_late(m)

        return carry

    lax.fori_loop(0, members, member_back, 0)
    for chip in range(members, chips):
        pass_late(chip)
    early_ref[SMALL // 2] = jnp.transpose(pack_ref[...])
    first.wait()

    @pl.when(parity == 1)
    def _():
        for i in range(depth):
            for chip in range(chips):
                early_copy(chip, i * (depth - 1) % depth).start()

    lax.fori_loop(0, depth, pass_early, 0)

    @pl.when((mine != SMALL // 2) & (parity == 0))
    def _():
        lax.fori_loop(0, depth, pass_low, 0)

    sources = [lax.rem(mine + i, chips) for i in range(1, chips)]
    def z_copy(b):
        d = lax.rem(b - z + depth, depth)
        return remote(acc_ref.at[part_of(b)], zr_ref.at[d], z_send.at[b], z_recv.at[d], {"row": b + 0 * z})

    def across_z(i, carry):
        b = both_ends(i)
        part = part_of(b)
        total = acc_ref[part, :]
        for c in sources:
            arrived(rcv_ref.at[c, part], p_recv.at[c, b])
            total = total + rcv_ref[c, part, :].astype(F32)
        acc_ref[part, :] = total

        @pl.when(slot == SMALL)
        def _():
            low = acc_ref[part, :]
            for c in sources:
                arrived(rcv_low_ref.at[c, part], q_recv.at[c, b])
                low = low + rcv_low_ref[c, part, :].astype(F32)
            acc_ref[part, :] = low

        @pl.when(z != b)
        def _():
            z_copy(b).start()

        return carry

    lax.fori_loop(0, depth, across_z, 0)
    zr_ref[0] = acc_ref[pl.ds(pl.multiple_of(z * rows, rows), rows), :]
    for d in range(1, depth):
        arrived(zr_ref.at[d], z_recv.at[d])
    g_own = zr_ref[z]
    for place in range(1, depth):
        g_own = g_own + zr_ref[lax.rem(z + depth - place, depth)]
    g_own_ref[...] = g_own
    momentum = (
        MUON_MOMENTUM * momentum_ref[...]
        + (2.0 / count_ref[0:1, 0:1]) * g_own
    )
    mb_ref[0] = momentum.astype(BF16)
    for d in range(1, depth):
        send(mb_ref.at[0], mb_ref.at[d], m_send.at[d], m_recv.at[d], to_z[d])
    g_copy = load(g_own_ref, g_ref.at[slot], g_local)
    for k in range(3):
        send(g_own_ref, g_ref.at[slot], g_send.at[k], g_recv.at[k], to_place[k])
    send(g_own_ref, g_ref.at[slot], g_send.at[3], g_recv.at[3], to_core)

    for d in range(1, depth):
        arrived(mb_ref.at[d], m_recv.at[d])
    everything = jnp.concatenate([mb_ref[d] for d in range(depth)], axis=0)
    wide = everything.astype(F32)
    squares = jnp.sum(jnp.sum(wide * wide, axis=1, keepdims=True), axis=0, keepdims=True)
    inverse = lax.rsqrt(squares + 1e-07)
    turn = momentum * inverse
    current = (wide * inverse).astype(BF16)
    turn_low = turn.astype(BF16)
    for sweep in range(NS_ITERS):
        gram = dot_tn(current, current)
        gram_low = gram.astype(BF16)
        mixing = NS_COEFFS[1] * gram + NS_COEFFS[2] * dot(gram_low, gram_low)
        mixing = mixing.astype(BF16)
        turn = NS_COEFFS[0] * turn + dot(turn_low, mixing)
        turn_low = turn.astype(BF16)
        if sweep < NS_ITERS - 1:
            current = (NS_COEFFS[0] * current.astype(F32) + dot(current, mixing)).astype(BF16)
    x_own_ref[...] = turn_low
    x_copy = pltpu.make_async_copy(x_own_ref, x_ref.at[slot], x_local)
    x_copy.start()
    for k in range(3):
        send(x_own_ref, x_ref.at[slot], x_send.at[k], x_recv.at[k], to_place[k])
    send(x_own_ref, x_ref.at[slot], x_send.at[3], x_recv.at[3], to_core)

    for target, send_sem, recv_sem in ((g_ref, g_send, g_recv), (x_ref, x_send, x_recv)):
        for k in range(3):
            chunk = target.at[places[k]]
            arrived(chunk, recv_sem.at[k])
            send(chunk, chunk, send_sem.at[4 + k], recv_sem.at[4 + k], to_core)
    for target, recv_sem in ((g_ref, g_recv), (x_ref, x_recv)):
        for k in range(3, 7):
            arrived(target.at[core], recv_sem.at[k])
    for copy in sent:
        copy.wait_send()
    @pl.when(parity == 0)
    def _():
        for chip in range(chips):
            late_copy(chip).wait_send()

    @pl.when(parity == 1)
    def _():
        for b in range(depth):
            for chip in range(chips):
                early_copy(chip, b).wait_send()

    for b in range(depth):
        for chip in range(chips):

            @pl.when(mine != chip)
            def _():
                chip_copy(chip, b).wait_send()

        @pl.when((mine != SMALL // 2) & (parity == 0))
        def _():
            low_copy(b).wait_send()

        @pl.when(z != b)
        def _():
            z_copy(b).wait_send()

    g_copy.wait()
    x_copy.wait()


def reduce_gradients(
    day, late, momentum, count, dmesh, dhalo, rows, kept, weights, small, gxd, dsum, gout, ggain, loss,
    depth,
):
    hbm = pl.BlockSpec(memory_space=pl.ANY)
    vmem = pl.BlockSpec(memory_space=pltpu.VMEM)
    dma = pltpu.SemaphoreType.DMA
    members, nodes, width = dmesh.shape
    height = LATENT
    share = height // depth
    halo = dhalo.shape[1]
    chips = SLOTS // 2

    return pl.pallas_call(
        partial(reduce_kernel, depth),
        in_specs=[pl.BlockSpec(memory_space=pltpu.SMEM), hbm, hbm, vmem, hbm, vmem, vmem]
        + [hbm] * len(kept)
        + [hbm]
        + [vmem] * 6,
        out_shape=[
            shape_of((SLOTS, share, width), F32),
            shape_of((SLOTS, share, width), BF16),
        ],
        out_specs=[hbm, hbm],
        scratch_shapes=[
            pltpu.VMEM((share, width), F32),
            pltpu.VMEM(dmesh.shape, F32),
            pltpu.VMEM(dhalo.shape, BF16),
            *(pltpu.VMEM(one.shape, one.dtype) for one in kept),
            pltpu.VMEM((2, height, width), BF16),
            pltpu.VMEM((nodes, halo), BF16),
            pltpu.VMEM((height, width), F32),
            pltpu.VMEM((4, height, width), F32),
            pltpu.VMEM((chips, height, width), F32),
            pltpu.VMEM((chips, height, width), F32),
            pltpu.VMEM((chips, height, width), BF16),
            pltpu.VMEM((chips, height, width), BF16),
            pltpu.VMEM((height, width), BF16),
            pltpu.VMEM((chips, height, width), BF16),
            pltpu.VMEM((height, width), F32),
            pltpu.VMEM((depth, share, width), F32),
            pltpu.VMEM((share, width), F32),
            pltpu.VMEM((depth, share, width), BF16),
            pltpu.VMEM((share, width), BF16),
            dma((len(kept) + 3, members)),
            dma((2, members)),
            dma((2, members)),
            dma((chips,)),
            dma((chips, depth)),
            dma((chips, depth)),
            dma((chips, depth)),
            dma((chips, depth)),
            dma((depth,)),
            dma((chips, depth)),
            dma((depth,)),
            dma((depth,)),
            dma((depth,)),
            dma((depth,)),
            dma,
            dma((7,)),
            dma((7,)),
            dma,
            dma((7,)),
            dma((7,)),
        ],
        compiler_params=pltpu.CompilerParams(
            collective_id=1, has_side_effects=True, vmem_limit_bytes=VMEM_BYTES
        ),
    )(
        day, late, momentum, count, dmesh, dhalo, rows, *kept, weights, small, gxd, dsum, gout,
        ggain, loss,
    )


def turn_whole(sums, count, momentum):
    blocks = jnp.stack([sums[slot_of(k)] for k in range(SLOTS - 1)])
    blocks = MUON_MOMENTUM * momentum + (2.0 / count[0, 0]) * blocks
    squares = lax.psum(jnp.sum(blocks * blocks, axis=(1, 2)), "row")
    current = blocks * lax.rsqrt(squares + 1e-07)[:, None, None]

    def product(expression, left, right):
        return jnp.einsum(expression, left, right, precision=lax.Precision.HIGHEST)

    for _ in range(NS_ITERS):
        gram = lax.psum(product("mrk,mrl->mkl", current, current), "row")
        mixing = NS_COEFFS[1] * gram + NS_COEFFS[2] * product("mkj,mjl->mkl", gram, gram)
        current = NS_COEFFS[0] * current + product("mrk,mkl->mrl", current, mixing)
    current = current.astype(BF16)
    by_slot = {slot_of(k): current[k] for k in range(SLOTS - 1)}
    return jnp.stack([by_slot.get(k, current[0]) for k in range(SLOTS)])


def finish_kernel(
    g_ref, rest_ref, x_ref, count_ref, matrix_ref, momentum_ref,
    in_ref, in1_ref, in2_ref, out_ref, out1_ref, out2_ref, gain_ref, gain1_ref, gain2_ref,
    date_ref, date1_ref, date2_ref,
    new_matrix_ref, new_momentum_ref,
    nin_ref, nin1_ref, nin2_ref, nout_ref, nout1_ref, nout2_ref, ngain_ref, ngain1_ref, ngain2_ref,
    ndate_ref, ndate1_ref, ndate2_ref, loss_ref, valid_ref,
):
    scale = 2.0 / count_ref[0:1, 0:1]
    new_momentum_ref[...] = MUON_MOMENTUM * momentum_ref[...] + scale * g_ref[...]
    new_matrix_ref[...] = (
        matrix_ref[...] * (1.0 - MUON_RATE * WEIGHT_DECAY) - MUON_RATE * x_ref[...].astype(F32)
    )

    @pl.when(pl.program_id(0) == 0)
    def _():
        rest = jnp.transpose(rest_ref[0])
        loss_ref[0, 0] = jnp.sum(rest[LOSS_ROW : LOSS_ROW + 1, 0:1])
        valid_ref[0, 0] = jnp.sum(count_ref[0:1, 0:1])
        rest = rest * scale
        for row, rate, decay, old, new in (
            (IN_ROW, MATRIX_RATE, WEIGHT_DECAY, (in_ref, in1_ref, in2_ref), (nin_ref, nin1_ref, nin2_ref)),
            (OUT_ROW, MATRIX_RATE, WEIGHT_DECAY, (out_ref, out1_ref, out2_ref),
             (nout_ref, nout1_ref, nout2_ref)),
            (GAIN_ROW, VECTOR_RATE, 0.0, (gain_ref, gain1_ref, gain2_ref),
             (ngain_ref, ngain1_ref, ngain2_ref)),
            (DATE_ROW, VECTOR_RATE, 0.0, (date_ref, date1_ref, date2_ref),
             (ndate_ref, ndate1_ref, ndate2_ref)),
        ):
            weight, first, second = (ref[...] for ref in old)
            gradient = rest[row : row + weight.shape[0], :]
            for ref, value in zip(new, adam_update(weight, gradient, first, second, rate, decay)):
                ref[...] = value


def finish(sums, turned, count, matrices, momentum, vectors):
    share, width = sums.shape[1:]

    def slot_block():
        return pl.BlockSpec((1, share, width), lambda m: (slot_of(m), 0, 0))

    one = pl.BlockSpec((1, share, width), lambda m: (m, 0, 0))
    return pl.pallas_call(
        finish_kernel,
        grid=(matrices.shape[0],),
        in_specs=[
            slot_block(), pl.BlockSpec((1, share, width), lambda m: (SMALL, 0, 0)), slot_block(),
            whole(count.shape), one, one, *(whole(v.shape) for v in vectors),
        ],
        out_shape=[shape_of(matrices.shape, F32)] * 2
        + [shape_of(v.shape, F32) for v in vectors]
        + [shape_of((1, 1), F32)] * 2,
        out_specs=[one, one] + [whole(v.shape) for v in vectors]
        + [pl.BlockSpec(memory_space=pltpu.SMEM)] * 2,
        compiler_params=pltpu.CompilerParams(
            dimension_semantics=("arbitrary",), vmem_limit_bytes=VMEM_BYTES
        ),
    )(sums, sums, turned, count, matrices, momentum, *vectors)


def adam_update(weight, gradient, first_moment, second_moment, step_rate, decay_rate):
    first_new = BETA_ONE * first_moment + (1.0 - BETA_ONE) * gradient
    second_new = BETA_TWO * second_moment + (1.0 - BETA_TWO) * gradient * gradient
    unbiased_one = first_new / (1.0 - BETA_ONE**STEP)
    unbiased_two = second_new / (1.0 - BETA_TWO**STEP)
    weight_new = weight * (1.0 - step_rate * decay_rate) - step_rate * unbiased_one / (
        jnp.sqrt(unbiased_two) + 1e-08
    )
    return (weight_new, first_new, second_new)


def body(
    inputs,
    targets,
    valid_steps,
    var_weights,
    grid_to_mesh,
    mesh_edges,
    send_rows,
    mesh_to_grid,
    date_index,
    matrices,
    matrices_momentum,
    in_proj,
    in_first,
    in_second,
    out_proj,
    out_first,
    out_second,
    norm_gains,
    gains_first,
    gains_second,
    date_table,
    date_first,
    date_second,
):
    inputs = jnp.swapaxes(inputs, 1, 2)
    targets = jnp.swapaxes(targets, 1, 2)
    members, variables, points = inputs.shape
    nodes = grid_to_mesh.shape[0]
    halo = send_rows.shape[0] // 2
    table = nodes + 2 * halo
    k_edge = mesh_edges.shape[1]
    k_pick = mesh_to_grid.shape[1]
    dates = date_table.shape[0]

    depth = lax.axis_size("row")
    regions = lax.axis_size("region")
    groups = [[g * SLOTS + q for g in range(regions // SLOTS)] for q in range(SLOTS)]
    scalars = pl.BlockSpec(memory_space=pltpu.SMEM)
    hbm = pl.BlockSpec(memory_space=pl.ANY)
    gathered, small, count, *kept, left, right, eh, eht, d, dt = encode(
        date_index, matrices, in_proj, out_proj.T, norm_gains, date_table, valid_steps, inputs,
        grid_to_mesh.T, send_rows[None, :], mesh_edges.T, mesh_to_grid.T, depth,
    )
    mesh1, sent = kept[6:]
    if regions > SLOTS:
        count = lax.psum(count, "region", axis_index_groups=groups)
    weights = gathered.reshape(SLOTS, LATENT, LATENT)
    node_block = per_member((nodes, LATENT))

    def matrix(j):
        place = slot_of(j)
        return pl.BlockSpec(
            (1, LATENT, LATENT), lambda m: (place, 0, 0), pipeline_mode=pl.Buffered(1)
        )

    out_shape = (variables, LATENT)
    late, gout, gxd, dsum, ggain_late, loss_row, dmesh, dhalo = call(
        partial(main_kernel, k_pick),
        members,
        [
            scalars,
            node_block,
            node_block,
            per_member((halo, LATENT)),
            per_member((halo, LATENT)),
            per_member((variables, points)),
            per_member((variables, points)),
            whole((members, points)),
            whole((1, variables)),
            hbm,
            hbm,
            hbm,
            hbm,
            whole((LATENT, LATENT)),
            matrix(2),
            matrix(3),
            matrix(4),
            matrix(5),
            matrix(6),
        ],
        [
            shape_of((5, LATENT, LATENT), F32),
            shape_of(out_shape, F32),
            shape_of((variables, variables), F32),
            shape_of((members, variables, 1), F32),
            shape_of((2, LATENT), F32),
            shape_of((variables, 1), F32),
            shape_of((members, nodes, LATENT), F32),
            shape_of((members, 2 * halo, LATENT), BF16),
        ],
        [
            hbm,
            whole(out_shape),
            whole((variables, variables)),
            per_member((variables, 1)),
            whole((2, LATENT)),
            whole((variables, 1)),
            node_block,
            per_member((2 * halo, LATENT)),
        ],
        main_scratch(k_edge, nodes, points, table),
        60_000_000_000,
    )(
        date_index,
        mesh1,
        sent,
        left,
        right,
        inputs,
        targets,
        valid_steps,
        var_weights[None, :],
        eh,
        eht,
        d,
        dt,
        small,
        weights,
        weights,
        weights,
        weights,
        weights,
    )

    sums, turned = reduce_gradients(
        date_index, late, matrices_momentum, count, dmesh, dhalo, send_rows[None, :], kept[:6], weights,
        small, gxd, dsum, gout, ggain_late, loss_row, depth,
    )
    if regions > SLOTS:
        sums = lax.psum(sums, "region", axis_index_groups=groups)
        turned = turn_whole(sums, count, matrices_momentum)
    vectors = (
        in_proj, in_first, in_second, out_proj.T, out_first.T, out_second.T,
        norm_gains, gains_first, gains_second, date_table, date_first, date_second,
    )
    new = finish(sums, turned, count, matrices, matrices_momentum, vectors)
    return (
        *new[:5],
        *(part.T for part in new[5:8]),
        *new[8:14],
        new[14].reshape(()),
        new[15].reshape(()),
    )


def solution(mesh):
    in_specs = (
        P("row", "region", None),
        P("row", "region", None),
        P("row", "region"),
        P(),
        P("region", None),
        P("region", None),
        P("region"),
        P("region", None),
        P("row"),
        P(None, "row", None),
        P(None, "row", None),
        P(None, "row"),
        P(None, "row"),
        P(None, "row"),
        P("row", None),
        P("row", None),
        P("row", None),
        P(None, "row"),
        P(None, "row"),
        P(None, "row"),
        P(None, "row"),
        P(None, "row"),
        P(None, "row"),
    )
    out_specs = (
        P(None, "row", None),
        P(None, "row", None),
        P(None, "row"),
        P(None, "row"),
        P(None, "row"),
        P("row", None),
        P("row", None),
        P("row", None),
        P(None, "row"),
        P(None, "row"),
        P(None, "row"),
        P(None, "row"),
        P(None, "row"),
        P(None, "row"),
        P(),
        P(),
    )
    return jax.shard_map(body, mesh=mesh, in_specs=in_specs, out_specs=out_specs, check_vma=False)
```

```python
from functools import partial

import jax
import jax.numpy as jnp
from jax import lax
from jax.experimental import pallas as pl
from jax.experimental.pallas import tpu as pltpu
from jax.sharding import PartitionSpec as P

NS_ITERS = 2
STEP = 10
NS_COEFFS = (3.4445, -4.775, 2.0315)
MUON_RATE = 0.8
MUON_MOMENTUM = 0.95
MATRIX_RATE = 0.05
VECTOR_RATE = 0.2
BETA_ONE = 0.9
BETA_TWO = 0.95
WEIGHT_DECAY = 0.01

F32 = jnp.float32
BF16 = jnp.bfloat16
LATENT = 512
BLOCK = 1024
PARTS = 1
T_TYPE = BF16
VMEM_BYTES = 60 * 1024 * 1024
MESH = pl.DeviceIdType.MESH
SLOTS = 8
SMALL = 6
IN_ROW, OUT_ROW, GAIN_ROW, DATE_ROW, LOSS_ROW = 0, 240, 480, 496, 504


def dot(left, right):
    return jnp.dot(left, right, preferred_element_type=F32)


def dot_nt(left, right):
    return lax.dot_general(left, right, (((1,), (1,)), ((), ())), preferred_element_type=F32)


def dot_tn(left, right):
    return lax.dot_general(left, right, (((0,), (0,)), ((), ())), preferred_element_type=F32)


def split_two(values):
    high = values.astype(BF16)
    return high, (values - high.astype(F32)).astype(BF16)


def silu_parts(half):
    bend = jnp.tanh(half)
    gate = 0.5 * bend + 0.5
    hid = half * bend + half
    return hid, gate + hid * (1.0 - gate)


def normalise(values):
    centred = values - jnp.mean(values, axis=-1, keepdims=True)
    spread = jnp.mean(centred * centred, axis=-1, keepdims=True)
    scale = lax.rsqrt(spread + 1e-05)
    return centred * scale, scale


def norm_back(grad, gain, unit, scale):
    scaled = gain * grad
    mean_one = jnp.mean(scaled, axis=-1, keepdims=True)
    mean_two = jnp.mean(scaled * unit, axis=-1, keepdims=True)
    return scale * (scaled - mean_one - unit * mean_two)


def in_turn(parts):
    parts = list(parts)
    while parts:
        parts = [part for part in parts if next(part, None) is not None]


def count_columns(index, width, count):
    lanes = lax.broadcasted_iota(jnp.int32, (index.shape[0], width), 1)
    total = None
    for k in range(count):
        one = jnp.where(lanes == index[:, k : k + 1], 1.0, 0.0)
        total = one if total is None else total + one
    return total.astype(BF16)


def gain_row(small_ref, k):
    return small_ref[GAIN_ROW : GAIN_ROW + 16, :].astype(F32)[k : k + 1, :]


def date_row(small_ref, day):
    table = small_ref[DATE_ROW : DATE_ROW + 16, :].astype(F32)
    lines = lax.broadcasted_iota(jnp.int32, table.shape, 0)
    return jnp.sum(jnp.where(lines == day, table, 0.0), axis=0, keepdims=True)


def columns_of(index):
    short = 8 - index.shape[0]
    if short > 0:
        index = jnp.concatenate([index, jnp.zeros((short, index.shape[1]), index.dtype)], axis=0)
    return jnp.transpose(index)


def count_rows(index, height):
    lines = lax.broadcasted_iota(jnp.int32, (height, index.shape[1]), 0)
    total = None
    for k in range(index.shape[0]):
        one = jnp.where(lines == index[k : k + 1, :], 1.0, 0.0)
        total = one if total is None else total + one
    return total.astype(BF16)


def main_kernel(
    k_pick, day_ref, mesh_ref, sent_ref, left_ref, right_ref, x_ref, y_ref, valid_ref, varw_ref,
    eh_in, eht_in, d_in, dt_in, small_ref, m2_ref, m3_ref, m4_ref, m5_ref, m6_ref,
    slots_ref, gout_ref, gxd_ref, dsum_ref, ggain_ref, loss_ref, dmesh_ref, dhalo_ref,
    gm_ref, out_sem, in_sem, eh_ref, eht_ref, d_ref, dt_ref, ext_ref, t_ref, mm_ref, acc_ref, sender_ref,
):
    nodes = mesh_ref.shape[1]
    table = ext_ref.shape[0]
    variables, points = x_ref.shape[1:]
    k_edge = eh_ref.shape[0] // nodes
    counts = [
        pltpu.make_async_copy(source, target, in_sem.at[k])
        for k, (source, target) in enumerate(
            ((eh_in, eh_ref), (d_in, d_ref), (dt_in, dt_ref), (eht_in, eht_ref))
        )
    ]

    def counts_ready(*which):
        @pl.when(pl.program_id(0) == 0)
        def _():
            for k in which:
                counts[k].wait()

    halo = left_ref.shape[1]

    @pl.when(pl.program_id(0) == 0)
    def _():
        for copy in counts:
            copy.start()
        gm_ref[...] = jnp.zeros_like(gm_ref)
        gout_ref[...] = jnp.zeros_like(gout_ref)
        gxd_ref[...] = jnp.zeros_like(gxd_ref)
        ggain_ref[...] = jnp.zeros_like(ggain_ref)
        loss_ref[...] = jnp.zeros_like(loss_ref)

    sent = sent_ref[0]
    ext_ref[:nodes, :] = sent
    ext_ref[nodes : nodes + halo, :] = left_ref[0]
    ext_ref[nodes + halo :, :] = right_ref[0]
    receivers = 0.5 * dot(sent, m3_ref[0])
    sender_ref[...] = (0.5 * dot(ext_ref[...], m2_ref[0])).astype(BF16)

    counts_ready(0)

    def edge(k, carry):
        hid_sum, t_sum = carry
        rows = pl.ds(pl.multiple_of(k * nodes, nodes), nodes)
        hid, t = silu_parts(1.0 * dot(eh_ref[rows, :], sender_ref[...]) + receivers)
        t_ref[rows, :] = t.astype(t_ref.dtype)
        return hid_sum + hid.astype(BF16).astype(F32), t_sum + t

    zero = jnp.zeros((nodes, LATENT), F32)
    hid_sum, t_sum = lax.fori_loop(0, k_edge, edge, (zero, zero), unroll=k_edge)
    h_high = (hid_sum * (1.0 / k_edge)).astype(BF16)
    gain2 = gain_row(small_ref, 1)
    unit2, scale2 = normalise(dot(h_high, m4_ref[0]))
    mesh2 = mesh_ref[0] + unit2 * gain2
    mm_ref[...] = mesh2.astype(BF16)

    counts_ready(1, 2)
    acc_ref[...] = jnp.zeros_like(acc_ref)
    dsum_ref[...] = jnp.zeros_like(dsum_ref)
    member = pl.program_id(0)
    date = date_row(small_ref, day_ref[member])
    gain3 = gain_row(small_ref, 2)
    wout = small_ref[OUT_ROW : OUT_ROW + variables, :]
    square = (variables, variables)
    same = lax.broadcasted_iota(jnp.int32, square, 0) == lax.broadcasted_iota(jnp.int32, square, 1)
    varw = jnp.sum(jnp.where(same, varw_ref[...], 0.0), axis=1, keepdims=True)

    def decode_part(rows):
        dec = dot(d_ref[rows, :], mm_ref[...])
        a2 = (dec * (1.0 / k_pick)).astype(BF16)
        yield True
        hid, t = silu_parts(0.5 * dot(a2, m5_ref[0]))
        h2 = hid.astype(BF16)
        yield True
        unit, scale = normalise(dot(h2, m6_ref[0]))
        yield True
        x = x_ref[0, :, rows]
        grid = dot_tn(x, small_ref[IN_ROW : IN_ROW + variables, :]) + date + unit * gain3
        grid = grid.astype(BF16)
        yield True
        misfit = x.astype(F32) + dot_nt(wout, grid) - y_ref[0, :, rows].astype(F32)
        valid = valid_ref[pl.ds(member, 1), rows].astype(F32)
        weighted = valid * varw * misfit
        loss_ref[...] += jnp.sum(weighted * misfit, axis=1, keepdims=True)
        dsum_ref[0] += jnp.sum(weighted, axis=1, keepdims=True)
        dp = weighted.astype(BF16)
        gout_ref[...] += dot(dp, grid)
        gxd_ref[...] += dot_nt(x, dp)
        yield True
        dgrid = dot_tn(dp, wout)
        ggain_ref[1:2, :] += jnp.sum(dgrid * unit, axis=0, keepdims=True)
        dc = norm_back(dgrid, gain3, unit, scale).astype(BF16)
        gm_ref[4] += dot_tn(h2, dc)
        yield True
        du = (dot_nt(dc, m6_ref[0]) * t).astype(BF16)
        gm_ref[3] += dot_tn(a2, du)
        yield True
        ddec = dot_nt(du, m5_ref[0]).astype(BF16)
        acc_ref[...] += dot(dt_ref[:, rows], ddec)
        yield True

    def grid_block(i, carry):
        part = BLOCK // PARTS
        in_turn(
            decode_part(pl.ds(pl.multiple_of(i * BLOCK + k * part, part), part)) for k in range(PARTS)
        )
        return carry

    lax.fori_loop(0, points // BLOCK, grid_block, 0)

    counts_ready(3)
    decoder_copy = pltpu.make_async_copy(gm_ref.at[3:5], slots_ref.at[3:5], out_sem.at[0])

    @pl.when(member == pl.num_programs(0) - 1)
    def _():
        decoder_copy.start()

    dmesh2 = acc_ref[...] * (1.0 / k_pick)
    ggain_ref[0:1, :] += jnp.sum(dmesh2 * unit2, axis=0, keepdims=True)
    dagg = norm_back(dmesh2, gain2, unit2, scale2).astype(BF16)
    gm_ref[2] += dot_tn(h_high, dagg)
    dhid = dot_nt(dagg, m4_ref[0]) * (1.0 / k_edge)
    dr = (dhid * t_sum).astype(BF16)
    gm_ref[1] += dot_tn(sent, dr)

    def edge_back(k, total):
        rows = pl.ds(pl.multiple_of(k * nodes, nodes), nodes)
        dpre = (dhid * t_ref[rows, :].astype(F32)).astype(BF16)
        return total + dot(eht_ref[:, rows], dpre)

    ds = lax.fori_loop(
        0, k_edge, edge_back, jnp.zeros((table, LATENT), F32), unroll=k_edge
    ).astype(BF16)
    gm_ref[0] += dot_tn(ext_ref[...], ds)
    dext = dot_nt(ds, m2_ref[0])
    dmesh_ref[0] = dmesh2 + dext[:nodes, :] + dot_nt(dr, m3_ref[0])
    dhalo_ref[0] = dext[nodes:, :].astype(BF16)

    @pl.when(member == pl.num_programs(0) - 1)
    def _():
        copy = pltpu.make_async_copy(gm_ref.at[0:3], slots_ref.at[0:3], out_sem.at[1])
        copy.start()
        copy.wait()
        decoder_copy.wait()


def main_scratch(k_edge, nodes, points, table):
    return [
        pltpu.VMEM((5, LATENT, LATENT), F32),
        pltpu.SemaphoreType.DMA((2,)),
        pltpu.SemaphoreType.DMA((4,)),
        pltpu.VMEM((k_edge * nodes, table), BF16),
        pltpu.VMEM((table, k_edge * nodes), BF16),
        pltpu.VMEM((points, nodes), BF16),
        pltpu.VMEM((nodes, points), BF16),
        pltpu.VMEM((table, LATENT), BF16),
        pltpu.VMEM((k_edge * nodes, LATENT), T_TYPE),
        pltpu.VMEM((nodes, LATENT), BF16),
        pltpu.VMEM((nodes, LATENT), F32),
        pltpu.VMEM((table, LATENT), BF16),
    ]


def whole(shape):
    return pl.BlockSpec(shape, lambda m: (0,) * len(shape), pipeline_mode=pl.Buffered(1))


def per_member(shape):
    return pl.BlockSpec((1,) + shape, lambda m: (m, 0, 0))


def call(kernel, members, in_specs, out_shapes, out_specs, scratch, cost, aliases=None):
    return pl.pallas_call(
        kernel,
        grid=(members,),
        in_specs=in_specs,
        out_shape=out_shapes,
        out_specs=out_specs,
        scratch_shapes=scratch,
        input_output_aliases=aliases or {},
        compiler_params=pltpu.CompilerParams(
            dimension_semantics=("arbitrary",), vmem_limit_bytes=VMEM_BYTES
        ),
        cost_estimate=pl.CostEstimate(flops=cost, bytes_accessed=32 << 20, transcendentals=0),
    )


def shape_of(shape, dtype):
    return jax.ShapeDtypeStruct(shape, dtype)


def slot_of(matrix):
    return 2 * matrix - 5 * ((matrix + 1) // 4)


def neighbours():
    region = lax.axis_index("region")
    slot = lax.rem(region, SLOTS)
    base = region - slot
    one = lax.rem(slot, 2)
    two = lax.rem(slot // 2, 2)
    four = slot // 4
    core = slot + 1 - 2 * one
    side = slot + 2 - 4 * two
    up = slot + 4 - 8 * four
    far = side + 4 - 8 * four
    return base, slot, core, side, up, far


def remote(source, target, send, receive, where):
    return pltpu.make_async_remote_copy(
        src_ref=source, dst_ref=target, send_sem=send, recv_sem=receive,
        device_id=where, device_id_type=MESH,
    )


def greet(places):
    barrier = pltpu.get_barrier_semaphore()
    for place in places:
        pl.semaphore_signal(barrier, inc=1, device_id=place, device_id_type=MESH)


def greeted(places):
    pl.semaphore_wait(pltpu.get_barrier_semaphore(), len(places))


def around():
    region, count = lax.axis_index("region"), lax.axis_size("region")
    following, previous = lax.rem(region + 1, count), lax.rem(region + count - 1, count)
    return {"region": following}, {"region": previous}


def encode_kernel(
    depth, day_ref, matrices_ref, in_ref, outp_ref, gains_ref, dates_ref, valid_ref, x_in, picks_ref,
    rows_ref, edge_ref, near_ref,
    full_ref, small_out_ref, total_ref, x4_out, a0_out, h1_out, t1_out, unit_out, scale_out, mesh_out,
    sent_out, left_ref, right_ref, eh_out, eht_out, d_out, dt_out,
    x_ref, edge_cols_ref, grid_cols_ref, eh_ref, eht_ref, d_ref, dt_ref, block_ref, pack_ref, pick_ref, out_ref, x4_ref, xl_ref, a0_ref, h1_ref, t1_ref, unit_ref, scale_ref,
    mesh_ref, sent_ref, buf_ref, w_ref, small_ref, count_ref, counts_ref, sums_ref, heard_ref,
    local_sem, z_send, z_recv, p_send, p_recv, d_send, d_recv, c_send, c_recv, n_send, n_recv,
    s_send, s_recv, w_sem, o_sem, e_send, e_recv, q_sem, b_sem, x_sem,
):
    base, slot, core, side, up, far = neighbours()
    z = lax.axis_index("row")
    half = block_ref.shape[1] // 2
    low, high = pl.ds(0, half), pl.ds(half, half)
    to_core, to_side, to_up = ({"region": base + place} for place in (core, side, up))
    to_next, to_previous = around()
    to_z = [None] + [{"row": lax.rem(z + d, depth)} for d in range(1, depth)]
    steps = range(1, depth)
    members, variables, points = x_in.shape
    nodes = a0_ref.shape[1]
    halo = left_ref.shape[1]
    peers = to_z[1:] + [to_core, to_side, to_up, to_next, to_previous]
    greet(peers)

    def at(d):
        return lax.rem(z + depth - d, depth)

    def arrived(target, receive):
        remote(target, target, receive, receive, to_core).wait_recv()

    def gone(origin, receive):
        remote(origin, origin, receive, receive, to_core).wait_send()

    x_copy = pltpu.make_async_copy(x_in, x_ref, x_sem)
    x_copy.start()

    for k in range(SLOTS - 1):
        block_ref[slot_of(k)] = matrices_ref[k].astype(BF16)
    pack_ref[...] = jnp.zeros_like(pack_ref)
    pack_ref[IN_ROW : IN_ROW + variables, :] = in_ref[...]
    pack_ref[OUT_ROW : OUT_ROW + variables, :] = outp_ref[...]
    pack_ref[GAIN_ROW : GAIN_ROW + gains_ref.shape[0], :] = gains_ref[...]
    pack_ref[DATE_ROW : DATE_ROW + dates_ref.shape[0], :] = dates_ref[...]
    block_ref[SMALL] = jnp.transpose(pack_ref[...]).astype(BF16)
    own = pltpu.make_async_copy(block_ref, full_ref.at[:, z], local_sem)
    own.start()
    table, k_edge, k_near = eht_ref.shape[0], edge_ref.shape[0], near_ref.shape[0]
    k_grid = picks_ref.shape[0]
    wide = 128
    pieces = nodes // wide
    edge_cols_ref[...] = columns_of(edge_ref[...])
    grid_cols_ref[...] = columns_of(picks_ref[...])

    def build_edges(i, carry):
        k, piece = i // pieces, lax.rem(i, pieces)
        inside = pl.ds(pl.multiple_of(piece * wide, wide), wide)
        across = pl.ds(pl.multiple_of(i * wide, wide), wide)
        columns = edge_cols_ref[inside, :].astype(F32)
        chosen = lax.broadcasted_iota(jnp.int32, columns.shape, 1) == k
        column = jnp.sum(jnp.where(chosen, columns, 0.0), axis=1, keepdims=True).astype(jnp.int32)
        eh_ref[across, :] = count_columns(column, table, 1)
        lines = edge_ref[:, inside].astype(F32)
        chosen = lax.broadcasted_iota(jnp.int32, lines.shape, 0) == k
        line = jnp.sum(jnp.where(chosen, lines, 0.0), axis=0, keepdims=True).astype(jnp.int32)
        eht_ref[:, across] = count_rows(line, table)
        return carry

    def build_near(i, carry):
        inside = pl.ds(pl.multiple_of(i * wide, wide), wide)
        near = near_ref[:, inside]
        d_ref[inside, :] = count_columns(columns_of(near), nodes, k_near)
        dt_ref[:, inside] = count_rows(near, nodes)
        return carry

    def build_grid(i, carry):
        inside = pl.ds(pl.multiple_of(i * 64, 64), 64)
        pick_ref[inside, :] = count_columns(grid_cols_ref[inside, :], points, k_grid)
        return carry

    valid = jnp.sum(valid_ref[...].astype(F32), axis=1, keepdims=True)
    valid = jnp.sum(valid, axis=0, keepdims=True)
    count_ref[...] = jnp.broadcast_to(valid, count_ref.shape)
    out_ref[...] = count_columns(columns_of(rows_ref[...]), nodes, 1)
    greeted(peers)
    for d in steps:
        remote(
            block_ref.at[slot], full_ref.at[slot, z], z_send.at[d], z_recv.at[d], to_z[d]
        ).start()
    for d in steps:
        remote(count_ref, counts_ref.at[d], n_send.at[d], n_recv.at[d], to_z[d]).start()

    lax.fori_loop(0, nodes // 64, build_grid, 0)
    edges, nears = k_edge * pieces, points // wide
    first = edges // 4
    share = -(-(edges - first) // (2 * depth - 2))

    def some_edges(i):
        return lax.fori_loop(
            first + i * share, jnp.minimum(first + (i + 1) * share, edges), build_edges, 0
        )

    lax.fori_loop(0, first, build_edges, 0)

    def from_z(d, carry):
        chunk = full_ref.at[slot, at(d)]
        arrived(chunk, z_recv.at[d])
        remote(chunk, chunk, p_send.at[0, d], p_recv.at[0, d], to_side).start()
        remote(chunk, chunk, p_send.at[1, d], p_recv.at[1, d], to_up).start()
        remote(chunk, chunk, c_send.at[0, d], c_recv.at[0, d], to_core).start()
        some_edges(d - 1)
        return carry

    lax.fori_loop(1, depth, from_z, 0)
    builds = [
        pltpu.make_async_copy(ref, target, b_sem.at[k])
        for k, (ref, target) in enumerate(
            ((eh_ref, eh_out), (eht_ref, eht_out), (d_ref, d_out), (dt_ref, dt_out))
        )
    ]

    total = count_ref[...]
    for d in steps:
        arrived(counts_ref.at[d], n_recv.at[d])
        total = total + counts_ref[d]
    sums_ref[0] = total
    partners = (to_core, to_side, to_up)

    def count_copy(step):
        return remote(
            sums_ref.at[step], heard_ref.at[step], s_send.at[step], s_recv.at[step], partners[step]
        )

    count_copy(0).start()

    def from_sides(d, carry):
        chunk = full_ref.at[side, at(d)]
        arrived(chunk, p_recv.at[0, d])
        part = full_ref.at[side, at(d), low]
        remote(part, part, d_send.at[0, d], d_recv.at[0, d], to_up).start()
        remote(chunk, chunk, c_send.at[1, d], c_recv.at[1, d], to_core).start()
        chunk = full_ref.at[up, at(d)]
        arrived(chunk, p_recv.at[1, d])
        part = full_ref.at[up, at(d), high]
        remote(part, part, d_send.at[1, d], d_recv.at[1, d], to_side).start()
        remote(chunk, chunk, c_send.at[2, d], c_recv.at[2, d], to_core).start()
        some_edges(depth - 2 + d)
        return carry

    lax.fori_loop(1, depth, from_sides, 0)
    builds[0].start()
    builds[1].start()

    def gather_inputs(m, carry):
        x4 = dot_nt(pick_ref[...], x_ref[m]) * (1.0 / k_grid)
        top, rest = split_two(x4)
        x4_ref[m] = top
        xl_ref[m] = rest
        return carry

    x_copy.wait()
    lax.fori_loop(0, members, gather_inputs, 0)
    for step in (1, 2):
        count_copy(step - 1).wait_recv()
        total = total + heard_ref[step - 1]
        sums_ref[step] = total
        count_copy(step).start()

    def from_far(d, carry):
        arrived(full_ref.at[far, at(d), low], d_recv.at[0, d])
        arrived(full_ref.at[far, at(d), high], d_recv.at[1, d])
        chunk = full_ref.at[far, at(d)]
        remote(chunk, chunk, c_send.at[3, d], c_recv.at[3, d], to_core).start()
        return carry

    lax.fori_loop(1, depth, from_far, 0)
    lax.fori_loop(0, nears, build_near, 0)
    builds[2].start()
    builds[3].start()
    count_copy(2).wait_recv()
    total_ref[...] = total + heard_ref[2]

    def from_core(d, carry):
        for k in range(4):
            arrived(full_ref.at[core, at(d)], c_recv.at[k, d])
        return carry

    lax.fori_loop(1, depth, from_core, 0)
    own.wait()

    loads = [
        pltpu.make_async_copy(full_ref.at[j], w_ref.at[k], w_sem.at[k])
        for k, j in enumerate((SMALL, slot_of(0), slot_of(1)))
    ]
    for copy in loads:
        copy.start()
    for copy in loads:
        copy.wait()
    small_ref[...] = jnp.transpose(w_ref[0].reshape(LATENT, LATENT))
    small_copy = pltpu.make_async_copy(small_ref, small_out_ref, q_sem)
    small_copy.start()
    kept = (
        (x4_ref, x4_out), (a0_ref, a0_out), (h1_ref, h1_out), (t1_ref, t1_out), (unit_ref, unit_out),
        (scale_ref, scale_out), (mesh_ref, mesh_out), (sent_ref, sent_out),
    )

    def kept_copies(m):
        return [
            pltpu.make_async_copy(ref.at[m], target.at[m], o_sem.at[k, m])
            for k, (ref, target) in enumerate(kept)
        ]

    def halo_copies(m):
        return [
            remote(buf_ref.at[m, halo:], left_ref.at[m], e_send.at[0, m], e_recv.at[0, m], to_next),
            remote(buf_ref.at[m, :halo], right_ref.at[m], e_send.at[1, m], e_recv.at[1, m], to_previous),
        ]

    def encode_member(m, carry):
        win = small_ref[IN_ROW : IN_ROW + variables, :]
        agg = dot(x4_ref[m], win) + dot(xl_ref[m], win) + date_row(small_ref, day_ref[m])
        a0 = agg.astype(BF16)
        hid, t1 = silu_parts(0.5 * dot(a0, w_ref[1].reshape(LATENT, LATENT)))
        h1 = hid.astype(BF16)
        unit, scale = normalise(dot(h1, w_ref[2].reshape(LATENT, LATENT)))
        mesh = agg + unit * gain_row(small_ref, 0)
        low_mesh = mesh.astype(BF16)
        buf_ref[m] = dot(out_ref[...], low_mesh).astype(BF16)
        for copy in halo_copies(m):
            copy.start()
        a0_ref[m] = a0
        h1_ref[m] = h1
        t1_ref[m] = t1.astype(BF16)
        unit_ref[m] = unit
        scale_ref[m] = scale
        mesh_ref[m] = mesh
        sent_ref[m] = low_mesh
        for copy in kept_copies(m):
            copy.start()
        return carry

    lax.fori_loop(0, members, encode_member, 0)

    def finish_member(m, carry):
        for copy in halo_copies(m) + kept_copies(m):
            copy.wait()
        return carry

    def finish_row(d, carry):
        gone(block_ref.at[slot], z_send.at[d])
        gone(count_ref, n_send.at[d])
        chunk = full_ref.at[slot, at(d)]
        for k in range(2):
            gone(chunk, p_send.at[k, d])
            gone(full_ref.at[slot, at(d), low], d_send.at[k, d])
        for k in range(4):
            gone(chunk, c_send.at[k, d])
        return carry

    lax.fori_loop(0, members, finish_member, 0)
    lax.fori_loop(1, depth, finish_row, 0)
    for step in range(3):
        count_copy(step).wait_send()
    for copy in builds:
        copy.wait()
    small_copy.wait()


def encode(
    day, matrices, in_proj, out_proj, gains, dates, valid, inputs, picks, rows, edges, near, depth
):
    hbm = pl.BlockSpec(memory_space=pl.ANY)
    vmem = pl.BlockSpec(memory_space=pltpu.VMEM)
    dma = pltpu.SemaphoreType.DMA
    members, variables, points = inputs.shape
    nodes = picks.shape[1]
    halo = rows.shape[1] // 2
    share = matrices.shape[1]
    nodes_of = (members, nodes, LATENT)
    table, pairs = nodes + 2 * halo, edges.shape[0] * nodes
    counts = ((pairs, table), (table, pairs), (points, nodes), (nodes, points))
    kept = [
        ((members, nodes, variables), BF16),
        (nodes_of, BF16),
        (nodes_of, BF16),
        (nodes_of, BF16),
        (nodes_of, F32),
        ((members, nodes, 1), F32),
        (nodes_of, F32),
        (nodes_of, BF16),
    ]
    return pl.pallas_call(
        partial(encode_kernel, depth),
        in_specs=[pl.BlockSpec(memory_space=pltpu.SMEM)] + [vmem] * 6 + [hbm] + [vmem] * 4,
        out_shape=[
            shape_of((SLOTS, depth, share, LATENT), BF16),
            shape_of((LATENT, LATENT), BF16),
            shape_of((8, 128), F32),
            *(shape_of(*one) for one in kept),
            shape_of((members, halo, LATENT), BF16),
            shape_of((members, halo, LATENT), BF16),
            *(shape_of(one, BF16) for one in counts),
        ],
        out_specs=[hbm, hbm, vmem] + [hbm] * (len(kept) + 2 + len(counts)),
        scratch_shapes=[
            pltpu.VMEM(inputs.shape, BF16),
            pltpu.VMEM((nodes, 8), jnp.int32),
            pltpu.VMEM((nodes, 8), jnp.int32),
            *(pltpu.VMEM(one, BF16) for one in counts),
            pltpu.VMEM((SLOTS, share, LATENT), BF16),
            pltpu.VMEM((LATENT, share), F32),
            pltpu.VMEM((nodes, points), BF16),
            pltpu.VMEM((2 * halo, nodes), BF16),
            pltpu.VMEM(*kept[0]),
            *(pltpu.VMEM(*one) for one in kept),
            pltpu.VMEM((members, 2 * halo, LATENT), BF16),
            pltpu.VMEM((3, depth, share, LATENT), BF16),
            pltpu.VMEM((LATENT, LATENT), BF16),
            pltpu.VMEM((8, 128), F32),
            pltpu.VMEM((depth, 8, 128), F32),
            pltpu.VMEM((3, 8, 128), F32),
            pltpu.VMEM((3, 8, 128), F32),
            dma,
            dma((depth,)),
            dma((depth,)),
            dma((2, depth)),
            dma((2, depth)),
            dma((2, depth)),
            dma((2, depth)),
            dma((4, depth)),
            dma((4, depth)),
            dma((depth,)),
            dma((depth,)),
            dma((3,)),
            dma((3,)),
            dma((3,)),
            dma((len(kept), members)),
            dma((2, members)),
            dma((2, members)),
            dma,
            dma((len(counts),)),
            dma,
        ],
        compiler_params=pltpu.CompilerParams(
            collective_id=0, has_side_effects=True, vmem_limit_bytes=VMEM_BYTES
        ),
    )(
        day, matrices, in_proj, out_proj, gains, dates, valid, inputs, picks, rows, edges, near
    )


def reduce_kernel(
    depth, day_ref, late_ref, momentum_in, count_ref, dmesh_in, dhalo_ref, rows_ref, x4_in, a0_in,
    h1_in, t1_in, unit_in, scale_in, weights_ref, small_ref, gxd_ref, dsum_ref, gout_ref, ggain_ref,
    loss_ref,
    g_ref, x_ref,
    momentum_ref, dmesh_ref, ret_ref, x4_ref, a0_ref, h1_ref, t1_ref, unit_ref, scale_ref, m_ref, back_ref, pack_ref,
    early_ref, own_ref, heard_ref, snd_ref, rcv_ref, snd_low_ref, rcv_low_ref, acc_ref, zr_ref,
    g_own_ref, mb_ref, x_own_ref,
    i_sem, e_send, e_recv, l_sem, h_send, h_recv, p_send, p_recv, q_send, q_recv, z_send, z_recv,
    m_send, m_recv, g_local, g_send, g_recv, x_local, x_send, x_recv,
):
    base, slot, core, side, up, far = neighbours()
    z = lax.axis_index("row")
    rows = acc_ref.shape[0] // depth
    chips = SLOTS // 2
    mine = slot // 2
    parity = lax.rem(slot, 2)
    members, variables = x4_ref.shape[0], x4_ref.shape[2]
    halo = dhalo_ref.shape[1] // 2
    to_core, to_side, to_up, to_far = ({"region": base + place} for place in (core, side, up, far))
    to_next, to_previous = around()
    to_place = (to_far, to_side, to_up)
    places = (far, side, up)
    to_z = [None] + [{"row": lax.rem(z + d, depth)} for d in range(1, depth)]
    peers = to_z[1:] + [to_core, to_side, to_up, to_far, to_next, to_previous]
    greet(peers)
    sent = []

    def both_ends(i):
        return lax.rem(i * (depth - 1), depth)

    def part_of(b):
        return pl.ds(pl.multiple_of(b * rows, rows), rows)

    def send(*args):
        copy = remote(*args)
        copy.start()
        sent.append(copy)

    def arrived(target, receive):
        remote(target, target, receive, receive, to_core).wait_recv()

    def load(*args):
        copy = pltpu.make_async_copy(*args)
        copy.start()
        return copy

    def halo_copies(m):
        return [
            remote(dhalo_ref.at[m, halo:], ret_ref.at[m, :halo], e_send.at[0, m], e_recv.at[0, m], to_next),
            remote(
                dhalo_ref.at[m, :halo], ret_ref.at[m, halo:], e_send.at[1, m], e_recv.at[1, m], to_previous
            ),
        ]

    inner = ((dmesh_in, dmesh_ref), (x4_in, x4_ref), (a0_in, a0_ref), (h1_in, h1_ref), (t1_in, t1_ref),
             (unit_in, unit_ref), (scale_in, scale_ref))

    def inner_loads(m):
        return [
            pltpu.make_async_copy(ref.at[m], target.at[m], i_sem.at[k, m])
            for k, (ref, target) in enumerate(inner)
        ]

    for m in range(members):
        for copy in inner_loads(m):
            copy.start()
    m_loads = [
        load(momentum_in.at[mine + (SLOTS // 2 - 1) * parity], momentum_ref, i_sem.at[len(inner) + 1, 0])
    ]
    first = load(late_ref.at[0], early_ref.at[2], i_sem.at[len(inner), 0])
    for k in range(2):
        m_loads.append(load(weights_ref.at[slot_of(k)], m_ref.at[k], i_sem.at[len(inner), 1 + k]))

    def late_copy(chip):
        return remote(
            late_ref.at[1 + chip], heard_ref.at[chip], h_send.at[chip, 0], h_recv.at[chip, 0], to_core
        )

    def late_load(chip):
        return pltpu.make_async_copy(late_ref.at[1 + chip], own_ref.at[chip], l_sem.at[chip])

    def early_copy(chip, b):
        return remote(
            early_ref.at[chip, part_of(b)], heard_ref.at[chip, part_of(b)], h_send.at[chip, b],
            h_recv.at[chip, b], to_core,
        )

    def low_copy(b):
        return remote(
            snd_low_ref.at[part_of(b)], rcv_low_ref.at[mine, part_of(b)], q_send.at[b], q_recv.at[mine, b],
            {"region": base + SMALL},
        )

    def chip_copy(chip, b):
        return remote(
            snd_ref.at[chip, part_of(b)], rcv_ref.at[mine, part_of(b)], p_send.at[chip, b],
            p_recv.at[mine, b], {"region": base + 2 * chip + parity},
        )

    def pass_on(chip, b, own):
        part = part_of(b)
        total = own[chip, part, :] + heard_ref[chip, part, :]

        @pl.when(mine == chip)
        def _():
            acc_ref[part, :] = total

        @pl.when(mine != chip)
        def _():
            snd_ref[chip, part, :] = total.astype(BF16)
            chip_copy(chip, b).start()

    def pass_late(chip):
        @pl.when(parity == 1)
        def _():
            late_load(chip).wait()
            late_copy(chip).wait_recv()

            def piece(b, carry):
                pass_on(chip, b, own_ref)
                return carry

            lax.fori_loop(0, depth, piece, 0)

    def pass_early(i, carry):
        b = both_ends(i)

        @pl.when(parity == 0)
        def _():
            def piece(chip, carry):
                early_copy(chip, b).wait_recv()
                pass_on(chip, b, early_ref)
                return carry

            lax.fori_loop(0, chips, piece, 0)

        return carry

    def pass_low(b, carry):
        part = part_of(b)
        total = early_ref[SMALL // 2, part, :] + heard_ref[SMALL // 2, part, :]
        snd_low_ref[part, :] = (total - total.astype(BF16).astype(F32)).astype(BF16)
        low_copy(b).start()
        return carry

    @pl.when(parity == 1)
    def _():
        for chip in range(chips):
            late_load(chip).start()

    lines = lax.broadcasted_iota(jnp.int32, (16, LATENT), 0)
    back_ref[...] = count_rows(rows_ref[...], back_ref.shape[0])
    wout = small_ref[OUT_ROW : OUT_ROW + variables, :]
    pack_ref[...] = jnp.zeros_like(pack_ref)
    top, rest = split_two(gxd_ref[...])
    pack_ref[IN_ROW : IN_ROW + variables, :] = dot(top, wout) + dot(rest, wout)
    pack_ref[OUT_ROW : OUT_ROW + variables, :] = gout_ref[...]
    pack_ref[GAIN_ROW + 1 : GAIN_ROW + 3, :] = ggain_ref[...]
    loss = jnp.sum(loss_ref[...], axis=0, keepdims=True)
    pack_ref[LOSS_ROW : LOSS_ROW + 1, :] = jnp.broadcast_to(loss, (1, LATENT))
    early_ref[0:2] = jnp.zeros((2, LATENT, LATENT), F32)
    greeted(peers)
    for m in range(members):
        for copy in halo_copies(m):
            copy.start()

    @pl.when(parity == 0)
    def _():
        for chip in range(chips):
            late_copy(chip).start()

    for copy in m_loads:
        copy.wait()

    def member_back(m, carry):
        for copy in inner_loads(m):
            copy.wait()
        for copy in halo_copies(m):
            copy.wait()
        dmesh = dmesh_ref[m] + dot(back_ref[...], ret_ref[m])
        unit = unit_ref[m]
        pack_ref[GAIN_ROW : GAIN_ROW + 1, :] += jnp.sum(dmesh * unit, axis=0, keepdims=True)
        dc = norm_back(dmesh, gain_row(small_ref, 0), unit, scale_ref[m]).astype(BF16)
        early_ref[1] += dot_tn(h1_ref[m], dc)
        du = (dot_nt(dc, m_ref[1]) * t1_ref[m].astype(F32)).astype(BF16)
        early_ref[0] += dot_tn(a0_ref[m], du)
        dagg = dmesh + dot_nt(du, m_ref[0])
        pack_ref[IN_ROW : IN_ROW + variables, :] += dot_tn(x4_ref[m], dagg.astype(BF16))
        top, rest = split_two(dsum_ref[m])
        date = jnp.sum(dagg, axis=0, keepdims=True) + dot_tn(top, wout) + dot_tn(rest, wout)
        pack_ref[DATE_ROW : DATE_ROW + 16, :] += jnp.where(lines == day_ref[m], date, 0.0)

        @pl.when(m < chips)
        def _():
            pass_late(m)

        return carry

    lax.fori_loop(0, members, member_back, 0)
    for chip in range(members, chips):
        pass_late(chip)
    early_ref[SMALL // 2] = jnp.transpose(pack_ref[...])
    first.wait()

    @pl.when(parity == 1)
    def _():
        for i in range(depth):
            for chip in range(chips):
                early_copy(chip, i * (depth - 1) % depth).start()

    lax.fori_loop(0, depth, pass_early, 0)

    @pl.when((mine != SMALL // 2) & (parity == 0))
    def _():
        lax.fori_loop(0, depth, pass_low, 0)

    sources = [lax.rem(mine + i, chips) for i in range(1, chips)]
    def z_copy(b):
        d = lax.rem(b - z + depth, depth)
        return remote(acc_ref.at[part_of(b)], zr_ref.at[d], z_send.at[b], z_recv.at[d], {"row": b + 0 * z})

    def across_z(i, carry):
        b = both_ends(i)
        part = part_of(b)
        total = acc_ref[part, :]
        for c in sources:
            arrived(rcv_ref.at[c, part], p_recv.at[c, b])
            total = total + rcv_ref[c, part, :].astype(F32)
        acc_ref[part, :] = total

        @pl.when(slot == SMALL)
        def _():
            low = acc_ref[part, :]
            for c in sources:
                arrived(rcv_low_ref.at[c, part], q_recv.at[c, b])
                low = low + rcv_low_ref[c, part, :].astype(F32)
            acc_ref[part, :] = low

        @pl.when(z != b)
        def _():
            z_copy(b).start()

        return carry

    lax.fori_loop(0, depth, across_z, 0)
    zr_ref[0] = acc_ref[pl.ds(pl.multiple_of(z * rows, rows), rows), :]
    for d in range(1, depth):
        arrived(zr_ref.at[d], z_recv.at[d])
    g_own = zr_ref[z]
    for place in range(1, depth):
        g_own = g_own + zr_ref[lax.rem(z + depth - place, depth)]
    g_own_ref[...] = g_own
    momentum = (
        MUON_MOMENTUM * momentum_ref[...]
        + (2.0 / count_ref[0:1, 0:1]) * g_own
    )
    mb_ref[0] = momentum.astype(BF16)
    for d in range(1, depth):
        send(mb_ref.at[0], mb_ref.at[d], m_send.at[d], m_recv.at[d], to_z[d])
    g_copy = load(g_own_ref, g_ref.at[slot], g_local)
    for k in range(3):
        send(g_own_ref, g_ref.at[slot], g_send.at[k], g_recv.at[k], to_place[k])
    send(g_own_ref, g_ref.at[slot], g_send.at[3], g_recv.at[3], to_core)

    for d in range(1, depth):
        arrived(mb_ref.at[d], m_recv.at[d])
    everything = jnp.concatenate([mb_ref[d] for d in range(depth)], axis=0)
    wide = everything.astype(F32)
    squares = jnp.sum(jnp.sum(wide * wide, axis=1, keepdims=True), axis=0, keepdims=True)
    inverse = lax.rsqrt(squares + 1e-07)
    turn = momentum * inverse
    current = (wide * inverse).astype(BF16)
    turn_low = turn.astype(BF16)
    for sweep in range(NS_ITERS):
        gram = dot_tn(current, current)
        gram_low = gram.astype(BF16)
        mixing = NS_COEFFS[1] * gram + NS_COEFFS[2] * dot(gram_low, gram_low)
        mixing = mixing.astype(BF16)
        turn = NS_COEFFS[0] * turn + dot(turn_low, mixing)
        turn_low = turn.astype(BF16)
        if sweep < NS_ITERS - 1:
            current = (NS_COEFFS[0] * current.astype(F32) + dot(current, mixing)).astype(BF16)
    x_own_ref[...] = turn_low
    x_copy = pltpu.make_async_copy(x_own_ref, x_ref.at[slot], x_local)
    x_copy.start()
    for k in range(3):
        send(x_own_ref, x_ref.at[slot], x_send.at[k], x_recv.at[k], to_place[k])
    send(x_own_ref, x_ref.at[slot], x_send.at[3], x_recv.at[3], to_core)

    for target, send_sem, recv_sem in ((g_ref, g_send, g_recv), (x_ref, x_send, x_recv)):
        for k in range(3):
            chunk = target.at[places[k]]
            arrived(chunk, recv_sem.at[k])
            send(chunk, chunk, send_sem.at[4 + k], recv_sem.at[4 + k], to_core)
    for target, recv_sem in ((g_ref, g_recv), (x_ref, x_recv)):
        for k in range(3, 7):
            arrived(target.at[core], recv_sem.at[k])
    for copy in sent:
        copy.wait_send()
    @pl.when(parity == 0)
    def _():
        for chip in range(chips):
            late_copy(chip).wait_send()

    @pl.when(parity == 1)
    def _():
        for b in range(depth):
            for chip in range(chips):
                early_copy(chip, b).wait_send()

    for b in range(depth):
        for chip in range(chips):

            @pl.when(mine != chip)
            def _():
                chip_copy(chip, b).wait_send()

        @pl.when((mine != SMALL // 2) & (parity == 0))
        def _():
            low_copy(b).wait_send()

        @pl.when(z != b)
        def _():
            z_copy(b).wait_send()

    g_copy.wait()
    x_copy.wait()


def reduce_gradients(
    day, late, momentum, count, dmesh, dhalo, rows, kept, weights, small, gxd, dsum, gout, ggain, loss,
    depth,
):
    hbm = pl.BlockSpec(memory_space=pl.ANY)
    vmem = pl.BlockSpec(memory_space=pltpu.VMEM)
    dma = pltpu.SemaphoreType.DMA
    members, nodes, width = dmesh.shape
    height = LATENT
    share = height // depth
    halo = dhalo.shape[1]
    chips = SLOTS // 2

    return pl.pallas_call(
        partial(reduce_kernel, depth),
        in_specs=[pl.BlockSpec(memory_space=pltpu.SMEM), hbm, hbm, vmem, hbm, vmem, vmem]
        + [hbm] * len(kept)
        + [hbm]
        + [vmem] * 6,
        out_shape=[
            shape_of((SLOTS, share, width), F32),
            shape_of((SLOTS, share, width), BF16),
        ],
        out_specs=[hbm, hbm],
        scratch_shapes=[
            pltpu.VMEM((share, width), F32),
            pltpu.VMEM(dmesh.shape, F32),
            pltpu.VMEM(dhalo.shape, BF16),
            *(pltpu.VMEM(one.shape, one.dtype) for one in kept),
            pltpu.VMEM((2, height, width), BF16),
            pltpu.VMEM((nodes, halo), BF16),
            pltpu.VMEM((height, width), F32),
            pltpu.VMEM((4, height, width), F32),
            pltpu.VMEM((chips, height, width), F32),
            pltpu.VMEM((chips, height, width), F32),
            pltpu.VMEM((chips, height, width), BF16),
            pltpu.VMEM((chips, height, width), BF16),
            pltpu.VMEM((height, width), BF16),
            pltpu.VMEM((chips, height, width), BF16),
            pltpu.VMEM((height, width), F32),
            pltpu.VMEM((depth, share, width), F32),
            pltpu.VMEM((share, width), F32),
            pltpu.VMEM((depth, share, width), BF16),
            pltpu.VMEM((share, width), BF16),
            dma((len(kept) + 3, members)),
            dma((2, members)),
            dma((2, members)),
            dma((chips,)),
            dma((chips, depth)),
            dma((chips, depth)),
            dma((chips, depth)),
            dma((chips, depth)),
            dma((depth,)),
            dma((chips, depth)),
            dma((depth,)),
            dma((depth,)),
            dma((depth,)),
            dma((depth,)),
            dma,
            dma((7,)),
            dma((7,)),
            dma,
            dma((7,)),
            dma((7,)),
        ],
        compiler_params=pltpu.CompilerParams(
            collective_id=1, has_side_effects=True, vmem_limit_bytes=VMEM_BYTES
        ),
    )(
        day, late, momentum, count, dmesh, dhalo, rows, *kept, weights, small, gxd, dsum, gout,
        ggain, loss,
    )


def turn_whole(sums, count, momentum):
    blocks = jnp.stack([sums[slot_of(k)] for k in range(SLOTS - 1)])
    blocks = MUON_MOMENTUM * momentum + (2.0 / count[0, 0]) * blocks
    squares = lax.psum(jnp.sum(blocks * blocks, axis=(1, 2)), "row")
    current = blocks * lax.rsqrt(squares + 1e-07)[:, None, None]

    def product(expression, left, right):
        return jnp.einsum(expression, left, right, precision=lax.Precision.HIGHEST)

    for _ in range(NS_ITERS):
        gram = lax.psum(product("mrk,mrl->mkl", current, current), "row")
        mixing = NS_COEFFS[1] * gram + NS_COEFFS[2] * product("mkj,mjl->mkl", gram, gram)
        current = NS_COEFFS[0] * current + product("mrk,mkl->mrl", current, mixing)
    current = current.astype(BF16)
    by_slot = {slot_of(k): current[k] for k in range(SLOTS - 1)}
    return jnp.stack([by_slot.get(k, current[0]) for k in range(SLOTS)])


def finish_kernel(
    g_ref, rest_ref, x_ref, count_ref, matrix_ref, momentum_ref,
    in_ref, in1_ref, in2_ref, out_ref, out1_ref, out2_ref, gain_ref, gain1_ref, gain2_ref,
    date_ref, date1_ref, date2_ref,
    new_matrix_ref, new_momentum_ref,
    nin_ref, nin1_ref, nin2_ref, nout_ref, nout1_ref, nout2_ref, ngain_ref, ngain1_ref, ngain2_ref,
    ndate_ref, ndate1_ref, ndate2_ref, loss_ref, valid_ref,
):
    scale = 2.0 / count_ref[0:1, 0:1]
    new_momentum_ref[...] = MUON_MOMENTUM * momentum_ref[...] + scale * g_ref[...]
    new_matrix_ref[...] = (
        matrix_ref[...] * (1.0 - MUON_RATE * WEIGHT_DECAY) - MUON_RATE * x_ref[...].astype(F32)
    )

    @pl.when(pl.program_id(0) == pl.num_programs(0) // 2)
    def _():
        rest = jnp.transpose(rest_ref[0])
        loss_ref[0, 0] = jnp.sum(rest[LOSS_ROW : LOSS_ROW + 1, 0:1])
        valid_ref[0, 0] = jnp.sum(count_ref[0:1, 0:1])
        rest = rest * scale
        for row, rate, decay, old, new in (
            (IN_ROW, MATRIX_RATE, WEIGHT_DECAY, (in_ref, in1_ref, in2_ref), (nin_ref, nin1_ref, nin2_ref)),
            (OUT_ROW, MATRIX_RATE, WEIGHT_DECAY, (out_ref, out1_ref, out2_ref),
             (nout_ref, nout1_ref, nout2_ref)),
            (GAIN_ROW, VECTOR_RATE, 0.0, (gain_ref, gain1_ref, gain2_ref),
             (ngain_ref, ngain1_ref, ngain2_ref)),
            (DATE_ROW, VECTOR_RATE, 0.0, (date_ref, date1_ref, date2_ref),
             (ndate_ref, ndate1_ref, ndate2_ref)),
        ):
            weight, first, second = (ref[...] for ref in old)
            gradient = rest[row : row + weight.shape[0], :]
            for ref, value in zip(new, adam_update(weight, gradient, first, second, rate, decay)):
                ref[...] = value


def finish(sums, turned, count, matrices, momentum, vectors):
    share, width = sums.shape[1:]

    def slot_block():
        return pl.BlockSpec((1, share, width), lambda m: (slot_of(m), 0, 0))

    one = pl.BlockSpec((1, share, width), lambda m: (m, 0, 0))
    return pl.pallas_call(
        finish_kernel,
        grid=(matrices.shape[0],),
        in_specs=[
            slot_block(), pl.BlockSpec((1, share, width), lambda m: (SMALL, 0, 0)), slot_block(),
            whole(count.shape), one, one, *(whole(v.shape) for v in vectors),
        ],
        out_shape=[shape_of(matrices.shape, F32)] * 2
        + [shape_of(v.shape, F32) for v in vectors]
        + [shape_of((1, 1), F32)] * 2,
        out_specs=[one, one] + [whole(v.shape) for v in vectors]
        + [pl.BlockSpec(memory_space=pltpu.SMEM)] * 2,
        compiler_params=pltpu.CompilerParams(
            dimension_semantics=("arbitrary",), vmem_limit_bytes=VMEM_BYTES
        ),
    )(sums, sums, turned, count, matrices, momentum, *vectors)


def adam_update(weight, gradient, first_moment, second_moment, step_rate, decay_rate):
    first_new = BETA_ONE * first_moment + (1.0 - BETA_ONE) * gradient
    second_new = BETA_TWO * second_moment + (1.0 - BETA_TWO) * gradient * gradient
    unbiased_one = first_new / (1.0 - BETA_ONE**STEP)
    unbiased_two = second_new / (1.0 - BETA_TWO**STEP)
    weight_new = weight * (1.0 - step_rate * decay_rate) - step_rate * unbiased_one / (
        jnp.sqrt(unbiased_two) + 1e-08
    )
    return (weight_new, first_new, second_new)


def body(
    inputs,
    targets,
    valid_steps,
    var_weights,
    grid_to_mesh,
    mesh_edges,
    send_rows,
    mesh_to_grid,
    date_index,
    matrices,
    matrices_momentum,
    in_proj,
    in_first,
    in_second,
    out_proj,
    out_first,
    out_second,
    norm_gains,
    gains_first,
    gains_second,
    date_table,
    date_first,
    date_second,
):
    inputs = jnp.swapaxes(inputs, 1, 2)
    targets = jnp.swapaxes(targets, 1, 2)
    members, variables, points = inputs.shape
    nodes = grid_to_mesh.shape[0]
    halo = send_rows.shape[0] // 2
    table = nodes + 2 * halo
    k_edge = mesh_edges.shape[1]
    k_pick = mesh_to_grid.shape[1]
    dates = date_table.shape[0]

    depth = lax.axis_size("row")
    regions = lax.axis_size("region")
    groups = [[g * SLOTS + q for g in range(regions // SLOTS)] for q in range(SLOTS)]
    scalars = pl.BlockSpec(memory_space=pltpu.SMEM)
    hbm = pl.BlockSpec(memory_space=pl.ANY)
    gathered, small, count, *kept, left, right, eh, eht, d, dt = encode(
        date_index, matrices, in_proj, out_proj.T, norm_gains, date_table, valid_steps, inputs,
        grid_to_mesh.T, send_rows[None, :], mesh_edges.T, mesh_to_grid.T, depth,
    )
    mesh1, sent = kept[6:]
    if regions > SLOTS:
        count = lax.psum(count, "region", axis_index_groups=groups)
    weights = gathered.reshape(SLOTS, LATENT, LATENT)
    node_block = per_member((nodes, LATENT))

    def matrix(j):
        place = slot_of(j)
        return pl.BlockSpec(
            (1, LATENT, LATENT), lambda m: (place, 0, 0), pipeline_mode=pl.Buffered(1)
        )

    out_shape = (variables, LATENT)
    late, gout, gxd, dsum, ggain_late, loss_row, dmesh, dhalo = call(
        partial(main_kernel, k_pick),
        members,
        [
            scalars,
            node_block,
            node_block,
            per_member((halo, LATENT)),
            per_member((halo, LATENT)),
            per_member((variables, points)),
            per_member((variables, points)),
            whole((members, points)),
            whole((1, variables)),
            hbm,
            hbm,
            hbm,
            hbm,
            whole((LATENT, LATENT)),
            matrix(2),
            matrix(3),
            matrix(4),
            matrix(5),
            matrix(6),
        ],
        [
            shape_of((5, LATENT, LATENT), F32),
            shape_of(out_shape, F32),
            shape_of((variables, variables), F32),
            shape_of((members, variables, 1), F32),
            shape_of((2, LATENT), F32),
            shape_of((variables, 1), F32),
            shape_of((members, nodes, LATENT), F32),
            shape_of((members, 2 * halo, LATENT), BF16),
        ],
        [
            hbm,
            whole(out_shape),
            whole((variables, variables)),
            per_member((variables, 1)),
            whole((2, LATENT)),
            whole((variables, 1)),
            node_block,
            per_member((2 * halo, LATENT)),
        ],
        main_scratch(k_edge, nodes, points, table),
        60_000_000_000,
    )(
        date_index,
        mesh1,
        sent,
        left,
        right,
        inputs,
        targets,
        valid_steps,
        var_weights[None, :],
        eh,
        eht,
        d,
        dt,
        small,
        weights,
        weights,
        weights,
        weights,
        weights,
    )

    sums, turned = reduce_gradients(
        date_index, late, matrices_momentum, count, dmesh, dhalo, send_rows[None, :], kept[:6], weights,
        small, gxd, dsum, gout, ggain_late, loss_row, depth,
    )
    if regions > SLOTS:
        sums = lax.psum(sums, "region", axis_index_groups=groups)
        turned = turn_whole(sums, count, matrices_momentum)
    vectors = (
        in_proj, in_first, in_second, out_proj.T, out_first.T, out_second.T,
        norm_gains, gains_first, gains_second, date_table, date_first, date_second,
    )
    new = finish(sums, turned, count, matrices, matrices_momentum, vectors)
    return (
        *new[:5],
        *(part.T for part in new[5:8]),
        *new[8:14],
        new[14].reshape(()),
        new[15].reshape(()),
    )


def solution(mesh):
    in_specs = (
        P("row", "region", None),
        P("row", "region", None),
        P("row", "region"),
        P(),
        P("region", None),
        P("region", None),
        P("region"),
        P("region", None),
        P("row"),
        P(None, "row", None),
        P(None, "row", None),
        P(None, "row"),
        P(None, "row"),
        P(None, "row"),
        P("row", None),
        P("row", None),
        P("row", None),
        P(None, "row"),
        P(None, "row"),
        P(None, "row"),
        P(None, "row"),
        P(None, "row"),
        P(None, "row"),
    )
    out_specs = (
        P(None, "row", None),
        P(None, "row", None),
        P(None, "row"),
        P(None, "row"),
        P(None, "row"),
        P("row", None),
        P("row", None),
        P("row", None),
        P(None, "row"),
        P(None, "row"),
        P(None, "row"),
        P(None, "row"),
        P(None, "row"),
        P(None, "row"),
        P(),
        P(),
    )
    return jax.shard_map(body, mesh=mesh, in_specs=in_specs, out_specs=out_specs, check_vma=False)
```

```python
from functools import partial

import jax
import jax.numpy as jnp
from jax import lax
from jax.experimental import pallas as pl
from jax.experimental.pallas import tpu as pltpu
from jax.sharding import PartitionSpec as P

NS_ITERS = 2
STEP = 10
NS_COEFFS = (3.4445, -4.775, 2.0315)
MUON_RATE = 0.8
MUON_MOMENTUM = 0.95
MATRIX_RATE = 0.05
VECTOR_RATE = 0.2
BETA_ONE = 0.9
BETA_TWO = 0.95
WEIGHT_DECAY = 0.01

F32 = jnp.float32
BF16 = jnp.bfloat16
LATENT = 512
BLOCK = 1024
PARTS = 1
T_TYPE = BF16
VMEM_BYTES = 60 * 1024 * 1024
MESH = pl.DeviceIdType.MESH
SLOTS = 8
SMALL = 6
IN_ROW, OUT_ROW, GAIN_ROW, DATE_ROW, LOSS_ROW = 0, 240, 480, 496, 504


def dot(left, right):
    return jnp.dot(left, right, preferred_element_type=F32)


def dot_nt(left, right):
    return lax.dot_general(left, right, (((1,), (1,)), ((), ())), preferred_element_type=F32)


def dot_tn(left, right):
    return lax.dot_general(left, right, (((0,), (0,)), ((), ())), preferred_element_type=F32)


def split_two(values):
    high = values.astype(BF16)
    return high, (values - high.astype(F32)).astype(BF16)


def silu_parts(half):
    bend = jnp.tanh(half)
    gate = 0.5 * bend + 0.5
    hid = half * bend + half
    return hid, gate + hid * (1.0 - gate)


def normalise(values):
    centred = values - jnp.mean(values, axis=-1, keepdims=True)
    spread = jnp.mean(centred * centred, axis=-1, keepdims=True)
    scale = lax.rsqrt(spread + 1e-05)
    return centred * scale, scale


def norm_back(grad, gain, unit, scale):
    scaled = gain * grad
    mean_one = jnp.mean(scaled, axis=-1, keepdims=True)
    mean_two = jnp.mean(scaled * unit, axis=-1, keepdims=True)
    return scale * (scaled - mean_one - unit * mean_two)


def in_turn(parts):
    parts = list(parts)
    while parts:
        parts = [part for part in parts if next(part, None) is not None]


def count_columns(index, width, count):
    lanes = lax.broadcasted_iota(jnp.int32, (index.shape[0], width), 1)
    total = None
    for k in range(count):
        one = jnp.where(lanes == index[:, k : k + 1], 1.0, 0.0)
        total = one if total is None else total + one
    return total.astype(BF16)


def gain_row(small_ref, k):
    return small_ref[GAIN_ROW : GAIN_ROW + 16, :].astype(F32)[k : k + 1, :]


def date_row(small_ref, day):
    table = small_ref[DATE_ROW : DATE_ROW + 16, :].astype(F32)
    lines = lax.broadcasted_iota(jnp.int32, table.shape, 0)
    return jnp.sum(jnp.where(lines == day, table, 0.0), axis=0, keepdims=True)


def columns_of(index):
    short = 8 - index.shape[0]
    if short > 0:
        index = jnp.concatenate([index, jnp.zeros((short, index.shape[1]), index.dtype)], axis=0)
    return jnp.transpose(index)


def count_rows(index, height):
    lines = lax.broadcasted_iota(jnp.int32, (height, index.shape[1]), 0)
    total = None
    for k in range(index.shape[0]):
        one = jnp.where(lines == index[k : k + 1, :], 1.0, 0.0)
        total = one if total is None else total + one
    return total.astype(BF16)


def main_kernel(
    k_pick, day_ref, mesh_ref, sent_ref, left_ref, right_ref, x_ref, y_ref, valid_ref, varw_ref,
    eh_in, eht_in, d_in, dt_in, small_ref, m2_ref, m3_ref, m4_ref, m5_ref, m6_ref,
    slots_ref, gout_ref, gxd_ref, dsum_ref, ggain_ref, loss_ref, dmesh_ref, dhalo_ref,
    gm_ref, out_sem, in_sem, eh_ref, eht_ref, d_ref, dt_ref, ext_ref, t_ref, mm_ref, acc_ref, sender_ref,
):
    nodes = mesh_ref.shape[1]
    table = ext_ref.shape[0]
    variables, points = x_ref.shape[1:]
    k_edge = eh_ref.shape[0] // nodes
    counts = [
        pltpu.make_async_copy(source, target, in_sem.at[k])
        for k, (source, target) in enumerate(
            ((eh_in, eh_ref), (d_in, d_ref), (dt_in, dt_ref), (eht_in, eht_ref))
        )
    ]

    def counts_ready(*which):
        @pl.when(pl.program_id(0) == 0)
        def _():
            for k in which:
                counts[k].wait()

    halo = left_ref.shape[1]

    @pl.when(pl.program_id(0) == 0)
    def _():
        for copy in counts:
            copy.start()
        gm_ref[...] = jnp.zeros_like(gm_ref)
        gout_ref[...] = jnp.zeros_like(gout_ref)
        gxd_ref[...] = jnp.zeros_like(gxd_ref)
        ggain_ref[...] = jnp.zeros_like(ggain_ref)
        loss_ref[...] = jnp.zeros_like(loss_ref)

    sent = sent_ref[0]
    ext_ref[:nodes, :] = sent
    ext_ref[nodes : nodes + halo, :] = left_ref[0]
    ext_ref[nodes + halo :, :] = right_ref[0]
    receivers = 0.5 * dot(sent, m3_ref[0])
    sender_ref[...] = (0.5 * dot(ext_ref[...], m2_ref[0])).astype(BF16)

    counts_ready(0)

    def edge(k, carry):
        hid_sum, t_sum = carry
        rows = pl.ds(pl.multiple_of(k * nodes, nodes), nodes)
        hid, t = silu_parts(1.0 * dot(eh_ref[rows, :], sender_ref[...]) + receivers)
        t_ref[rows, :] = t.astype(t_ref.dtype)
        return hid_sum + hid.astype(BF16).astype(F32), t_sum + t

    zero = jnp.zeros((nodes, LATENT), F32)
    hid_sum, t_sum = lax.fori_loop(0, k_edge, edge, (zero, zero), unroll=k_edge)
    h_high = (hid_sum * (1.0 / k_edge)).astype(BF16)
    gain2 = gain_row(small_ref, 1)
    unit2, scale2 = normalise(dot(h_high, m4_ref[0]))
    mesh2 = mesh_ref[0] + unit2 * gain2
    mm_ref[...] = mesh2.astype(BF16)

    counts_ready(1, 2)
    acc_ref[...] = jnp.zeros_like(acc_ref)
    dsum_ref[...] = jnp.zeros_like(dsum_ref)
    member = pl.program_id(0)
    date = date_row(small_ref, day_ref[member])
    gain3 = gain_row(small_ref, 2)
    wout = small_ref[OUT_ROW : OUT_ROW + variables, :]
    square = (variables, variables)
    same = lax.broadcasted_iota(jnp.int32, square, 0) == lax.broadcasted_iota(jnp.int32, square, 1)
    varw = jnp.sum(jnp.where(same, varw_ref[...], 0.0), axis=1, keepdims=True)

    def decode_part(rows):
        dec = dot(d_ref[rows, :], mm_ref[...])
        a2 = (dec * (1.0 / k_pick)).astype(BF16)
        yield True
        hid, t = silu_parts(0.5 * dot(a2, m5_ref[0]))
        h2 = hid.astype(BF16)
        yield True
        unit, scale = normalise(dot(h2, m6_ref[0]))
        yield True
        x = x_ref[0, :, rows]
        grid = dot_tn(x, small_ref[IN_ROW : IN_ROW + variables, :]) + date + unit * gain3
        grid = grid.astype(BF16)
        yield True
        misfit = x.astype(F32) + dot_nt(wout, grid) - y_ref[0, :, rows].astype(F32)
        valid = valid_ref[pl.ds(member, 1), rows].astype(F32)
        weighted = valid * varw * misfit
        loss_ref[...] += jnp.sum(weighted * misfit, axis=1, keepdims=True)
        dsum_ref[0] += jnp.sum(weighted, axis=1, keepdims=True)
        dp = weighted.astype(BF16)
        gout_ref[...] += dot(dp, grid)
        gxd_ref[...] += dot_nt(x, dp)
        yield True
        dgrid = dot_tn(dp, wout)
        ggain_ref[1:2, :] += jnp.sum(dgrid * unit, axis=0, keepdims=True)
        dc = norm_back(dgrid, gain3, unit, scale).astype(BF16)
        gm_ref[4] += dot_tn(h2, dc)
        yield True
        du = (dot_nt(dc, m6_ref[0]) * t).astype(BF16)
        gm_ref[3] += dot_tn(a2, du)
        yield True
        ddec = dot_nt(du, m5_ref[0]).astype(BF16)
        acc_ref[...] += dot(dt_ref[:, rows], ddec)
        yield True

    def grid_block(i, carry):
        part = BLOCK // PARTS
        in_turn(
            decode_part(pl.ds(pl.multiple_of(i * BLOCK + k * part, part), part)) for k in range(PARTS)
        )
        return carry

    lax.fori_loop(0, points // BLOCK, grid_block, 0)

    counts_ready(3)
    decoder_copy = pltpu.make_async_copy(gm_ref.at[3:5], slots_ref.at[3:5], out_sem.at[0])

    @pl.when(member == pl.num_programs(0) - 1)
    def _():
        decoder_copy.start()

    dmesh2 = acc_ref[...] * (1.0 / k_pick)
    ggain_ref[0:1, :] += jnp.sum(dmesh2 * unit2, axis=0, keepdims=True)
    dagg = norm_back(dmesh2, gain2, unit2, scale2).astype(BF16)
    gm_ref[2] += dot_tn(h_high, dagg)
    dhid = dot_nt(dagg, m4_ref[0]) * (1.0 / k_edge)
    dr = (dhid * t_sum).astype(BF16)
    gm_ref[1] += dot_tn(sent, dr)

    def edge_back(k, total):
        rows = pl.ds(pl.multiple_of(k * nodes, nodes), nodes)
        dpre = (dhid * t_ref[rows, :].astype(F32)).astype(BF16)
        return total + dot(eht_ref[:, rows], dpre)

    ds = lax.fori_loop(
        0, k_edge, edge_back, jnp.zeros((table, LATENT), F32), unroll=k_edge
    ).astype(BF16)
    gm_ref[0] += dot_tn(ext_ref[...], ds)
    dext = dot_nt(ds, m2_ref[0])
    dmesh_ref[0] = dmesh2 + dext[:nodes, :] + dot_nt(dr, m3_ref[0])
    dhalo_ref[0] = dext[nodes:, :].astype(BF16)

    @pl.when(member == pl.num_programs(0) - 1)
    def _():
        copy = pltpu.make_async_copy(gm_ref.at[0:3], slots_ref.at[0:3], out_sem.at[1])
        copy.start()
        copy.wait()
        decoder_copy.wait()


def main_scratch(k_edge, nodes, points, table):
    return [
        pltpu.VMEM((5, LATENT, LATENT), F32),
        pltpu.SemaphoreType.DMA((2,)),
        pltpu.SemaphoreType.DMA((4,)),
        pltpu.VMEM((k_edge * nodes, table), BF16),
        pltpu.VMEM((table, k_edge * nodes), BF16),
        pltpu.VMEM((points, nodes), BF16),
        pltpu.VMEM((nodes, points), BF16),
        pltpu.VMEM((table, LATENT), BF16),
        pltpu.VMEM((k_edge * nodes, LATENT), T_TYPE),
        pltpu.VMEM((nodes, LATENT), BF16),
        pltpu.VMEM((nodes, LATENT), F32),
        pltpu.VMEM((table, LATENT), BF16),
    ]


def whole(shape):
    return pl.BlockSpec(shape, lambda m: (0,) * len(shape), pipeline_mode=pl.Buffered(1))


def per_member(shape):
    return pl.BlockSpec((1,) + shape, lambda m: (m, 0, 0))


def call(kernel, members, in_specs, out_shapes, out_specs, scratch, cost, aliases=None):
    return pl.pallas_call(
        kernel,
        grid=(members,),
        in_specs=in_specs,
        out_shape=out_shapes,
        out_specs=out_specs,
        scratch_shapes=scratch,
        input_output_aliases=aliases or {},
        compiler_params=pltpu.CompilerParams(
            dimension_semantics=("arbitrary",), vmem_limit_bytes=VMEM_BYTES
        ),
        cost_estimate=pl.CostEstimate(flops=cost, bytes_accessed=32 << 20, transcendentals=0),
    )


def shape_of(shape, dtype):
    return jax.ShapeDtypeStruct(shape, dtype)


def slot_of(matrix):
    return 2 * matrix - 5 * ((matrix + 1) // 4)


def neighbours():
    region = lax.axis_index("region")
    slot = lax.rem(region, SLOTS)
    base = region - slot
    one = lax.rem(slot, 2)
    two = lax.rem(slot // 2, 2)
    four = slot // 4
    core = slot + 1 - 2 * one
    side = slot + 2 - 4 * two
    up = slot + 4 - 8 * four
    far = side + 4 - 8 * four
    return base, slot, core, side, up, far


def remote(source, target, send, receive, where):
    return pltpu.make_async_remote_copy(
        src_ref=source, dst_ref=target, send_sem=send, recv_sem=receive,
        device_id=where, device_id_type=MESH,
    )


def greet(places):
    barrier = pltpu.get_barrier_semaphore()
    for place in places:
        pl.semaphore_signal(barrier, inc=1, device_id=place, device_id_type=MESH)


def greeted(places):
    pl.semaphore_wait(pltpu.get_barrier_semaphore(), len(places))


def around():
    region, count = lax.axis_index("region"), lax.axis_size("region")
    following, previous = lax.rem(region + 1, count), lax.rem(region + count - 1, count)
    return {"region": following}, {"region": previous}


def encode_kernel(
    depth, day_ref, matrices_ref, in_ref, outp_ref, gains_ref, dates_ref, valid_ref, x_ref, picks_ref,
    rows_ref, edge_ref, near_ref,
    full_ref, small_out_ref, total_ref, x4_out, a0_out, h1_out, t1_out, unit_out, scale_out, mesh_out,
    sent_out, left_ref, right_ref, eh_out, eht_out, d_out, dt_out,
    edge_cols_ref, grid_cols_ref, eh_ref, eht_ref, d_ref, dt_ref, block_ref, pack_ref, pick_ref, out_ref, x4_ref, xl_ref, a0_ref, h1_ref, t1_ref, unit_ref, scale_ref,
    mesh_ref, sent_ref, buf_ref, w_ref, small_ref, count_ref, counts_ref, sums_ref, heard_ref,
    local_sem, z_send, z_recv, p_send, p_recv, d_send, d_recv, c_send, c_recv, n_send, n_recv,
    s_send, s_recv, w_sem, o_sem, e_send, e_recv, q_sem, b_sem,
):
    base, slot, core, side, up, far = neighbours()
    z = lax.axis_index("row")
    half = block_ref.shape[1] // 2
    low, high = pl.ds(0, half), pl.ds(half, half)
    to_core, to_side, to_up = ({"region": base + place} for place in (core, side, up))
    to_next, to_previous = around()
    to_z = [None] + [{"row": lax.rem(z + d, depth)} for d in range(1, depth)]
    steps = range(1, depth)
    members, variables, points = x_ref.shape
    nodes = a0_ref.shape[1]
    halo = left_ref.shape[1]
    peers = to_z[1:] + [to_core, to_side, to_up, to_next, to_previous]
    greet(peers)

    def at(d):
        return lax.rem(z + depth - d, depth)

    def arrived(target, receive):
        remote(target, target, receive, receive, to_core).wait_recv()

    def gone(origin, receive):
        remote(origin, origin, receive, receive, to_core).wait_send()

    for k in range(SLOTS - 1):
        block_ref[slot_of(k)] = matrices_ref[k].astype(BF16)
    pack_ref[...] = jnp.zeros_like(pack_ref)
    pack_ref[IN_ROW : IN_ROW + variables, :] = in_ref[...]
    pack_ref[OUT_ROW : OUT_ROW + variables, :] = outp_ref[...]
    pack_ref[GAIN_ROW : GAIN_ROW + gains_ref.shape[0], :] = gains_ref[...]
    pack_ref[DATE_ROW : DATE_ROW + dates_ref.shape[0], :] = dates_ref[...]
    block_ref[SMALL] = jnp.transpose(pack_ref[...]).astype(BF16)
    own = pltpu.make_async_copy(block_ref, full_ref.at[:, z], local_sem)
    own.start()
    table, k_edge, k_near = eht_ref.shape[0], edge_ref.shape[0], near_ref.shape[0]
    k_grid = picks_ref.shape[0]
    wide = 128
    pieces = nodes // wide
    edge_cols_ref[...] = columns_of(edge_ref[...])
    grid_cols_ref[...] = columns_of(picks_ref[...])

    def build_edges(i, carry):
        k, piece = i // pieces, lax.rem(i, pieces)
        inside = pl.ds(pl.multiple_of(piece * wide, wide), wide)
        across = pl.ds(pl.multiple_of(i * wide, wide), wide)
        columns = edge_cols_ref[inside, :].astype(F32)
        chosen = lax.broadcasted_iota(jnp.int32, columns.shape, 1) == k
        column = jnp.sum(jnp.where(chosen, columns, 0.0), axis=1, keepdims=True).astype(jnp.int32)
        eh_ref[across, :] = count_columns(column, table, 1)
        lines = edge_ref[:, inside].astype(F32)
        chosen = lax.broadcasted_iota(jnp.int32, lines.shape, 0) == k
        line = jnp.sum(jnp.where(chosen, lines, 0.0), axis=0, keepdims=True).astype(jnp.int32)
        eht_ref[:, across] = count_rows(line, table)
        return carry

    def build_near(i, carry):
        inside = pl.ds(pl.multiple_of(i * wide, wide), wide)
        near = near_ref[:, inside]
        d_ref[inside, :] = count_columns(columns_of(near), nodes, k_near)
        dt_ref[:, inside] = count_rows(near, nodes)
        return carry

    def build_grid(i, carry):
        inside = pl.ds(pl.multiple_of(i * 64, 64), 64)
        pick_ref[inside, :] = count_columns(grid_cols_ref[inside, :], points, k_grid)
        return carry

    valid = jnp.sum(valid_ref[...].astype(F32), axis=1, keepdims=True)
    valid = jnp.sum(valid, axis=0, keepdims=True)
    count_ref[...] = jnp.broadcast_to(valid, count_ref.shape)
    out_ref[...] = count_columns(columns_of(rows_ref[...]), nodes, 1)
    greeted(peers)
    for d in steps:
        remote(
            block_ref.at[slot], full_ref.at[slot, z], z_send.at[d], z_recv.at[d], to_z[d]
        ).start()
    for d in steps:
        remote(count_ref, counts_ref.at[d], n_send.at[d], n_recv.at[d], to_z[d]).start()

    lax.fori_loop(0, nodes // 64, build_grid, 0)
    edges, nears = k_edge * pieces, points // wide
    first = edges // 4
    share = -(-(edges - first) // (2 * depth - 2))

    def some_edges(i):
        return lax.fori_loop(
            first + i * share, jnp.minimum(first + (i + 1) * share, edges), build_edges, 0
        )

    lax.fori_loop(0, first, build_edges, 0)

    def from_z(d, carry):
        chunk = full_ref.at[slot, at(d)]
        arrived(chunk, z_recv.at[d])
        remote(chunk, chunk, p_send.at[0, d], p_recv.at[0, d], to_side).start()
        remote(chunk, chunk, p_send.at[1, d], p_recv.at[1, d], to_up).start()
        remote(chunk, chunk, c_send.at[0, d], c_recv.at[0, d], to_core).start()
        some_edges(d - 1)
        return carry

    lax.fori_loop(1, depth, from_z, 0)
    builds = [
        pltpu.make_async_copy(ref, target, b_sem.at[k])
        for k, (ref, target) in enumerate(
            ((eh_ref, eh_out), (eht_ref, eht_out), (d_ref, d_out), (dt_ref, dt_out))
        )
    ]

    total = count_ref[...]
    for d in steps:
        arrived(counts_ref.at[d], n_recv.at[d])
        total = total + counts_ref[d]
    sums_ref[0] = total
    partners = (to_core, to_side, to_up)

    def count_copy(step):
        return remote(
            sums_ref.at[step], heard_ref.at[step], s_send.at[step], s_recv.at[step], partners[step]
        )

    count_copy(0).start()

    def from_sides(d, carry):
        chunk = full_ref.at[side, at(d)]
        arrived(chunk, p_recv.at[0, d])
        part = full_ref.at[side, at(d), low]
        remote(part, part, d_send.at[0, d], d_recv.at[0, d], to_up).start()
        remote(chunk, chunk, c_send.at[1, d], c_recv.at[1, d], to_core).start()
        chunk = full_ref.at[up, at(d)]
        arrived(chunk, p_recv.at[1, d])
        part = full_ref.at[up, at(d), high]
        remote(part, part, d_send.at[1, d], d_recv.at[1, d], to_side).start()
        remote(chunk, chunk, c_send.at[2, d], c_recv.at[2, d], to_core).start()
        some_edges(depth - 2 + d)
        return carry

    lax.fori_loop(1, depth, from_sides, 0)
    builds[0].start()
    builds[1].start()

    def gather_inputs(m, carry):
        x4 = dot_nt(pick_ref[...], x_ref[m]) * (1.0 / k_grid)
        top, rest = split_two(x4)
        x4_ref[m] = top
        xl_ref[m] = rest
        return carry

    lax.fori_loop(0, members, gather_inputs, 0)
    for step in (1, 2):
        count_copy(step - 1).wait_recv()
        total = total + heard_ref[step - 1]
        sums_ref[step] = total
        count_copy(step).start()

    def from_far(d, carry):
        arrived(full_ref.at[far, at(d), low], d_recv.at[0, d])
        arrived(full_ref.at[far, at(d), high], d_recv.at[1, d])
        chunk = full_ref.at[far, at(d)]
        remote(chunk, chunk, c_send.at[3, d], c_recv.at[3, d], to_core).start()
        return carry

    lax.fori_loop(1, depth, from_far, 0)
    lax.fori_loop(0, nears, build_near, 0)
    builds[2].start()
    builds[3].start()
    count_copy(2).wait_recv()
    total_ref[...] = total + heard_ref[2]

    def from_core(d, carry):
        for k in range(4):
            arrived(full_ref.at[core, at(d)], c_recv.at[k, d])
        return carry

    lax.fori_loop(1, depth, from_core, 0)
    own.wait()

    loads = [
        pltpu.make_async_copy(full_ref.at[j], w_ref.at[k], w_sem.at[k])
        for k, j in enumerate((SMALL, slot_of(0), slot_of(1)))
    ]
    for copy in loads:
        copy.start()
    for copy in loads:
        copy.wait()
    small_ref[...] = jnp.transpose(w_ref[0].reshape(LATENT, LATENT))
    small_copy = pltpu.make_async_copy(small_ref, small_out_ref, q_sem)
    small_copy.start()
    kept = (
        (x4_ref, x4_out), (a0_ref, a0_out), (h1_ref, h1_out), (t1_ref, t1_out), (unit_ref, unit_out),
        (scale_ref, scale_out), (mesh_ref, mesh_out), (sent_ref, sent_out),
    )

    def kept_copies(m):
        return [
            pltpu.make_async_copy(ref.at[m], target.at[m], o_sem.at[k, m])
            for k, (ref, target) in enumerate(kept)
        ]

    def halo_copies(m):
        return [
            remote(buf_ref.at[m, halo:], left_ref.at[m], e_send.at[0, m], e_recv.at[0, m], to_next),
            remote(buf_ref.at[m, :halo], right_ref.at[m], e_send.at[1, m], e_recv.at[1, m], to_previous),
        ]

    def encode_member(m, carry):
        win = small_ref[IN_ROW : IN_ROW + variables, :]
        agg = dot(x4_ref[m], win) + dot(xl_ref[m], win) + date_row(small_ref, day_ref[m])
        a0 = agg.astype(BF16)
        hid, t1 = silu_parts(0.5 * dot(a0, w_ref[1].reshape(LATENT, LATENT)))
        h1 = hid.astype(BF16)
        unit, scale = normalise(dot(h1, w_ref[2].reshape(LATENT, LATENT)))
        mesh = agg + unit * gain_row(small_ref, 0)
        low_mesh = mesh.astype(BF16)
        buf_ref[m] = dot(out_ref[...], low_mesh).astype(BF16)
        for copy in halo_copies(m):
            copy.start()
        a0_ref[m] = a0
        h1_ref[m] = h1
        t1_ref[m] = t1.astype(BF16)
        unit_ref[m] = unit
        scale_ref[m] = scale
        mesh_ref[m] = mesh
        sent_ref[m] = low_mesh
        for copy in kept_copies(m):
            copy.start()
        return carry

    lax.fori_loop(0, members, encode_member, 0)

    def finish_member(m, carry):
        for copy in halo_copies(m) + kept_copies(m):
            copy.wait()
        return carry

    def finish_row(d, carry):
        gone(block_ref.at[slot], z_send.at[d])
        gone(count_ref, n_send.at[d])
        chunk = full_ref.at[slot, at(d)]
        for k in range(2):
            gone(chunk, p_send.at[k, d])
            gone(full_ref.at[slot, at(d), low], d_send.at[k, d])
        for k in range(4):
            gone(chunk, c_send.at[k, d])
        return carry

    lax.fori_loop(0, members, finish_member, 0)
    lax.fori_loop(1, depth, finish_row, 0)
    for step in range(3):
        count_copy(step).wait_send()
    for copy in builds:
        copy.wait()
    small_copy.wait()


def encode(
    day, matrices, in_proj, out_proj, gains, dates, valid, inputs, picks, rows, edges, near, depth
):
    hbm = pl.BlockSpec(memory_space=pl.ANY)
    vmem = pl.BlockSpec(memory_space=pltpu.VMEM)
    dma = pltpu.SemaphoreType.DMA
    members, variables, points = inputs.shape
    nodes = picks.shape[1]
    halo = rows.shape[1] // 2
    share = matrices.shape[1]
    nodes_of = (members, nodes, LATENT)
    table, pairs = nodes + 2 * halo, edges.shape[0] * nodes
    counts = ((pairs, table), (table, pairs), (points, nodes), (nodes, points))
    kept = [
        ((members, nodes, variables), BF16),
        (nodes_of, BF16),
        (nodes_of, BF16),
        (nodes_of, BF16),
        (nodes_of, F32),
        ((members, nodes, 1), F32),
        (nodes_of, F32),
        (nodes_of, BF16),
    ]
    return pl.pallas_call(
        partial(encode_kernel, depth),
        in_specs=[pl.BlockSpec(memory_space=pltpu.SMEM)] + [vmem] * 11,
        out_shape=[
            shape_of((SLOTS, depth, share, LATENT), BF16),
            shape_of((LATENT, LATENT), BF16),
            shape_of((8, 128), F32),
            *(shape_of(*one) for one in kept),
            shape_of((members, halo, LATENT), BF16),
            shape_of((members, halo, LATENT), BF16),
            *(shape_of(one, BF16) for one in counts),
        ],
        out_specs=[hbm, hbm, vmem] + [hbm] * (len(kept) + 2 + len(counts)),
        scratch_shapes=[
            pltpu.VMEM((nodes, 8), jnp.int32),
            pltpu.VMEM((nodes, 8), jnp.int32),
            *(pltpu.VMEM(one, BF16) for one in counts),
            pltpu.VMEM((SLOTS, share, LATENT), BF16),
            pltpu.VMEM((LATENT, share), F32),
            pltpu.VMEM((nodes, points), BF16),
            pltpu.VMEM((2 * halo, nodes), BF16),
            pltpu.VMEM(*kept[0]),
            *(pltpu.VMEM(*one) for one in kept),
            pltpu.VMEM((members, 2 * halo, LATENT), BF16),
            pltpu.VMEM((3, depth, share, LATENT), BF16),
            pltpu.VMEM((LATENT, LATENT), BF16),
            pltpu.VMEM((8, 128), F32),
            pltpu.VMEM((depth, 8, 128), F32),
            pltpu.VMEM((3, 8, 128), F32),
            pltpu.VMEM((3, 8, 128), F32),
            dma,
            dma((depth,)),
            dma((depth,)),
            dma((2, depth)),
            dma((2, depth)),
            dma((2, depth)),
            dma((2, depth)),
            dma((4, depth)),
            dma((4, depth)),
            dma((depth,)),
            dma((depth,)),
            dma((3,)),
            dma((3,)),
            dma((3,)),
            dma((len(kept), members)),
            dma((2, members)),
            dma((2, members)),
            dma,
            dma((len(counts),)),
        ],
        compiler_params=pltpu.CompilerParams(
            collective_id=0, has_side_effects=True, vmem_limit_bytes=VMEM_BYTES
        ),
    )(
        day, matrices, in_proj, out_proj, gains, dates, valid, inputs, picks, rows, edges, near
    )


def reduce_kernel(
    depth, day_ref, late_ref, momentum_in, count_ref, dmesh_in, dhalo_ref, rows_ref, x4_in, a0_in,
    h1_in, t1_in, unit_in, scale_in, weights_ref, small_ref, gxd_ref, dsum_ref, gout_ref, ggain_ref,
    loss_ref,
    g_ref, x_ref,
    momentum_ref, dmesh_ref, ret_ref, x4_ref, a0_ref, h1_ref, t1_ref, unit_ref, scale_ref, m_ref, back_ref, pack_ref,
    early_ref, own_ref, heard_ref, snd_ref, rcv_ref, snd_low_ref, rcv_low_ref, acc_ref, zr_ref,
    g_own_ref, mb_ref, x_own_ref,
    i_sem, e_send, e_recv, l_sem, h_send, h_recv, p_send, p_recv, q_send, q_recv, z_send, z_recv,
    m_send, m_recv, g_local, g_send, g_recv, x_local, x_send, x_recv,
):
    base, slot, core, side, up, far = neighbours()
    z = lax.axis_index("row")
    rows = acc_ref.shape[0] // depth
    chips = SLOTS // 2
    mine = slot // 2
    parity = lax.rem(slot, 2)
    members, variables = x4_ref.shape[0], x4_ref.shape[2]
    halo = dhalo_ref.shape[1] // 2
    to_core, to_side, to_up, to_far = ({"region": base + place} for place in (core, side, up, far))
    to_next, to_previous = around()
    to_place = (to_far, to_side, to_up)
    places = (far, side, up)
    to_z = [None] + [{"row": lax.rem(z + d, depth)} for d in range(1, depth)]
    peers = to_z[1:] + [to_core, to_side, to_up, to_far, to_next, to_previous]
    greet(peers)
    sent = []

    def both_ends(i):
        return lax.rem(i * (depth - 1), depth)

    def part_of(b):
        return pl.ds(pl.multiple_of(b * rows, rows), rows)

    def send(*args):
        copy = remote(*args)
        copy.start()
        sent.append(copy)

    def arrived(target, receive):
        remote(target, target, receive, receive, to_core).wait_recv()

    def load(*args):
        copy = pltpu.make_async_copy(*args)
        copy.start()
        return copy

    def halo_copies(m):
        return [
            remote(dhalo_ref.at[m, halo:], ret_ref.at[m, :halo], e_send.at[0, m], e_recv.at[0, m], to_next),
            remote(
                dhalo_ref.at[m, :halo], ret_ref.at[m, halo:], e_send.at[1, m], e_recv.at[1, m], to_previous
            ),
        ]

    inner = ((dmesh_in, dmesh_ref), (x4_in, x4_ref), (a0_in, a0_ref), (h1_in, h1_ref), (t1_in, t1_ref),
             (unit_in, unit_ref), (scale_in, scale_ref))

    def inner_loads(m):
        return [
            pltpu.make_async_copy(ref.at[m], target.at[m], i_sem.at[k, m])
            for k, (ref, target) in enumerate(inner)
        ]

    for m in range(members):
        for copy in inner_loads(m):
            copy.start()
    m_loads = [
        load(momentum_in.at[mine + (SLOTS // 2 - 1) * parity], momentum_ref, i_sem.at[len(inner) + 1, 0])
    ]
    first = load(late_ref.at[0], early_ref.at[2], i_sem.at[len(inner), 0])
    for k in range(2):
        m_loads.append(load(weights_ref.at[slot_of(k)], m_ref.at[k], i_sem.at[len(inner), 1 + k]))

    def late_copy(chip):
        return remote(
            late_ref.at[1 + chip], heard_ref.at[chip], h_send.at[chip, 0], h_recv.at[chip, 0], to_core
        )

    def late_load(chip):
        return pltpu.make_async_copy(late_ref.at[1 + chip], own_ref.at[chip], l_sem.at[chip])

    def early_copy(chip, b):
        return remote(
            early_ref.at[chip, part_of(b)], heard_ref.at[chip, part_of(b)], h_send.at[chip, b],
            h_recv.at[chip, b], to_core,
        )

    def low_copy(b):
        return remote(
            snd_low_ref.at[part_of(b)], rcv_low_ref.at[mine, part_of(b)], q_send.at[b], q_recv.at[mine, b],
            {"region": base + SMALL},
        )

    def chip_copy(chip, b):
        return remote(
            snd_ref.at[chip, part_of(b)], rcv_ref.at[mine, part_of(b)], p_send.at[chip, b],
            p_recv.at[mine, b], {"region": base + 2 * chip + parity},
        )

    def pass_on(chip, b, own):
        part = part_of(b)
        total = own[chip, part, :] + heard_ref[chip, part, :]

        @pl.when(mine == chip)
        def _():
            acc_ref[part, :] = total

        @pl.when(mine != chip)
        def _():
            snd_ref[chip, part, :] = total.astype(BF16)
            chip_copy(chip, b).start()

    def pass_late(chip):
        @pl.when(parity == 1)
        def _():
            late_load(chip).wait()
            late_copy(chip).wait_recv()

            def piece(b, carry):
                pass_on(chip, b, own_ref)
                return carry

            lax.fori_loop(0, depth, piece, 0)

    def pass_early(i, carry):
        b = both_ends(i)

        @pl.when(parity == 0)
        def _():
            def piece(chip, carry):
                early_copy(chip, b).wait_recv()
                pass_on(chip, b, early_ref)
                return carry

            lax.fori_loop(0, chips, piece, 0)

        return carry

    def pass_low(b, carry):
        part = part_of(b)
        total = early_ref[SMALL // 2, part, :] + heard_ref[SMALL // 2, part, :]
        snd_low_ref[part, :] = (total - total.astype(BF16).astype(F32)).astype(BF16)
        low_copy(b).start()
        return carry

    @pl.when(parity == 1)
    def _():
        for chip in range(chips):
            late_load(chip).start()

    lines = lax.broadcasted_iota(jnp.int32, (16, LATENT), 0)
    back_ref[...] = count_rows(rows_ref[...], back_ref.shape[0])
    wout = small_ref[OUT_ROW : OUT_ROW + variables, :]
    pack_ref[...] = jnp.zeros_like(pack_ref)
    top, rest = split_two(gxd_ref[...])
    pack_ref[IN_ROW : IN_ROW + variables, :] = dot(top, wout) + dot(rest, wout)
    pack_ref[OUT_ROW : OUT_ROW + variables, :] = gout_ref[...]
    pack_ref[GAIN_ROW + 1 : GAIN_ROW + 3, :] = ggain_ref[...]
    loss = jnp.sum(loss_ref[...], axis=0, keepdims=True)
    pack_ref[LOSS_ROW : LOSS_ROW + 1, :] = jnp.broadcast_to(loss, (1, LATENT))
    early_ref[0:2] = jnp.zeros((2, LATENT, LATENT), F32)
    greeted(peers)
    for m in range(members):
        for copy in halo_copies(m):
            copy.start()

    @pl.when(parity == 0)
    def _():
        for chip in range(chips):
            late_copy(chip).start()

    for copy in m_loads:
        copy.wait()

    def member_back(m, carry):
        for copy in inner_loads(m):
            copy.wait()
        for copy in halo_copies(m):
            copy.wait()
        dmesh = dmesh_ref[m] + dot(back_ref[...], ret_ref[m])
        unit = unit_ref[m]
        pack_ref[GAIN_ROW : GAIN_ROW + 1, :] += jnp.sum(dmesh * unit, axis=0, keepdims=True)
        dc = norm_back(dmesh, gain_row(small_ref, 0), unit, scale_ref[m]).astype(BF16)
        early_ref[1] += dot_tn(h1_ref[m], dc)
        du = (dot_nt(dc, m_ref[1]) * t1_ref[m].astype(F32)).astype(BF16)
        early_ref[0] += dot_tn(a0_ref[m], du)
        dagg = dmesh + dot_nt(du, m_ref[0])
        pack_ref[IN_ROW : IN_ROW + variables, :] += dot_tn(x4_ref[m], dagg.astype(BF16))
        top, rest = split_two(dsum_ref[m])
        date = jnp.sum(dagg, axis=0, keepdims=True) + dot_tn(top, wout) + dot_tn(rest, wout)
        pack_ref[DATE_ROW : DATE_ROW + 16, :] += jnp.where(lines == day_ref[m], date, 0.0)

        @pl.when(m < chips)
        def _():
            pass_late(m)

        return carry

    lax.fori_loop(0, members, member_back, 0)
    for chip in range(members, chips):
        pass_late(chip)
    early_ref[SMALL // 2] = jnp.transpose(pack_ref[...])
    first.wait()

    @pl.when(parity == 1)
    def _():
        for i in range(depth):
            for chip in range(chips):
                early_copy(chip, i * (depth - 1) % depth).start()

    lax.fori_loop(0, depth, pass_early, 0)

    @pl.when((mine != SMALL // 2) & (parity == 0))
    def _():
        lax.fori_loop(0, depth, pass_low, 0)

    sources = [lax.rem(mine + i, chips) for i in range(1, chips)]
    def z_copy(b):
        d = lax.rem(b - z + depth, depth)
        return remote(acc_ref.at[part_of(b)], zr_ref.at[d], z_send.at[b], z_recv.at[d], {"row": b + 0 * z})

    def across_z(i, carry):
        b = both_ends(i)
        part = part_of(b)
        total = acc_ref[part, :]
        for c in sources:
            arrived(rcv_ref.at[c, part], p_recv.at[c, b])
            total = total + rcv_ref[c, part, :].astype(F32)
        acc_ref[part, :] = total

        @pl.when(slot == SMALL)
        def _():
            low = acc_ref[part, :]
            for c in sources:
                arrived(rcv_low_ref.at[c, part], q_recv.at[c, b])
                low = low + rcv_low_ref[c, part, :].astype(F32)
            acc_ref[part, :] = low

        @pl.when(z != b)
        def _():
            z_copy(b).start()

        return carry

    lax.fori_loop(0, depth, across_z, 0)
    zr_ref[0] = acc_ref[pl.ds(pl.multiple_of(z * rows, rows), rows), :]
    for d in range(1, depth):
        arrived(zr_ref.at[d], z_recv.at[d])
    g_own = zr_ref[z]
    for place in range(1, depth):
        g_own = g_own + zr_ref[lax.rem(z + depth - place, depth)]
    g_own_ref[...] = g_own
    momentum = (
        MUON_MOMENTUM * momentum_ref[...]
        + (2.0 / count_ref[0:1, 0:1]) * g_own
    )
    mb_ref[0] = momentum.astype(BF16)
    for d in range(1, depth):
        send(mb_ref.at[0], mb_ref.at[d], m_send.at[d], m_recv.at[d], to_z[d])
    g_copy = load(g_own_ref, g_ref.at[slot], g_local)
    for k in range(3):
        send(g_own_ref, g_ref.at[slot], g_send.at[k], g_recv.at[k], to_place[k])
    send(g_own_ref, g_ref.at[slot], g_send.at[3], g_recv.at[3], to_core)

    for d in range(1, depth):
        arrived(mb_ref.at[d], m_recv.at[d])
    everything = jnp.concatenate([mb_ref[d] for d in range(depth)], axis=0)
    wide = everything.astype(F32)
    squares = jnp.sum(jnp.sum(wide * wide, axis=1, keepdims=True), axis=0, keepdims=True)
    inverse = lax.rsqrt(squares + 1e-07)
    turn = momentum * inverse
    current = (wide * inverse).astype(BF16)
    turn_low = turn.astype(BF16)
    for sweep in range(NS_ITERS):
        gram = dot_tn(current, current)
        gram_low = gram.astype(BF16)
        mixing = NS_COEFFS[1] * gram + NS_COEFFS[2] * dot(gram_low, gram_low)
        mixing = mixing.astype(BF16)
        turn = NS_COEFFS[0] * turn + dot(turn_low, mixing)
        turn_low = turn.astype(BF16)
        if sweep < NS_ITERS - 1:
            current = (NS_COEFFS[0] * current.astype(F32) + dot(current, mixing)).astype(BF16)
    x_own_ref[...] = turn_low
    x_copy = pltpu.make_async_copy(x_own_ref, x_ref.at[slot], x_local)
    x_copy.start()
    for k in range(3):
        send(x_own_ref, x_ref.at[slot], x_send.at[k], x_recv.at[k], to_place[k])
    send(x_own_ref, x_ref.at[slot], x_send.at[3], x_recv.at[3], to_core)

    for target, send_sem, recv_sem in ((g_ref, g_send, g_recv), (x_ref, x_send, x_recv)):
        for k in range(3):
            chunk = target.at[places[k]]
            arrived(chunk, recv_sem.at[k])
            send(chunk, chunk, send_sem.at[4 + k], recv_sem.at[4 + k], to_core)
    for target, recv_sem in ((g_ref, g_recv), (x_ref, x_recv)):
        for k in range(3, 7):
            arrived(target.at[core], recv_sem.at[k])
    for copy in sent:
        copy.wait_send()
    @pl.when(parity == 0)
    def _():
        for chip in range(chips):
            late_copy(chip).wait_send()

    @pl.when(parity == 1)
    def _():
        for b in range(depth):
            for chip in range(chips):
                early_copy(chip, b).wait_send()

    for b in range(depth):
        for chip in range(chips):

            @pl.when(mine != chip)
            def _():
                chip_copy(chip, b).wait_send()

        @pl.when((mine != SMALL // 2) & (parity == 0))
        def _():
            low_copy(b).wait_send()

        @pl.when(z != b)
        def _():
            z_copy(b).wait_send()

    g_copy.wait()
    x_copy.wait()


def reduce_gradients(
    day, late, momentum, count, dmesh, dhalo, rows, kept, weights, small, gxd, dsum, gout, ggain, loss,
    depth,
):
    hbm = pl.BlockSpec(memory_space=pl.ANY)
    vmem = pl.BlockSpec(memory_space=pltpu.VMEM)
    dma = pltpu.SemaphoreType.DMA
    members, nodes, width = dmesh.shape
    height = LATENT
    share = height // depth
    halo = dhalo.shape[1]
    chips = SLOTS // 2

    return pl.pallas_call(
        partial(reduce_kernel, depth),
        in_specs=[pl.BlockSpec(memory_space=pltpu.SMEM), hbm, hbm, vmem, hbm, vmem, vmem]
        + [hbm] * len(kept)
        + [hbm]
        + [vmem] * 6,
        out_shape=[
            shape_of((SLOTS, share, width), F32),
            shape_of((SLOTS, share, width), BF16),
        ],
        out_specs=[hbm, hbm],
        scratch_shapes=[
            pltpu.VMEM((share, width), F32),
            pltpu.VMEM(dmesh.shape, F32),
            pltpu.VMEM(dhalo.shape, BF16),
            *(pltpu.VMEM(one.shape, one.dtype) for one in kept),
            pltpu.VMEM((2, height, width), BF16),
            pltpu.VMEM((nodes, halo), BF16),
            pltpu.VMEM((height, width), F32),
            pltpu.VMEM((4, height, width), F32),
            pltpu.VMEM((chips, height, width), F32),
            pltpu.VMEM((chips, height, width), F32),
            pltpu.VMEM((chips, height, width), BF16),
            pltpu.VMEM((chips, height, width), BF16),
            pltpu.VMEM((height, width), BF16),
            pltpu.VMEM((chips, height, width), BF16),
            pltpu.VMEM((height, width), F32),
            pltpu.VMEM((depth, share, width), F32),
            pltpu.VMEM((share, width), F32),
            pltpu.VMEM((depth, share, width), BF16),
            pltpu.VMEM((share, width), BF16),
            dma((len(kept) + 3, members)),
            dma((2, members)),
            dma((2, members)),
            dma((chips,)),
            dma((chips, depth)),
            dma((chips, depth)),
            dma((chips, depth)),
            dma((chips, depth)),
            dma((depth,)),
            dma((chips, depth)),
            dma((depth,)),
            dma((depth,)),
            dma((depth,)),
            dma((depth,)),
            dma,
            dma((7,)),
            dma((7,)),
            dma,
            dma((7,)),
            dma((7,)),
        ],
        compiler_params=pltpu.CompilerParams(
            collective_id=1, has_side_effects=True, vmem_limit_bytes=VMEM_BYTES
        ),
    )(
        day, late, momentum, count, dmesh, dhalo, rows, *kept, weights, small, gxd, dsum, gout,
        ggain, loss,
    )


def turn_whole(sums, count, momentum):
    blocks = jnp.stack([sums[slot_of(k)] for k in range(SLOTS - 1)])
    blocks = MUON_MOMENTUM * momentum + (2.0 / count[0, 0]) * blocks
    squares = lax.psum(jnp.sum(blocks * blocks, axis=(1, 2)), "row")
    current = blocks * lax.rsqrt(squares + 1e-07)[:, None, None]

    def product(expression, left, right):
        return jnp.einsum(expression, left, right, precision=lax.Precision.HIGHEST)

    for _ in range(NS_ITERS):
        gram = lax.psum(product("mrk,mrl->mkl", current, current), "row")
        mixing = NS_COEFFS[1] * gram + NS_COEFFS[2] * product("mkj,mjl->mkl", gram, gram)
        current = NS_COEFFS[0] * current + product("mrk,mkl->mrl", current, mixing)
    current = current.astype(BF16)
    by_slot = {slot_of(k): current[k] for k in range(SLOTS - 1)}
    return jnp.stack([by_slot.get(k, current[0]) for k in range(SLOTS)])


def finish_kernel(
    g_ref, rest_ref, x_ref, count_ref, matrix_ref, momentum_ref,
    in_ref, in1_ref, in2_ref, out_ref, out1_ref, out2_ref, gain_ref, gain1_ref, gain2_ref,
    date_ref, date1_ref, date2_ref,
    new_matrix_ref, new_momentum_ref,
    nin_ref, nin1_ref, nin2_ref, nout_ref, nout1_ref, nout2_ref, ngain_ref, ngain1_ref, ngain2_ref,
    ndate_ref, ndate1_ref, ndate2_ref, loss_ref, valid_ref,
):
    scale = 2.0 / count_ref[0:1, 0:1]
    new_momentum_ref[...] = MUON_MOMENTUM * momentum_ref[...] + scale * g_ref[...]
    new_matrix_ref[...] = (
        matrix_ref[...] * (1.0 - MUON_RATE * WEIGHT_DECAY) - MUON_RATE * x_ref[...].astype(F32)
    )

    @pl.when(pl.program_id(0) == pl.num_programs(0) // 2)
    def _():
        rest = jnp.transpose(rest_ref[0])
        loss_ref[0, 0] = jnp.sum(rest[LOSS_ROW : LOSS_ROW + 1, 0:1])
        valid_ref[0, 0] = jnp.sum(count_ref[0:1, 0:1])
        rest = rest * scale
        for row, rate, decay, old, new in (
            (IN_ROW, MATRIX_RATE, WEIGHT_DECAY, (in_ref, in1_ref, in2_ref), (nin_ref, nin1_ref, nin2_ref)),
            (OUT_ROW, MATRIX_RATE, WEIGHT_DECAY, (out_ref, out1_ref, out2_ref),
             (nout_ref, nout1_ref, nout2_ref)),
            (GAIN_ROW, VECTOR_RATE, 0.0, (gain_ref, gain1_ref, gain2_ref),
             (ngain_ref, ngain1_ref, ngain2_ref)),
            (DATE_ROW, VECTOR_RATE, 0.0, (date_ref, date1_ref, date2_ref),
             (ndate_ref, ndate1_ref, ndate2_ref)),
        ):
            weight, first, second = (ref[...] for ref in old)
            gradient = rest[row : row + weight.shape[0], :]
            for ref, value in zip(new, adam_update(weight, gradient, first, second, rate, decay)):
                ref[...] = value


def finish(sums, turned, count, matrices, momentum, vectors):
    share, width = sums.shape[1:]

    def slot_block():
        return pl.BlockSpec((1, share, width), lambda m: (slot_of(m), 0, 0))

    one = pl.BlockSpec((1, share, width), lambda m: (m, 0, 0))
    return pl.pallas_call(
        finish_kernel,
        grid=(matrices.shape[0],),
        in_specs=[
            slot_block(), pl.BlockSpec((1, share, width), lambda m: (SMALL, 0, 0)), slot_block(),
            whole(count.shape), one, one, *(whole(v.shape) for v in vectors),
        ],
        out_shape=[shape_of(matrices.shape, F32)] * 2
        + [shape_of(v.shape, F32) for v in vectors]
        + [shape_of((1, 1), F32)] * 2,
        out_specs=[one, one] + [whole(v.shape) for v in vectors]
        + [pl.BlockSpec(memory_space=pltpu.SMEM)] * 2,
        compiler_params=pltpu.CompilerParams(
            dimension_semantics=("arbitrary",), vmem_limit_bytes=VMEM_BYTES
        ),
    )(sums, sums, turned, count, matrices, momentum, *vectors)


def adam_update(weight, gradient, first_moment, second_moment, step_rate, decay_rate):
    first_new = BETA_ONE * first_moment + (1.0 - BETA_ONE) * gradient
    second_new = BETA_TWO * second_moment + (1.0 - BETA_TWO) * gradient * gradient
    unbiased_one = first_new / (1.0 - BETA_ONE**STEP)
    unbiased_two = second_new / (1.0 - BETA_TWO**STEP)
    weight_new = weight * (1.0 - step_rate * decay_rate) - step_rate * unbiased_one / (
        jnp.sqrt(unbiased_two) + 1e-08
    )
    return (weight_new, first_new, second_new)


def body(
    inputs,
    targets,
    valid_steps,
    var_weights,
    grid_to_mesh,
    mesh_edges,
    send_rows,
    mesh_to_grid,
    date_index,
    matrices,
    matrices_momentum,
    in_proj,
    in_first,
    in_second,
    out_proj,
    out_first,
    out_second,
    norm_gains,
    gains_first,
    gains_second,
    date_table,
    date_first,
    date_second,
):
    inputs = jnp.swapaxes(inputs, 1, 2)
    targets = jnp.swapaxes(targets, 1, 2)
    members, variables, points = inputs.shape
    nodes = grid_to_mesh.shape[0]
    halo = send_rows.shape[0] // 2
    table = nodes + 2 * halo
    k_edge = mesh_edges.shape[1]
    k_pick = mesh_to_grid.shape[1]
    dates = date_table.shape[0]

    depth = lax.axis_size("row")
    regions = lax.axis_size("region")
    groups = [[g * SLOTS + q for g in range(regions // SLOTS)] for q in range(SLOTS)]
    scalars = pl.BlockSpec(memory_space=pltpu.SMEM)
    hbm = pl.BlockSpec(memory_space=pl.ANY)
    gathered, small, count, *kept, left, right, eh, eht, d, dt = encode(
        date_index, matrices, in_proj, out_proj.T, norm_gains, date_table, valid_steps, inputs,
        grid_to_mesh.T, send_rows[None, :], mesh_edges.T, mesh_to_grid.T, depth,
    )
    mesh1, sent = kept[6:]
    if regions > SLOTS:
        count = lax.psum(count, "region", axis_index_groups=groups)
    weights = gathered.reshape(SLOTS, LATENT, LATENT)
    node_block = per_member((nodes, LATENT))

    def matrix(j):
        place = slot_of(j)
        return pl.BlockSpec(
            (1, LATENT, LATENT), lambda m: (place, 0, 0), pipeline_mode=pl.Buffered(1)
        )

    out_shape = (variables, LATENT)
    late, gout, gxd, dsum, ggain_late, loss_row, dmesh, dhalo = call(
        partial(main_kernel, k_pick),
        members,
        [
            scalars,
            node_block,
            node_block,
            per_member((halo, LATENT)),
            per_member((halo, LATENT)),
            per_member((variables, points)),
            per_member((variables, points)),
            whole((members, points)),
            whole((1, variables)),
            hbm,
            hbm,
            hbm,
            hbm,
            whole((LATENT, LATENT)),
            matrix(2),
            matrix(3),
            matrix(4),
            matrix(5),
            matrix(6),
        ],
        [
            shape_of((5, LATENT, LATENT), F32),
            shape_of(out_shape, F32),
            shape_of((variables, variables), F32),
            shape_of((members, variables, 1), F32),
            shape_of((2, LATENT), F32),
            shape_of((variables, 1), F32),
            shape_of((members, nodes, LATENT), F32),
            shape_of((members, 2 * halo, LATENT), BF16),
        ],
        [
            hbm,
            whole(out_shape),
            whole((variables, variables)),
            per_member((variables, 1)),
            whole((2, LATENT)),
            whole((variables, 1)),
            node_block,
            per_member((2 * halo, LATENT)),
        ],
        main_scratch(k_edge, nodes, points, table),
        60_000_000_000,
    )(
        date_index,
        mesh1,
        sent,
        left,
        right,
        inputs,
        targets,
        valid_steps,
        var_weights[None, :],
        eh,
        eht,
        d,
        dt,
        small,
        weights,
        weights,
        weights,
        weights,
        weights,
    )

    sums, turned = reduce_gradients(
        date_index, late, matrices_momentum, count, dmesh, dhalo, send_rows[None, :], kept[:6], weights,
        small, gxd, dsum, gout, ggain_late, loss_row, depth,
    )
    if regions > SLOTS:
        sums = lax.psum(sums, "region", axis_index_groups=groups)
        turned = turn_whole(sums, count, matrices_momentum)
    vectors = (
        in_proj, in_first, in_second, out_proj.T, out_first.T, out_second.T,
        norm_gains, gains_first, gains_second, date_table, date_first, date_second,
    )
    new = finish(sums, turned, count, matrices, matrices_momentum, vectors)
    return (
        *new[:5],
        *(part.T for part in new[5:8]),
        *new[8:14],
        new[14].reshape(()),
        new[15].reshape(()),
    )


def solution(mesh):
    in_specs = (
        P("row", "region", None),
        P("row", "region", None),
        P("row", "region"),
        P(),
        P("region", None),
        P("region", None),
        P("region"),
        P("region", None),
        P("row"),
        P(None, "row", None),
        P(None, "row", None),
        P(None, "row"),
        P(None, "row"),
        P(None, "row"),
        P("row", None),
        P("row", None),
        P("row", None),
        P(None, "row"),
        P(None, "row"),
        P(None, "row"),
        P(None, "row"),
        P(None, "row"),
        P(None, "row"),
    )
    out_specs = (
        P(None, "row", None),
        P(None, "row", None),
        P(None, "row"),
        P(None, "row"),
        P(None, "row"),
        P("row", None),
        P("row", None),
        P("row", None),
        P(None, "row"),
        P(None, "row"),
        P(None, "row"),
        P(None, "row"),
        P(None, "row"),
        P(None, "row"),
        P(),
        P(),
    )
    return jax.shard_map(body, mesh=mesh, in_specs=in_specs, out_specs=out_specs, check_vma=False)
```
